256 devices in a mesh: dp: 8 (over x, core), res: 32 (over z, y).
Axes of the slice: x: 4, y: 4, z: 8, core: 2. Of those that a mesh axis runs over, the one named last changes fastest.
Arguments:
- alignment: bfloat16 [8, 128, 256, 256], P('dp', None, 'res'), may hold values from -6 to 6
- chain_ids: int32 [8, 256], P('dp'), may hold values from 0 to 11, never falling along the last dimension, each value on 1 to 64 neighbouring positions
- row_counts: int32 [8, 12], P('dp'), may hold values from 1 to 16, 64 in all within a row
- norm_gain: float32 [256], replicated, may hold values from 0.5 to 1.5
- norm_shift: float32 [256], replicated, may hold values from -3 to 3
- left_weight: bfloat16 [256, 32], replicated, may hold values from -0.375 to 0.375
- left_bias: float32 [32], replicated, may hold values from -3 to 3
- right_weight: bfloat16 [256, 32], replicated, may hold values from -0.375 to 0.375
- right_bias: float32 [32], replicated, may hold values from -3 to 3
- out_weight: bfloat16 [1024, 128], replicated, may hold values from -1 to 1
- out_bias: float32 [128], replicated, may hold values from -3 to 3
- pair_cotangent: bfloat16 [8, 256, 256, 128], P('dp', 'res'), may hold values from -6 to 6
Outputs:
- pair_update: bfloat16 [8, 256, 256, 128], P('dp', 'res')
- alignment_grad: bfloat16 [8, 128, 256, 256], P('dp', None, 'res')
- left_weight_grad: float32 [256, 32], replicated
- left_bias_grad: float32 [32], replicated
- right_weight_grad: float32 [256, 32], replicated
- right_bias_grad: float32 [32], replicated
- out_weight_grad: float32 [1024, 128], replicated
- out_bias_grad: float32 [128], replicated
- norm_gain_grad: float32 [256], replicated
- norm_shift_grad: float32 [256], replicated
The draws below stay inside these ranges and needn't reach their ends.
Inputs may be any that keep to these rules, and one draw needn't show every extreme that they name: `chain_ids`: never falls along the residues; every chain 0 to 11 holds at least one residue. `row_counts`: each complex's counts sum to 64, and the largest count is exactly 16.
All inputs are finite; a program needn't handle non-finite values.
Results may differ from the reference program's by a relative error of at most 0.018.
Values may be sent and summed in bfloat16 or wider, within the bound.
A program may use at most 128 MiB of HBM per device.

```python
import math
import jax
import jax.numpy as jnp
import numpy as np
from jax import lax

C_M = 256
C_H = 32
C_Z = 128
PAIRED = 64
UNP = 64
CHAINS = 12
MOST = 16
S = 128
N = 256
B = 8


def steps_of(rng, shape, cuts, least, top_value):
    def one(position, parts):
        heights = jax.random.uniform(jax.random.fold_in(jax.random.fold_in(rng, 6), position), (parts,), jnp.float32, least / len(cuts), top_value / len(cuts))
        return jnp.repeat(jnp.exp(heights), shape[position] // parts).reshape((-1,) + (1,) * (len(shape) - position - 1))

    gain = one(*cuts[0])
    for cut in cuts[1:]:
        gain = gain * one(*cut)
    return gain


def profile(count, total, most, lean):
    loads = [(1 << 20) // math.isqrt(rank ** lean) + 1 for rank in range(2, count + 1)]
    surplus, given = total - most - (count - 1), [1] * (count - 1)
    while surplus > 0:
        movable = [i for i in range(count - 1) if given[i] < most]
        mass, left = sum([loads[i] for i in movable]), surplus
        for i in movable:
            more = min(most - given[i], max(1, left * loads[i] // mass), surplus)
            given[i] = given[i] + more
            surplus = surplus - more
    return np.array([most] + given)


def ragged(key, count, total, limit, skew):
    if count == 2:
        one = jax.random.randint(key, (), max(1, total - limit), min(limit, total - 1) + 1)
        return jnp.stack([one, total - one])
    tallies = jnp.asarray(profile(count, total, limit, skew), jnp.int32)
    twos = (count - 1) // 2
    giver, taker = tallies[1:1 + 2 * twos:2], tallies[2:2 + 2 * twos:2]
    slack = jnp.minimum(giver - 1, limit - taker)
    shifted = jax.random.randint(jax.random.fold_in(key, 1), (twos,), 0, 1 << 20) % (slack + 1)
    tallies = tallies.at[1:1 + 2 * twos:2].set(giver - shifted).at[2:2 + 2 * twos:2].set(taker + shifted)
    return tallies[jax.random.permutation(jax.random.fold_in(key, 2), count)]


def noise(rng, shape, spread, reach, split=(), held_as=jnp.bfloat16):
    loudness = steps_of(rng, shape, split, -0.22, 0.18) if split else 1.0
    values = jax.random.normal(rng, shape, jnp.float32) * spread * loudness
    return jnp.minimum(jnp.maximum(values, -reach), reach).astype(held_as)


def setup_inputs(seed: int = 0) -> dict:
    key_list = jax.random.split(jax.random.key(seed), 13)
    return {
        "alignment": noise(key_list[0], (B, S, N, C_M), 1.0, 6.0, ((0, 8), (2, 32))),
        "chain_ids": jax.vmap(lambda own: jnp.searchsorted(jnp.cumsum(ragged(own, CHAINS, N, N // 4, 2)), jnp.arange(N), side="right"))(jax.random.split(key_list[1], B)).reshape((B, N)).astype(jnp.int32),
        "row_counts": jax.vmap(lambda own: ragged(own, CHAINS, UNP, MOST, 2))(jax.random.split(key_list[2], B)).reshape((B, CHAINS)).astype(jnp.int32),
        "norm_gain": jnp.clip(1.0 + 0.1 * jax.random.normal(key_list[3], (C_M,), jnp.float32), 0.5, 1.5),
        "norm_shift": noise(key_list[4], (C_M,), 0.5, 3.0, (), jnp.float32),
        "left_weight": noise(key_list[5], (C_M, C_H), C_M ** -0.5, 0.375),
        "left_bias": noise(key_list[6], (C_H,), 0.5, 3.0, (), jnp.float32),
        "right_weight": noise(key_list[7], (C_M, C_H), C_M ** -0.5, 0.375),
        "right_bias": noise(key_list[8], (C_H,), 0.5, 3.0, (), jnp.float32),
        "out_weight": noise(key_list[9], (C_H * C_H, C_Z), C_H ** -0.5, 1.0),
        "out_bias": noise(key_list[10], (C_Z,), 0.5, 3.0, (), jnp.float32),
        "pair_cotangent": noise(key_list[11], (B, N, N, C_Z), 1.0, 6.0, ((0, 8), (1, 32))),
    }


EPSILON = 1e-05
NORM_FLOOR = 0.001

def per_residue(lookup, residue_ids):
    labels = jnp.arange(lookup.shape[0], dtype=jnp.int32)
    picked = jnp.where(residue_ids[:, None] == labels[None, :], lookup[None, :], jnp.zeros_like(lookup[None, :]))
    return lax.optimization_barrier(jnp.sum(picked, axis=1))

def unpaired_chain(chain_counts):
    row_ends = jnp.cumsum(chain_counts).astype(jnp.int32)
    row_place = jnp.arange(UNP, dtype=jnp.int32)
    return lax.optimization_barrier(jnp.sum((row_place[:, None] >= row_ends[None, :]).astype(jnp.int32), axis=1))

def layer_norm(values, norm_gain, norm_shift):
    floats = values.astype(jnp.float32)
    centred = floats - lax.optimization_barrier(jnp.mean(floats, axis=-1, keepdims=True))
    inverse = lax.rsqrt(lax.optimization_barrier(jnp.mean(centred * centred, axis=-1, keepdims=True)) + EPSILON)
    scaled = centred * inverse
    normed = (scaled * norm_gain + norm_shift).astype(jnp.bfloat16)
    return (scaled, inverse, normed)

def project(normed, weight, offset, row_mask):
    channels = normed.shape[-1]
    flattened = normed.reshape(-1, channels)
    result = jnp.dot(flattened, weight, preferred_element_type=jnp.float32) + offset
    result = result.reshape(normed.shape[:-1] + (weight.shape[1],))
    return (result * row_mask[..., None]).astype(jnp.bfloat16)

def norm_backward(grad_normed, scaled, inverse, norm_gain):
    grad_scaled = grad_normed * norm_gain
    mean_grad = lax.optimization_barrier(jnp.mean(grad_scaled, axis=-1, keepdims=True))
    mean_prod = lax.optimization_barrier(jnp.mean(grad_scaled * scaled, axis=-1, keepdims=True))
    return inverse * (grad_scaled - mean_grad - scaled * mean_prod)

def one_complex(inputs, params):
    alignment, chain_ids, row_counts, pair_cotangent = inputs
    norm_gain, norm_shift, left_weight, left_bias, right_weight, right_bias, out_weight, out_bias = params
    row_chain = unpaired_chain(row_counts)
    unpaired_mask = (row_chain[:, None] == chain_ids[None, :]).astype(jnp.float32)
    row_mask = jnp.concatenate([jnp.ones((PAIRED, N), jnp.float32), unpaired_mask], axis=0)
    same_chain = (chain_ids[:, None] == chain_ids[None, :]).astype(jnp.float32)
    chain_rows = per_residue(row_counts, chain_ids).astype(jnp.float32)
    normalizer = PAIRED + same_chain * chain_rows[:, None] + NORM_FLOOR
    scaled, inverse, normed = layer_norm(alignment, norm_gain, norm_shift)
    left_rows = project(normed, left_weight, left_bias, row_mask)
    right_rows = project(normed, right_weight, right_bias, row_mask)
    block_rows = math.gcd(N, 64)
    right_floats = right_rows.astype(jnp.float32)

    def row_block(totals, block_index):
        column_grad, weight_total = totals
        row_start = block_index * block_rows
        left_block = lax.dynamic_slice_in_dim(left_rows, row_start, block_rows, 1).astype(jnp.float32)
        products = jnp.einsum('sic,sje->ijce', left_block, right_floats)
        block_norm = lax.dynamic_slice_in_dim(normalizer, row_start, block_rows, 0)[:, :, None, None]
        outer_mean = (products / block_norm).astype(jnp.bfloat16).reshape(block_rows * N, C_H * C_H)
        update = (jnp.dot(outer_mean, out_weight, preferred_element_type=jnp.float32) + out_bias).astype(jnp.bfloat16)
        cotangent = lax.dynamic_slice_in_dim(pair_cotangent, row_start, block_rows, 0).reshape(block_rows * N, C_Z)
        weight_total = weight_total + jnp.dot(outer_mean.T, cotangent, preferred_element_type=jnp.float32)
        back = jnp.dot(cotangent, out_weight.T, preferred_element_type=jnp.float32).reshape(block_rows, N, C_H, C_H)
        outer_grad = (back / block_norm).astype(jnp.bfloat16).astype(jnp.float32)
        left_grad = jnp.einsum('ijce,sje->sic', outer_grad, right_floats)
        column_grad = column_grad + jnp.einsum('ijce,sic->sje', outer_grad, left_block)
        return ((column_grad, weight_total), (update.reshape(block_rows, N, C_Z), left_grad))
    start_totals = (jnp.zeros((S, N, C_H), jnp.float32), jnp.zeros((C_H * C_H, C_Z), jnp.float32))
    block_ids = jnp.arange(N // block_rows, dtype=jnp.int32)
    (right_grad, out_weight_grad), (updates, left_parts) = lax.scan(row_block, start_totals, block_ids)
    pair_update = updates.reshape(N, N, C_Z)
    left_grad = jnp.transpose(left_parts, (1, 0, 2, 3)).reshape(S, N, C_H)
    left_act = (left_grad * row_mask[..., None]).astype(jnp.bfloat16)
    right_act = (right_grad * row_mask[..., None]).astype(jnp.bfloat16)
    flat_normed = normed.reshape(-1, C_M)
    flat_left = left_act.reshape(-1, C_H)
    flat_right = right_act.reshape(-1, C_H)
    left_weight_grad = jnp.dot(flat_normed.T, flat_left, preferred_element_type=jnp.float32)
    right_weight_grad = jnp.dot(flat_normed.T, flat_right, preferred_element_type=jnp.float32)
    left_bias_grad = lax.optimization_barrier(jnp.sum(flat_left.astype(jnp.float32), axis=0))
    right_bias_grad = lax.optimization_barrier(jnp.sum(flat_right.astype(jnp.float32), axis=0))
    grad_normed = jnp.dot(flat_left, left_weight.T, preferred_element_type=jnp.float32)
    grad_normed = grad_normed + jnp.dot(flat_right, right_weight.T, preferred_element_type=jnp.float32)
    grad_normed = grad_normed.reshape(S, N, C_M)
    gain_grad = lax.optimization_barrier(jnp.sum(grad_normed * scaled, axis=(0, 1)))
    shift_grad = lax.optimization_barrier(jnp.sum(grad_normed, axis=(0, 1)))
    alignment_grad = norm_backward(grad_normed, scaled, inverse, norm_gain).astype(jnp.bfloat16)
    out_bias_grad = lax.optimization_barrier(jnp.sum(pair_cotangent.astype(jnp.float32), axis=(0, 1)))
    grads = (left_weight_grad, left_bias_grad, right_weight_grad, right_bias_grad, out_weight_grad, out_bias_grad, gain_grad, shift_grad)
    return (pair_update, alignment_grad, grads)

def reference(alignment, chain_ids, row_counts, norm_gain, norm_shift, left_weight, left_bias, right_weight, right_bias, out_weight, out_bias, pair_cotangent):
    params = (norm_gain, norm_shift, left_weight, left_bias, right_weight, right_bias, out_weight, out_bias)
    pair_update, alignment_grad, grads = lax.map(lambda inputs: one_complex(inputs, params), (alignment, chain_ids, row_counts, pair_cotangent))
    summed = [lax.optimization_barrier(jnp.sum(entry, axis=0)) / N for entry in grads]
    return (pair_update, alignment_grad, summed[0], summed[1], summed[2], summed[3], summed[4], summed[5], summed[6], summed[7])
```

```python
import functools

import jax
import jax.numpy as jnp
from jax import lax
from jax.experimental import pallas as pl
from jax.experimental.pallas import tpu as pltpu
from jax.sharding import PartitionSpec as P

C_M = 256
C_H = 32
C_Z = 128
PAIRED = 64
UNP = 64
MOST = 16
CHAINS = 12
EPSILON = 1e-05
NORM_FLOOR = 0.001

ROWS = 8
SLOTS = PAIRED + MOST
NY, NZ, NDP = 4, 8, 8
NRES = NY * NZ
N = ROWS * NRES
ENT = ROWS * SLOTS
F32, BF16 = jnp.float32, jnp.bfloat16
MESH = pl.DeviceIdType.MESH

NN = (((1,), (0,)), ((), ()))
NT = (((1,), (1,)), ((), ()))
TN = (((0,), (0,)), ((), ()))


def dot(a, b, dims=NN):
    return lax.dot_general(a, b, dims, preferred_element_type=F32)


def iota(shape, dim):
    return lax.broadcasted_iota(jnp.int32, shape, dim)


def onehot(cond):
    return jnp.where(cond, 1.0, 0.0).astype(BF16)


def kernel(
    chain_s, counts_s, chain_v, x_ref, gain_ref, shift_ref, wt_ref, bias_ref, biascol_ref,
    w2_ref, obias_ref, cot_ref,
    upd_ref, agrad_ref, dw_ref, small_ref,
    xc, normed, inv_ref, lrow, lt, q_ref, tp, tu, g_ref, gm_ref, v_ref, rx, rp, ru,
    ry, vsum, rz, ucat, dwf, dws, a_rx, s1, b_rx, c_rx, s3, s4, d_rx,
    sm, t_rx, sm1, e_rx, sm2, f_rx, sm3, sm_out, ract,
    agz_s, agz_r, agy_s, agy_r, rsy_s, rsy_r, rsz_s, rsz_r,
    p_s, p_r, bz_s, bz_r, cy_s, cy_r, dz_s, dz_r, ed_s, ed_r,
    tz_s, tz_r, ud_s, ud_r, uy_s, uy_r, uz_s, uz_r,
):
    me = lax.axis_index("res")
    dp = lax.axis_index("dp")
    z, y = me // NY, me % NY

    def zpeer(k):
        return (z + k) % NZ

    def ypeer(k):
        return (y + k) % NY

    def dpeer(k):
        return (dp + k) % NDP

    def rc(src, dst, ss, rs, **where):
        return pltpu.make_async_remote_copy(
            src_ref=src, dst_ref=dst, send_sem=ss, recv_sem=rs,
            device_id=where, device_id_type=MESH,
        )

    barrier = pltpu.get_barrier_semaphore()
    for k in range(1, NZ):
        pl.semaphore_signal(barrier, inc=1, device_id={"res": zpeer(k) * NY + y}, device_id_type=MESH)
    for k in range(1, NY):
        pl.semaphore_signal(barrier, inc=1, device_id={"res": z * NY + ypeer(k)}, device_id_type=MESH)
    for k in range(1, NDP):
        pl.semaphore_signal(barrier, inc=1, device_id={"dp": dpeer(k)}, device_id_type=MESH)

    chain, start, count, base = [], [], [], []
    for r in range(ROWS):
        c = chain_s[0, me * ROWS + r]
        st = jnp.int32(0)
        ct = jnp.int32(0)
        for k in range(CHAINS):
            v = counts_s[0, k]
            st = st + jnp.where(c > k, v, 0)
            ct = ct + jnp.where(c == k, v, 0)
        chain.append(c)
        start.append(st)
        count.append(ct)
        base.append(jnp.minimum(st, UNP - MOST))

    def slot_mask(r, shape, dim):
        s = iota(shape, dim)
        row = s - PAIRED + base[r]
        live = (row >= start[r]) & (row < start[r] + count[r])
        return jnp.where((s < PAIRED) | live, 1.0, 0.0)

    ro, co = iota((128, 128), 0), iota((128, 128), 1)
    perm0 = onehot(co == (ro % 16) * ROWS + ro // 16)
    for b in range(PAIRED // 16):
        part = dot(perm0, x_ref[b * 128:(b + 1) * 128, :])
        for r in range(ROWS):
            xc[r * SLOTS + b * 16:r * SLOTS + b * 16 + 16, :] = part[r * 16:(r + 1) * 16]
    ru_i = iota((128, UNP * ROWS), 0)
    base_rows = jnp.zeros((128, UNP * ROWS), jnp.int32)
    for r in range(ROWS):
        base_rows = jnp.where(ru_i // 16 == r, base[r], base_rows)
    pick = onehot(iota((128, UNP * ROWS), 1) == (base_rows + ru_i % 16) * ROWS + ru_i // 16)
    part = dot(pick, x_ref[PAIRED * ROWS:, :])
    for r in range(ROWS):
        xc[r * SLOTS + PAIRED:(r + 1) * SLOTS, :] = part[r * 16:(r + 1) * 16]

    for r in range(ROWS):
        rows = slice(r * SLOTS, (r + 1) * SLOTS)
        floats = xc[rows, :]
        centred = floats - jnp.mean(floats, axis=-1, keepdims=True)
        inverse = lax.rsqrt(jnp.mean(centred * centred, axis=-1, keepdims=True) + EPSILON)
        scaled = centred * inverse
        nrm = (scaled * gain_ref[...] + shift_ref[...]).astype(BF16)
        xc[rows, :] = scaled
        inv_ref[rows, :] = inverse
        normed[rows, :] = nrm
        left = (dot(nrm, wt_ref[0:C_H, :], NT) + bias_ref[0:1, :]) * slot_mask(r, (SLOTS, C_H), 0)
        lrow[rows, :] = left.astype(BF16)
        right = (dot(wt_ref[C_H:, :], nrm, NT) + biascol_ref[C_H:, :]) * slot_mask(r, (C_H, SLOTS), 1)
        q_ref[r * C_H:(r + 1) * C_H, 0:SLOTS] = right.astype(BF16)
    re, ce = iota((256, 256), 0), iota((256, 256), 1)
    permq = onehot(ce == (re % 8) * 32 + ((re // 8) % 2) * 16 + re // 16)
    mixed = dot(permq, q_ref[:, 0:SLOTS])
    for p in range(8):
        rx[me, :, p * 128:(p + 1) * 128] = jnp.concatenate(
            [mixed[(2 * p + a) * 16:(2 * p + a + 1) * 16, 0:PAIRED] for a in range(2)], axis=1
        ).astype(BF16)
    for q in range(2):
        rx[me, :, 1024 + q * 128:1024 + (q + 1) * 128] = jnp.concatenate(
            [mixed[(8 * q + a) * 16:(8 * q + a + 1) * 16, PAIRED:SLOTS] for a in range(8)], axis=1
        ).astype(BF16)

    pl.semaphore_wait(barrier, NZ + NY + NDP - 3)

    def agz(k):
        return rc(rx.at[me], rx.at[me], agz_s.at[k], agz_r.at[k], res=zpeer(k) * NY + y)

    for k in (1, 7, 2, 6, 3, 5, 4):
        agz(k).start()

    lt[...] = jnp.transpose(lrow[...].astype(F32)).astype(BF16)

    @pl.loop(0, 16)
    def _(g):
        h, p = g // 8, g % 8
        t = dot(lrow[...], w2_ref[:, pl.ds(pl.multiple_of(g * 256, 256), 256)]).astype(BF16)
        rowp = pl.multiple_of((p * 2 + h) * 128, 128)
        rowu = pl.multiple_of(((p // 4) * 2 + h) * 128 + (p % 4) * 32, 32)
        for i in range(ROWS):
            for a in range(2):
                tp[pl.ds(rowp + a * 64, 64), i * 128:(i + 1) * 128] = t[i * SLOTS:i * SLOTS + PAIRED, a * 128:(a + 1) * 128]
                tu[pl.ds(rowu + a * 16, 16), i * 128:(i + 1) * 128] = t[i * SLOTS + PAIRED:(i + 1) * SLOTS, a * 128:(a + 1) * 128]

    def agy(k, kz):
        slot = ((z - kz + NZ) % NZ) * NY + y
        return rc(rx.at[slot], rx.at[slot], agy_s.at[k, kz], agy_r.at[k, kz], res=z * NY + ypeer(k))

    for kz in (0, 1, 7, 2, 6, 3, 5, 4):
        if kz:
            agz(kz).wait_recv()
        for k in (1, 3, 2):
            agy(k, kz).start()

    chain_col = jnp.transpose(jnp.broadcast_to(chain_v[...].astype(F32), (128, N)))
    obg = jnp.zeros((8, C_Z), F32)
    inv_own = []
    for i in range(ROWS):
        same = chain_col == chain[i].astype(F32)
        cntf = jnp.full((8, C_Z), count[i].astype(F32))
        inv_own.append((1.0 / (PAIRED + cntf + NORM_FLOOR))[0:1, :])
        raw = cot_ref[i].astype(F32)
        obg = obg + jnp.sum(raw.reshape(N // 8, 8, C_Z), axis=0)
        g = (raw * jnp.where(same, inv_own[i], 1.0 / (PAIRED + NORM_FLOOR))).astype(BF16)
        g_ref[:, i * 128:(i + 1) * 128] = g
        gm_ref[:, i * 128:(i + 1) * 128] = jnp.where(same, g.astype(F32), 0.0).astype(BF16)

    def put_v(v, lane):
        both = jnp.concatenate(
            [v[:, 0:128].reshape(NRES, ROWS, 128), v[:, 128:256].reshape(NRES, ROWS, 128)], axis=1
        )
        v_ref[:, :, pl.ds(lane, 128)] = both.astype(BF16)

    @pl.loop(0, 8)
    def _(p):
        put_v(dot(g_ref[...], tp[pl.ds(pl.multiple_of(p * 256, 256), 256), :], NT), pl.multiple_of(p * 128, 128))

    for q in range(2):
        put_v(dot(gm_ref[...], tu[q * 256:(q + 1) * 256, :], NT), 1024 + q * 128)

    def rsy(k, kz):
        dst = zpeer(kz) * NY + ypeer(k)
        return rc(v_ref.at[dst], ry.at[k, kz], rsy_s.at[k, kz], rsy_r.at[k, kz], res=z * NY + ypeer(k))

    for kz in (1, 7, 2, 6, 3, 5, 4, 0):
        for k in (1, 3, 2):
            rsy(k, kz).start()

    for kz in range(NZ):
        for k in range(1, NY):
            agy(k, kz).wait_recv()

    @pl.loop(0, NRES // 2)
    def _(d):
        a, b = rx[2 * d].astype(F32), rx[2 * d + 1].astype(F32)
        rows = pl.ds(pl.multiple_of(d * 16, 16), 16)
        for h in range(2):
            both = jnp.concatenate([a[h * 8:h * 8 + 8], b[h * 8:h * 8 + 8]], axis=0).astype(BF16)
            for p in range(8):
                rp[rows, p * 256 + h * 128:p * 256 + (h + 1) * 128] = both[:, p * 128:(p + 1) * 128]
            for q in range(2):
                ru[rows, q * 256 + h * 128:q * 256 + (h + 1) * 128] = both[:, 1024 + q * 128:1024 + (q + 1) * 128]

    @pl.loop(0, 8)
    def _(p):
        u = dot(rp[:, pl.ds(pl.multiple_of(p * 256, 256), 256)], g_ref[...], TN).astype(BF16)
        for h in range(2):
            for a in range(2):
                lane = pl.multiple_of((h * 16 + 2 * p + a) * 128, 128)
                for i in range(ROWS):
                    ucat[i * SLOTS:i * SLOTS + PAIRED, pl.ds(lane, 128)] = u[(h * 2 + a) * 64:(h * 2 + a + 1) * 64, i * 128:(i + 1) * 128]

    for q in range(2):
        u = dot(ru[:, q * 256:(q + 1) * 256], gm_ref[...], TN).astype(BF16)
        for h in range(2):
            for a in range(8):
                lane = (h * 16 + q * 8 + a) * 128
                for i in range(ROWS):
                    ucat[i * SLOTS + PAIRED:(i + 1) * SLOTS, lane:lane + 128] = u[(h * 8 + a) * 16:(h * 8 + a + 1) * 16, i * 128:(i + 1) * 128]

    @pl.loop(0, 16)
    def _(g):
        dw = dot(lt[...], ucat[:, pl.ds(pl.multiple_of(g * 256, 256), 256)])
        for a in range(2):
            part = dw[:, a * 128:(a + 1) * 128]
            row = pl.multiple_of((g % 2) * 64 + a * 32, 32)
            dwf[g // 2, pl.ds(row, 32), :] = part
            dws[g // 2, pl.ds(row, 32), :] = part.astype(BF16)

    def pdp(k):
        return rc(dws.at[dpeer(k)], a_rx.at[k], p_s.at[k], p_r.at[k], dp=dpeer(k))

    for k in range(1, NDP):
        pdp(k).start()

    def rsz(k):
        return rc(vsum.at[k], rz.at[k], rsz_s.at[k], rsz_r.at[k], res=zpeer(k) * NY + y)

    own = None
    for kz in (1, 7, 2, 6, 3, 5, 4, 0):
        total = v_ref[zpeer(kz) * NY + y].astype(F32)
        for k in range(1, NY):
            rsy(k, kz).wait_recv()
            total = total + ry[k, kz].astype(F32)
        if kz:
            vsum[kz] = total.astype(BF16)
            rsz(kz).start()
        else:
            own = total

    def left_step(k, acc):
        cols = pl.ds(pl.multiple_of(k * 512, 512), 512)
        return acc + dot(ucat[:, cols], w2_ref[:, cols], NT)

    lgrad = lax.fori_loop(0, 8, left_step, jnp.zeros((ENT, C_H), F32))

    @pl.loop(0, 4)
    def _(g):
        cols = pl.ds(pl.multiple_of(g * 256, 256), 256)
        main = dot(rp[...], tp[:, cols])
        side = dot(ru[...], tu[:, cols])
        for a in range(2):
            i = 2 * g + a
            ch = jnp.int32(0)
            iv = jnp.zeros((1, C_Z), F32)
            for r in range(ROWS):
                ch = jnp.where(i == r, chain[r], ch)
                iv = jnp.where(i == r, inv_own[r], iv)
            same = chain_col == ch.astype(F32)
            m, s = main[:, a * 128:(a + 1) * 128], side[:, a * 128:(a + 1) * 128]
            out = jnp.where(same, (m + s) * iv, m * (1.0 / (PAIRED + NORM_FLOOR))) + obias_ref[...]
            upd_ref[i] = out.astype(BF16)

    s = dwf[dp]
    for k in range(1, NDP):
        pdp(k).wait_recv()
        s = s + a_rx[k].astype(F32)
    s1[...] = s.reshape(NZ, 16, C_Z)

    def bz(k):
        return rc(s1.at[zpeer(k)], b_rx.at[k], bz_s.at[k], bz_r.at[k], res=zpeer(k) * NY + y)

    for k in range(1, NZ):
        bz(k).start()

    for kz in range(1, NZ):
        rsz(kz).wait_recv()
        own = own + rz[kz].astype(F32)
    tiles = []
    for e in range(16):
        tiles.append(jnp.concatenate([own[:, e * 64:(e + 1) * 64], own[:, 1024 + e * 16:1024 + (e + 1) * 16]], axis=1))
    back = dot(permq, jnp.concatenate(tiles, axis=0).astype(BF16), TN)

    gw_l = jnp.zeros((C_H, C_M), F32)
    gw_r = jnp.zeros((C_H, C_M), F32)
    gb_l = jnp.zeros((1, C_H), F32)
    gb_r = jnp.zeros((C_H, 1), F32)
    gain_g = jnp.zeros((1, C_M), F32)
    shift_g = jnp.zeros((1, C_M), F32)
    for r in range(ROWS):
        rows = slice(r * SLOTS, (r + 1) * SLOTS)
        nrm = normed[rows, :]
        lact = (lgrad[rows] * slot_mask(r, (SLOTS, C_H), 0)).astype(BF16)
        ract_t = (back[r * C_H:(r + 1) * C_H, :] * slot_mask(r, (C_H, SLOTS), 1)).astype(BF16)
        gw_l = gw_l + dot(lact, nrm, TN)
        gw_r = gw_r + dot(ract_t, nrm)
        gb_l = gb_l + jnp.sum(lact.astype(F32), axis=0, keepdims=True)
        gb_r = gb_r + jnp.sum(ract_t.astype(F32), axis=1, keepdims=True)
        gn = dot(lact, wt_ref[0:C_H, :]) + dot(ract_t, wt_ref[C_H:, :], TN)
        scaled = xc[rows, :]
        gs = gn * scaled
        gain_g = gain_g + jnp.sum(gs, axis=0, keepdims=True)
        shift_g = shift_g + jnp.sum(gn, axis=0, keepdims=True)
        gg = gn * gain_ref[...]
        mean_g = jnp.mean(gg, axis=-1, keepdims=True)
        mean_p = jnp.mean(gg * scaled, axis=-1, keepdims=True)
        ract[rows, :] = (inv_ref[rows, :] * (gg - mean_g - scaled * mean_p)).astype(BF16)

    smf = jnp.concatenate([gw_l, gw_r], axis=0)
    gbr_row = jnp.transpose(jnp.broadcast_to(gb_r, (C_H, 128)))[0:1, :]
    rows8 = iota((8, C_Z), 0)
    tail = jnp.zeros((8, C_Z), F32)
    tail_rows = (
        gain_g[:, 0:128], gain_g[:, 128:256], shift_g[:, 0:128], shift_g[:, 128:256],
        jnp.sum(obg, axis=0, keepdims=True),
        jnp.concatenate([gb_l, gbr_row, jnp.zeros((1, 64), F32)], axis=1),
    )
    for k, row in enumerate(tail_rows):
        tail = jnp.where(rows8 == k, row, tail)
    flat = jnp.concatenate([smf[:, 0:128], smf[:, 128:256], tail, jnp.zeros((56, C_Z), F32)], axis=0)
    sm[...] = flat.reshape(NZ, 24, C_Z)

    def tz(k):
        return rc(sm.at[zpeer(k)], t_rx.at[k], tz_s.at[k], tz_r.at[k], res=zpeer(k) * NY + y)

    for k in range(1, NZ):
        tz(k).start()

    s = s1[z]
    for k in range(1, NZ):
        bz(k).wait_recv()
        s = s + b_rx[k]
    c_rx[y] = s

    def cy(k):
        return rc(c_rx.at[y], c_rx.at[y], cy_s.at[k], cy_r.at[k], res=z * NY + ypeer(k))

    for k in range(1, NY):
        cy(k).start()

    s = sm[z]
    for k in range(1, NZ):
        tz(k).wait_recv()
        s = s + t_rx[k]
    e_rx[dp] = s

    def ud(k):
        return rc(e_rx.at[dp], e_rx.at[dp], ud_s.at[k], ud_r.at[k], dp=dpeer(k))

    for k in range(1, NDP):
        ud(k).start()

    for k in range(1, NY):
        cy(k).wait_recv()
    s4[z] = ((c_rx[0] + c_rx[1] + c_rx[2] + c_rx[3]) * (1.0 / N)).astype(BF16)

    def dz(k):
        return rc(s4.at[z], s4.at[z], dz_s.at[k], dz_r.at[k], res=zpeer(k) * NY + y)

    for k in range(1, NZ):
        dz(k).start()

    for k in range(1, NDP):
        ud(k).wait_recv()
    s = e_rx[0]
    for k in range(1, NDP):
        s = s + e_rx[k]
    f_rx[y] = s

    def uy(k):
        return rc(f_rx.at[y], f_rx.at[y], uy_s.at[k], uy_r.at[k], res=z * NY + ypeer(k))

    for k in range(1, NY):
        uy(k).start()

    for k in range(1, NZ):
        dz(k).wait_recv()
    d_rx[dp] = s4[...].reshape(128, C_Z)

    def ed(k):
        return rc(d_rx.at[dp], d_rx.at[dp], ed_s.at[k], ed_r.at[k], dp=dpeer(k))

    for k in range(1, NDP):
        ed(k).start()

    for k in range(1, NY):
        uy(k).wait_recv()
    sm_out[z] = (f_rx[0] + f_rx[1] + f_rx[2] + f_rx[3]) * (1.0 / N)

    def uz(k):
        return rc(sm_out.at[z], sm_out.at[z], uz_s.at[k], uz_r.at[k], res=zpeer(k) * NY + y)

    for k in range(1, NZ):
        uz(k).start()

    for b in range(PAIRED // 16):
        src = jnp.concatenate([ract[r * SLOTS + b * 16:r * SLOTS + b * 16 + 16, :] for r in range(ROWS)], axis=0)
        agrad_ref[b * 128:(b + 1) * 128, :] = dot(perm0, src, TN).astype(BF16)
    src = jnp.concatenate([ract[r * SLOTS + PAIRED:(r + 1) * SLOTS, :] for r in range(ROWS)], axis=0)
    agrad_ref[PAIRED * ROWS:, :] = dot(pick, src, TN).astype(BF16)

    for k in range(1, NZ):
        uz(k).wait_recv()
    small_ref[...] = sm_out[...]
    for k in range(1, NDP):
        ed(k).wait_recv()
    for d in range(NDP):
        for a in range(4):
            dw_ref[:, d * 4 + a, :] = d_rx[d, a * 32:(a + 1) * 32, :].astype(F32)

    for k in range(1, NZ):
        for c in (agz, rsz, bz, tz, dz, uz):
            c(k).wait_send()
    for k in range(1, NDP):
        for c in (pdp, ud, ed):
            c(k).wait_send()
    for k in range(1, NY):
        cy(k).wait_send()
        uy(k).wait_send()
        for kz in range(NZ):
            agy(k, kz).wait_send()
            rsy(k, kz).wait_send()


def body(
    alignment, chain_ids, row_counts, norm_gain, norm_shift, left_weight, left_bias,
    right_weight, right_bias, out_weight, out_bias, pair_cotangent,
):
    wt = jnp.concatenate([left_weight, right_weight], axis=1).T
    bias = jnp.concatenate([left_bias, right_bias])
    vm = pl.BlockSpec(memory_space=pltpu.VMEM)
    sm = pl.BlockSpec(memory_space=pltpu.SMEM)
    sems = lambda *shape: pltpu.SemaphoreType.DMA(shape)
    vmem = pltpu.VMEM
    scratch = [
        vmem((ENT, C_M), F32), vmem((ENT, C_M), BF16), vmem((ENT, 1), F32),
        vmem((ENT, C_H), BF16), vmem((C_H, ENT), BF16), vmem((256, 128), BF16),
        vmem((2048, 1024), BF16), vmem((512, 1024), BF16), vmem((N, 1024), BF16), vmem((N, 1024), BF16),
        vmem((NRES, 16, 1280), BF16), vmem((NRES, 16, 1280), BF16), vmem((N, 2048), BF16), vmem((N, 512), BF16),
        vmem((NY, NZ, 16, 1280), BF16), vmem((NZ, 16, 1280), BF16), vmem((NZ, 16, 1280), BF16),
        vmem((ENT, 4096), BF16),
        vmem((NDP, 128, C_Z), F32), vmem((NDP, 128, C_Z), BF16), vmem((NDP, 128, C_Z), BF16),
        vmem((NZ, 16, C_Z), F32), vmem((NZ, 16, C_Z), F32), vmem((NY, 16, C_Z), F32), vmem((16, C_Z), BF16),
        vmem((NZ, 16, C_Z), BF16), vmem((NDP, 128, C_Z), BF16),
        vmem((NZ, 24, C_Z), F32), vmem((NZ, 24, C_Z), F32), vmem((24, C_Z), F32), vmem((NDP, 24, C_Z), F32),
        vmem((24, C_Z), F32), vmem((NY, 24, C_Z), F32), vmem((24, C_Z), F32), vmem((NZ, 24, C_Z), F32),
        vmem((ENT, C_M), BF16),
        sems(NZ), sems(NZ), sems(NY, NZ), sems(NY, NZ), sems(NY, NZ), sems(NY, NZ), sems(NZ), sems(NZ),
        sems(NDP), sems(NDP), sems(NZ), sems(NZ), sems(NY), sems(NY), sems(NZ), sems(NZ), sems(NDP), sems(NDP),
        sems(NZ), sems(NZ), sems(NDP), sems(NDP), sems(NY), sems(NY), sems(NZ), sems(NZ),
    ]
    upd, agrad, dw, small = pl.pallas_call(
        kernel,
        out_shape=(
            jax.ShapeDtypeStruct((ROWS, N, C_Z), BF16),
            jax.ShapeDtypeStruct((128 * ROWS, C_M), BF16),
            jax.ShapeDtypeStruct((C_H, C_H, C_Z), F32),
            jax.ShapeDtypeStruct((NZ, 24, C_Z), F32),
        ),
        in_specs=[sm, sm] + [vm] * 10,
        out_specs=(vm,) * 4,
        scratch_shapes=scratch,
        compiler_params=pltpu.CompilerParams(
            collective_id=0, has_side_effects=True, vmem_limit_bytes=50 * 1024 * 1024
        ),
    )(
        chain_ids, row_counts, chain_ids, alignment.reshape(128 * ROWS, C_M),
        norm_gain.reshape(1, C_M), norm_shift.reshape(1, C_M), wt,
        bias.reshape(2, C_H), bias.reshape(2 * C_H, 1),
        out_weight.reshape(C_H, C_H * C_Z), out_bias.reshape(1, C_Z), pair_cotangent[0],
    )
    flat = small.reshape(192, C_Z)
    gw = jnp.concatenate([flat[0:64], flat[64:128]], axis=1).T
    return (
        upd[None],
        agrad.reshape(1, 128, ROWS, C_M),
        gw[:, 0:C_H],
        flat[133, 0:C_H],
        gw[:, C_H:],
        flat[133, C_H:2 * C_H],
        dw.reshape(C_H * C_H, C_Z),
        flat[132],
        flat[128:130].reshape(C_M),
        flat[130:132].reshape(C_M),
    )


def solution(mesh):
    return jax.shard_map(
        body,
        mesh=mesh,
        in_specs=(
            P("dp", None, "res", None), P("dp", None), P("dp", None), P(), P(), P(), P(), P(), P(), P(), P(),
            P("dp", "res", None, None),
        ),
        out_specs=(
            P("dp", "res", None, None), P("dp", None, "res", None), P(), P(), P(), P(), P(), P(), P(), P(),
        ),
        check_vma=False,
    )
```

```python
import functools

import jax
import jax.numpy as jnp
from jax import lax
from jax.experimental import pallas as pl
from jax.experimental.pallas import tpu as pltpu
from jax.sharding import PartitionSpec as P

C_M = 256
C_H = 32
C_Z = 128
PAIRED = 64
UNP = 64
MOST = 16
CHAINS = 12
EPSILON = 1e-05
NORM_FLOOR = 0.001

ROWS = 8
SLOTS = PAIRED + MOST
NY, NZ, NDP = 4, 8, 8
NRES = NY * NZ
N = ROWS * NRES
ENT = ROWS * SLOTS
HALF = 640
F32, BF16 = jnp.float32, jnp.bfloat16
MESH = pl.DeviceIdType.MESH

NN = (((1,), (0,)), ((), ()))
NT = (((1,), (1,)), ((), ()))
TN = (((0,), (0,)), ((), ()))


def dot(a, b, dims=NN):
    return lax.dot_general(a, b, dims, preferred_element_type=F32)


def iota(shape, dim):
    return lax.broadcasted_iota(jnp.int32, shape, dim)


def onehot(cond):
    return jnp.where(cond, 1.0, 0.0).astype(BF16)


def kernel(
    chain_s, counts_s, chain_v, x_hbm, gain_ref, shift_ref, wt_ref, bias_ref, biascol_ref,
    w2_ref, obias_ref, cot_hbm,
    upd_ref, agrad_ref, dw_ref, lw_ref, rw_ref, tail_ref,
    x_ref, cot_ref, xc, normed, inv_ref, lrow, lt, q_ref, tp, tu, g_ref, gm_ref, v_ref, rx, rp, ru,
    ry1, ry2, vsum, rz, ucat, dwf, dws, a_rx, s1, b_rx, c_rx, s4, d_rx,
    sm, t_rx, e_rx, so, ract,
    in_s, agz_s, agz_r, agy_s, agy_r, agf_s, agf_r, rs1_s, rs1_r, rs2_s, rs2_r, rsz_s, rsz_r,
    p_s, p_r, bz_s, bz_r, cy_s, cy_r, dz_s, dz_r, ed_s, ed_r,
    td_s, td_r, ur_s, ur_r, wd_s, wd_r,
):
    me = lax.axis_index("res")
    dp = lax.axis_index("dp")
    z, y = me // NY, me % NY

    def zpeer(k):
        return (z + k) % NZ

    def ypeer(k):
        return (y + k) % NY

    def dpeer(k):
        return (dp + k) % NDP

    def rc(src, dst, ss, rs, **where):
        return pltpu.make_async_remote_copy(
            src_ref=src, dst_ref=dst, send_sem=ss, recv_sem=rs,
            device_id=where, device_id_type=MESH,
        )

    x_in = pltpu.make_async_copy(x_hbm, x_ref, in_s.at[0])
    x_in.start()
    cot_in = pltpu.make_async_copy(cot_hbm, cot_ref, in_s.at[1])
    cot_in.start()

    barrier = pltpu.get_barrier_semaphore()

    @pl.loop(1, NRES)
    def _(k):
        pl.semaphore_signal(barrier, inc=1, device_id={"res": (me + k) % NRES}, device_id_type=MESH)

    for k in range(1, NDP):
        pl.semaphore_signal(barrier, inc=1, device_id={"dp": dpeer(k)}, device_id_type=MESH)

    chain, start, count, base = [], [], [], []
    for r in range(ROWS):
        c = chain_s[0, me * ROWS + r]
        st = jnp.int32(0)
        ct = jnp.int32(0)
        for k in range(CHAINS):
            v = counts_s[0, k]
            st = st + jnp.where(c > k, v, 0)
            ct = ct + jnp.where(c == k, v, 0)
        chain.append(c)
        start.append(st)
        count.append(ct)
        base.append(jnp.minimum(st, UNP - MOST))

    def slot_mask(r, shape, dim):
        s = iota(shape, dim)
        row = s - PAIRED + base[r]
        live = (row >= start[r]) & (row < start[r] + count[r])
        return jnp.where((s < PAIRED) | live, 1.0, 0.0)

    x_in.wait()
    ro, co = iota((128, 128), 0), iota((128, 128), 1)
    perm0 = onehot(co == (ro % 16) * ROWS + ro // 16)
    for b in range(PAIRED // 16):
        part = dot(perm0, x_ref[b * 128:(b + 1) * 128, :])
        for r in range(ROWS):
            xc[r * SLOTS + b * 16:r * SLOTS + b * 16 + 16, :] = part[r * 16:(r + 1) * 16]
    ru_i = iota((128, UNP * ROWS), 0)
    base_rows = jnp.zeros((128, UNP * ROWS), jnp.int32)
    for r in range(ROWS):
        base_rows = jnp.where(ru_i // 16 == r, base[r], base_rows)
    pick = onehot(iota((128, UNP * ROWS), 1) == (base_rows + ru_i % 16) * ROWS + ru_i // 16)
    part = dot(pick, x_ref[PAIRED * ROWS:, :])
    for r in range(ROWS):
        xc[r * SLOTS + PAIRED:(r + 1) * SLOTS, :] = part[r * 16:(r + 1) * 16]

    for r in range(ROWS):
        rows = slice(r * SLOTS, (r + 1) * SLOTS)
        floats = xc[rows, :]
        centred = floats - jnp.mean(floats, axis=-1, keepdims=True)
        inverse = lax.rsqrt(jnp.mean(centred * centred, axis=-1, keepdims=True) + EPSILON)
        scaled = centred * inverse
        nrm = (scaled * gain_ref[...] + shift_ref[...]).astype(BF16)
        xc[rows, :] = scaled
        inv_ref[rows, :] = inverse
        normed[rows, :] = nrm
        left = (dot(nrm, wt_ref[0:C_H, :], NT) + bias_ref[0:1, :]) * slot_mask(r, (SLOTS, C_H), 0)
        lrow[rows, :] = left.astype(BF16)
        right = (dot(wt_ref[C_H:, :], nrm, NT) + biascol_ref[C_H:, :]) * slot_mask(r, (C_H, SLOTS), 1)
        q_ref[r * C_H:(r + 1) * C_H, 0:SLOTS] = right.astype(BF16)
    re, ce = iota((256, 256), 0), iota((256, 256), 1)
    permq = onehot(ce == (re % 8) * 32 + ((re // 8) % 2) * 16 + re // 16)
    mixed = dot(permq, q_ref[:, 0:SLOTS])
    for p in range(8):
        rx[me, :, p * 128:(p + 1) * 128] = jnp.concatenate(
            [mixed[(2 * p + a) * 16:(2 * p + a + 1) * 16, 0:PAIRED] for a in range(2)], axis=1
        ).astype(BF16)
    for q in range(2):
        rx[me, :, 1024 + q * 128:1024 + (q + 1) * 128] = jnp.concatenate(
            [mixed[(8 * q + a) * 16:(8 * q + a + 1) * 16, PAIRED:SLOTS] for a in range(8)], axis=1
        ).astype(BF16)

    pl.semaphore_wait(barrier, NRES + NDP - 2)

    def agz(k):
        return rc(rx.at[me], rx.at[me], agz_s.at[k], agz_r.at[k], res=zpeer(k) * NY + y)

    def agy(d, kz):
        slot = ((z - kz + NZ) % NZ) * NY + y
        return rc(rx.at[slot], rx.at[slot], agy_s.at[d, kz], agy_r.at[d, kz], res=z * NY + ypeer(1 + 2 * d))

    def agf(d, kz):
        slot = ((z - kz + NZ) % NZ) * NY + ypeer(3 - 2 * d)
        part = rx.at[slot, :, d * HALF:(d + 1) * HALF]
        return rc(part, part, agf_s.at[d, kz], agf_r.at[d, kz], res=z * NY + ypeer(1 + 2 * d))

    def spread(*turns):
        for kz in turns:
            if kz:
                agz(kz).wait_recv()
            for d in range(2):
                agy(d, kz).start()

    def forward(*turns):
        for kz in turns:
            for d in range(2):
                agy(d, kz).wait_recv()
                agf(d, kz).start()

    spread(0)
    for k in (1, 7, 2, 6, 3, 5, 4):
        agz(k).start()

    lt[...] = jnp.transpose(lrow[...].astype(F32)).astype(BF16)

    def t_step(g):
        h, p = g // 8, g % 8
        t = dot(lrow[...], w2_ref[:, pl.ds(pl.multiple_of(g * 256, 256), 256)]).astype(BF16)
        rowp = pl.multiple_of((p * 2 + h) * 128, 128)
        rowu = pl.multiple_of(((p // 4) * 2 + h) * 128 + (p % 4) * 32, 32)
        for i in range(ROWS):
            for a in range(2):
                tp[pl.ds(rowp + a * 64, 64), i * 128:(i + 1) * 128] = t[i * SLOTS:i * SLOTS + PAIRED, a * 128:(a + 1) * 128]
                tu[pl.ds(rowu + a * 16, 16), i * 128:(i + 1) * 128] = t[i * SLOTS + PAIRED:(i + 1) * SLOTS, a * 128:(a + 1) * 128]

    pl.loop(0, 12)(t_step)
    spread(1, 7)
    pl.loop(12, 16)(t_step)
    spread(2, 6)
    forward(0)

    cot_in.wait()
    chain_col = jnp.transpose(jnp.broadcast_to(chain_v[...].astype(F32), (128, N)))
    obg = jnp.zeros((8, C_Z), F32)
    inv_own = []
    for i in range(ROWS):
        same = chain_col == chain[i].astype(F32)
        cntf = jnp.full((8, C_Z), count[i].astype(F32))
        inv_own.append((1.0 / (PAIRED + cntf + NORM_FLOOR))[0:1, :])
        raw = cot_ref[i].astype(F32)
        obg = obg + jnp.sum(raw.reshape(N // 8, 8, C_Z), axis=0)
        g = (raw * jnp.where(same, inv_own[i], 1.0 / (PAIRED + NORM_FLOOR))).astype(BF16)
        g_ref[:, i * 128:(i + 1) * 128] = g
        gm_ref[:, i * 128:(i + 1) * 128] = jnp.where(same, g.astype(F32), 0.0).astype(BF16)

    spread(3, 5)
    forward(1, 7)

    def put_v(v, lane):
        both = jnp.concatenate(
            [v[:, 0:128].reshape(NRES, ROWS, 128), v[:, 128:256].reshape(NRES, ROWS, 128)], axis=1
        )
        v_ref[:, :, pl.ds(lane, 128)] = both.astype(BF16)

    def v_step(p):
        put_v(dot(g_ref[...], tp[pl.ds(pl.multiple_of(p * 256, 256), 256), :], NT), pl.multiple_of(p * 128, 128))

    def rs1(d, kz):
        dst = zpeer(kz) * NY + ypeer(2)
        src = v_ref.at[dst, :, d * HALF:(d + 1) * HALF]
        return rc(src, ry1.at[d, kz], rs1_s.at[d, kz], rs1_r.at[d, kz], res=z * NY + ypeer(3 - 2 * d))

    def rs2(d, kz):
        dst = zpeer(kz) * NY + ypeer(3 - 2 * d)
        return rc(v_ref.at[dst], ry2.at[d, kz], rs2_s.at[d, kz], rs2_r.at[d, kz], res=z * NY + ypeer(3 - 2 * d))

    def rsz(k):
        return rc(vsum.at[k], rz.at[k], rsz_s.at[k], rsz_r.at[k], res=zpeer(k) * NY + y)

    def second(*turns):
        for kz in turns:
            for d in range(2):
                slab = zpeer(kz) * NY + ypeer(3 - 2 * d)
                lanes = slice(d * HALF, (d + 1) * HALF)
                rs1(d, kz).wait_recv()
                v_ref[slab, :, lanes] = (v_ref[slab, :, lanes].astype(F32) + ry1[d, kz].astype(F32)).astype(BF16)
                rs2(d, kz).start()

    def third(*turns):
        for kz in turns:
            total = v_ref[zpeer(kz) * NY + y].astype(F32)
            for d in range(2):
                rs2(d, kz).wait_recv()
                total = total + ry2[d, kz].astype(F32)
            if kz:
                vsum[kz] = total.astype(BF16)
                rsz(kz).start()
        return total

    pl.loop(0, 4)(v_step)
    spread(4)
    forward(2, 6)
    pl.loop(4, 8)(v_step)
    forward(3)
    for q in range(2):
        put_v(dot(gm_ref[...], tu[q * 256:(q + 1) * 256, :], NT), 1024 + q * 128)
    forward(5)
    for kz in (4, 3, 5, 2, 6):
        for d in range(2):
            rs1(d, kz).start()
    forward(4)
    for kz in (1, 7, 0):
        for d in range(2):
            rs1(d, kz).start()

    second(4, 3, 5)
    for kz in range(NZ):
        for d in range(2):
            agf(d, kz).wait_recv()

    @pl.loop(0, NRES // 2)
    def _(d):
        a, b = rx[2 * d].astype(F32), rx[2 * d + 1].astype(F32)
        rows = pl.ds(pl.multiple_of(d * 16, 16), 16)
        for h in range(2):
            both = jnp.concatenate([a[h * 8:h * 8 + 8], b[h * 8:h * 8 + 8]], axis=0).astype(BF16)
            for p in range(8):
                rp[rows, p * 256 + h * 128:p * 256 + (h + 1) * 128] = both[:, p * 128:(p + 1) * 128]
            for q in range(2):
                ru[rows, q * 256 + h * 128:q * 256 + (h + 1) * 128] = both[:, 1024 + q * 128:1024 + (q + 1) * 128]

    second(2, 6)

    def u_step(p):
        u = dot(rp[:, pl.ds(pl.multiple_of(p * 256, 256), 256)], g_ref[...], TN).astype(BF16)
        for h in range(2):
            for a in range(2):
                lane = pl.multiple_of((h * 16 + 2 * p + a) * 128, 128)
                for i in range(ROWS):
                    ucat[i * SLOTS:i * SLOTS + PAIRED, pl.ds(lane, 128)] = u[(h * 2 + a) * 64:(h * 2 + a + 1) * 64, i * 128:(i + 1) * 128]

    pl.loop(0, 3)(u_step)
    second(1, 7, 0)
    pl.loop(3, 6)(u_step)
    third(4, 3, 5)
    pl.loop(6, 8)(u_step)
    for q in range(2):
        u = dot(ru[:, q * 256:(q + 1) * 256], gm_ref[...], TN).astype(BF16)
        for h in range(2):
            for a in range(8):
                lane = (h * 16 + q * 8 + a) * 128
                for i in range(ROWS):
                    ucat[i * SLOTS + PAIRED:(i + 1) * SLOTS, lane:lane + 128] = u[(h * 8 + a) * 16:(h * 8 + a + 1) * 16, i * 128:(i + 1) * 128]

    @pl.loop(0, 16)
    def _(g):
        dw = dot(lt[...], ucat[:, pl.ds(pl.multiple_of(g * 256, 256), 256)])
        for a in range(2):
            part = dw[:, a * 128:(a + 1) * 128]
            row = pl.multiple_of((g % 2) * 64 + a * 32, 32)
            dwf[g // 2, pl.ds(row, 32), :] = part
            dws[g // 2, pl.ds(row, 32), :] = part.astype(BF16)

    def pdp(k):
        return rc(dws.at[dpeer(k)], a_rx.at[k], p_s.at[k], p_r.at[k], dp=dpeer(k))

    for k in range(1, NDP):
        pdp(k).start()

    third(2, 6)

    def left_step(k, acc):
        cols = pl.ds(pl.multiple_of(k * 512, 512), 512)
        return acc + dot(ucat[:, cols], w2_ref[:, cols], NT)

    lgrad = lax.fori_loop(0, 8, left_step, jnp.zeros((ENT, C_H), F32))
    own = third(1, 7, 0)

    def td(c, k):
        return rc(sm.at[c, dpeer(k)], t_rx.at[c, k], td_s.at[c, k], td_r.at[c, k], dp=dpeer(k))

    def ur(c, k):
        return rc(e_rx.at[c, me], e_rx.at[c, me], ur_s.at[c, k], ur_r.at[c, k], res=(me + k) % NRES)

    def wd(c, k):
        return rc(so.at[c, dp], so.at[c, dp], wd_s.at[c, k], wd_r.at[c, k], dp=dpeer(k))

    rows8 = iota((8, C_Z), 0)

    def small_first(c, gw, tail_rows):
        tail = jnp.zeros((8, C_Z), F32)
        for k, row in enumerate(tail_rows):
            tail = jnp.where(rows8 == k, row, tail)
        main = jnp.concatenate([gw[:, 0:128], gw[:, 128:256]], axis=0).reshape(8, 8, C_Z)
        tails = jnp.broadcast_to(tail.reshape(8, 1, C_Z), (8, 8, C_Z))
        sm[c] = jnp.concatenate([main, tails], axis=1).astype(BF16)
        for k in range(1, NDP):
            td(c, k).start()

    def small_second(c):
        s = sm[c, dp].astype(F32)
        for k in range(1, NDP):
            td(c, k).wait_recv()
            s = s + t_rx[c, k].astype(F32)
        e_rx[c, me] = s.astype(BF16)

        @pl.loop(1, NRES)
        def _(k):
            ur(c, k).start()

    def small_third(c):
        @pl.loop(1, NRES)
        def _(k):
            ur(c, k).wait_recv()

        so[c, dp] = (jnp.sum(e_rx[c].astype(F32), axis=0) * (1.0 / N)).astype(BF16)
        for k in range(1, NDP):
            wd(c, k).start()

    def small_last(c, gw_ref):
        for k in range(1, NDP):
            wd(c, k).wait_recv()
        for d in range(NDP):
            part = so[c, d].astype(F32)
            sm_f = part[0:8]
            tail_ref[c * 8 + d:c * 8 + d + 1, :] = part[8:9]
            if d == 0:
                blocks = []
            blocks.append(sm_f)
        gw_ref[0:128, :] = jnp.transpose(jnp.concatenate(blocks[0:4], axis=0))
        gw_ref[128:256, :] = jnp.transpose(jnp.concatenate(blocks[4:8], axis=0))

    gw_l = jnp.zeros((C_H, C_M), F32)
    gb_l = jnp.zeros((1, C_H), F32)
    for r in range(ROWS):
        rows = slice(r * SLOTS, (r + 1) * SLOTS)
        lact = (lgrad[rows] * slot_mask(r, (SLOTS, C_H), 0)).astype(BF16)
        gw_l = gw_l + dot(lact, normed[rows, :], TN)
        gb_l = gb_l + jnp.sum(lact.astype(F32), axis=0, keepdims=True)
        lrow[rows, :] = lact
    small_first(0, gw_l, (
        jnp.sum(obg, axis=0, keepdims=True),
        jnp.concatenate([gb_l, jnp.zeros((1, 96), F32)], axis=1),
    ))

    @pl.loop(0, 4)
    def _(g):
        cols = pl.ds(pl.multiple_of(g * 256, 256), 256)
        main = dot(rp[...], tp[:, cols])
        side = dot(ru[...], tu[:, cols])
        for a in range(2):
            i = 2 * g + a
            ch = jnp.int32(0)
            iv = jnp.zeros((1, C_Z), F32)
            for r in range(ROWS):
                ch = jnp.where(i == r, chain[r], ch)
                iv = jnp.where(i == r, inv_own[r], iv)
            same = chain_col == ch.astype(F32)
            m, s = main[:, a * 128:(a + 1) * 128], side[:, a * 128:(a + 1) * 128]
            out = jnp.where(same, (m + s) * iv, m * (1.0 / (PAIRED + NORM_FLOOR))) + obias_ref[...]
            upd_ref[i] = out.astype(BF16)

    s = dwf[dp]
    for k in range(1, NDP):
        pdp(k).wait_recv()
        s = s + a_rx[k].astype(F32)
    s1[...] = s.reshape(NZ, 16, C_Z)

    def bz(k):
        return rc(s1.at[zpeer(k)], b_rx.at[k], bz_s.at[k], bz_r.at[k], res=zpeer(k) * NY + y)

    for k in range(1, NZ):
        bz(k).start()

    small_second(0)

    for kz in (4, 3, 5, 2, 6, 1, 7):
        rsz(kz).wait_recv()
        own = own + rz[kz].astype(F32)
    tiles = []
    for e in range(16):
        tiles.append(jnp.concatenate([own[:, e * 64:(e + 1) * 64], own[:, 1024 + e * 16:1024 + (e + 1) * 16]], axis=1))
    back = dot(permq, jnp.concatenate(tiles, axis=0).astype(BF16), TN)

    gw_r = jnp.zeros((C_H, C_M), F32)
    gb_r = jnp.zeros((C_H, 1), F32)
    gain_g = jnp.zeros((1, C_M), F32)
    shift_g = jnp.zeros((1, C_M), F32)
    for r in range(ROWS):
        rows = slice(r * SLOTS, (r + 1) * SLOTS)
        ract_t = (back[r * C_H:(r + 1) * C_H, :] * slot_mask(r, (C_H, SLOTS), 1)).astype(BF16)
        gw_r = gw_r + dot(ract_t, normed[rows, :])
        gb_r = gb_r + jnp.sum(ract_t.astype(F32), axis=1, keepdims=True)
        gn = dot(lrow[rows, :], wt_ref[0:C_H, :]) + dot(ract_t, wt_ref[C_H:, :], TN)
        scaled = xc[rows, :]
        gain_g = gain_g + jnp.sum(gn * scaled, axis=0, keepdims=True)
        shift_g = shift_g + jnp.sum(gn, axis=0, keepdims=True)
        gg = gn * gain_ref[...]
        mean_g = jnp.mean(gg, axis=-1, keepdims=True)
        mean_p = jnp.mean(gg * scaled, axis=-1, keepdims=True)
        ract[rows, :] = (inv_ref[rows, :] * (gg - mean_g - scaled * mean_p)).astype(BF16)
    gbr_row = jnp.transpose(jnp.broadcast_to(gb_r, (C_H, 128)))[0:1, :]
    small_first(1, gw_r, (
        gain_g[:, 0:128], gain_g[:, 128:256], shift_g[:, 0:128], shift_g[:, 128:256],
        jnp.concatenate([gbr_row, jnp.zeros((1, 96), F32)], axis=1),
    ))

    s = s1[z]
    for k in range(1, NZ):
        bz(k).wait_recv()
        s = s + b_rx[k]
    c_rx[y] = s

    def cy(k):
        return rc(c_rx.at[y], c_rx.at[y], cy_s.at[k], cy_r.at[k], res=z * NY + ypeer(k))

    for k in range(1, NY):
        cy(k).start()

    small_second(1)

    for k in range(1, NY):
        cy(k).wait_recv()
    s4[z] = ((c_rx[0] + c_rx[1] + c_rx[2] + c_rx[3]) * (1.0 / N)).astype(BF16)

    def dz(k):
        return rc(s4.at[z], s4.at[z], dz_s.at[k], dz_r.at[k], res=zpeer(k) * NY + y)

    for k in range(1, NZ):
        dz(k).start()

    small_third(0)

    for b in range(PAIRED // 16):
        src = jnp.concatenate([ract[r * SLOTS + b * 16:r * SLOTS + b * 16 + 16, :] for r in range(ROWS)], axis=0)
        agrad_ref[b * 128:(b + 1) * 128, :] = dot(perm0, src, TN).astype(BF16)
    src = jnp.concatenate([ract[r * SLOTS + PAIRED:(r + 1) * SLOTS, :] for r in range(ROWS)], axis=0)
    agrad_ref[PAIRED * ROWS:, :] = dot(pick, src, TN).astype(BF16)

    for k in range(1, NZ):
        dz(k).wait_recv()
    d_rx[dp] = s4[...].reshape(128, C_Z)

    def ed(k):
        return rc(d_rx.at[dp], d_rx.at[dp], ed_s.at[k], ed_r.at[k], dp=dpeer(k))

    for k in range(1, NDP):
        ed(k).start()

    small_third(1)
    small_last(0, lw_ref)
    for k in range(1, NDP):
        ed(k).wait_recv()
    for d in range(NDP):
        for a in range(4):
            dw_ref[:, d * 4 + a, :] = d_rx[d, a * 32:(a + 1) * 32, :].astype(F32)

    small_last(1, rw_ref)

    for k in range(1, NZ):
        for c in (agz, rsz, bz, dz):
            c(k).wait_send()
    for k in range(1, NDP):
        for c in (pdp, ed):
            c(k).wait_send()
        for c in range(2):
            td(c, k).wait_send()
            wd(c, k).wait_send()
    for c in range(2):
        @pl.loop(1, NRES)
        def _(k):
            ur(c, k).wait_send()
    for k in range(1, NY):
        cy(k).wait_send()
    for kz in range(NZ):
        for d in range(2):
            for c in (agy, agf, rs1, rs2):
                c(d, kz).wait_send()


def body(
    alignment, chain_ids, row_counts, norm_gain, norm_shift, left_weight, left_bias,
    right_weight, right_bias, out_weight, out_bias, pair_cotangent,
):
    wt = jnp.concatenate([left_weight, right_weight], axis=1).T
    bias = jnp.concatenate([left_bias, right_bias])
    vm = pl.BlockSpec(memory_space=pltpu.VMEM)
    sm = pl.BlockSpec(memory_space=pltpu.SMEM)
    sems = lambda *shape: pltpu.SemaphoreType.DMA(shape)
    vmem = pltpu.VMEM
    scratch = [
        vmem((128 * ROWS, C_M), BF16), vmem((ROWS, N, C_Z), BF16),
        vmem((ENT, C_M), F32), vmem((ENT, C_M), BF16), vmem((ENT, 1), F32),
        vmem((ENT, C_H), BF16), vmem((C_H, ENT), BF16), vmem((256, 128), BF16),
        vmem((2048, 1024), BF16), vmem((512, 1024), BF16), vmem((N, 1024), BF16), vmem((N, 1024), BF16),
        vmem((NRES, 16, 1280), BF16), vmem((NRES, 16, 1280), BF16), vmem((N, 2048), BF16), vmem((N, 512), BF16),
        vmem((2, NZ, 16, HALF), BF16), vmem((2, NZ, 16, 1280), BF16), vmem((NZ, 16, 1280), BF16), vmem((NZ, 16, 1280), BF16),
        vmem((ENT, 4096), BF16),
        vmem((NDP, 128, C_Z), F32), vmem((NDP, 128, C_Z), BF16), vmem((NDP, 128, C_Z), BF16),
        vmem((NZ, 16, C_Z), F32), vmem((NZ, 16, C_Z), F32), vmem((NY, 16, C_Z), F32),
        vmem((NZ, 16, C_Z), BF16), vmem((NDP, 128, C_Z), BF16),
        vmem((2, NDP, 16, C_Z), BF16), vmem((2, NDP, 16, C_Z), BF16), vmem((2, NRES, 16, C_Z), BF16), vmem((2, NDP, 16, C_Z), BF16),
        vmem((ENT, C_M), BF16),
        sems(2), sems(NZ), sems(NZ), sems(2, NZ), sems(2, NZ), sems(2, NZ), sems(2, NZ),
        sems(2, NZ), sems(2, NZ), sems(2, NZ), sems(2, NZ), sems(NZ), sems(NZ),
        sems(NDP), sems(NDP), sems(NZ), sems(NZ), sems(NY), sems(NY), sems(NZ), sems(NZ), sems(NDP), sems(NDP),
        sems(2, NDP), sems(2, NDP), sems(2, NRES), sems(2, NRES), sems(2, NDP), sems(2, NDP),
    ]
    hbm = pl.BlockSpec(memory_space=pl.ANY)
    upd, agrad, dw, lw, rw, tails = pl.pallas_call(
        kernel,
        out_shape=(
            jax.ShapeDtypeStruct((ROWS, N, C_Z), BF16),
            jax.ShapeDtypeStruct((128 * ROWS, C_M), BF16),
            jax.ShapeDtypeStruct((C_H, C_H, C_Z), F32),
            jax.ShapeDtypeStruct((C_M, C_H), F32),
            jax.ShapeDtypeStruct((C_M, C_H), F32),
            jax.ShapeDtypeStruct((16, C_Z), F32),
        ),
        in_specs=[sm, sm, vm, hbm] + [vm] * 7 + [hbm],
        out_specs=(vm,) * 6,
        scratch_shapes=scratch,
        compiler_params=pltpu.CompilerParams(
            collective_id=0, has_side_effects=True, vmem_limit_bytes=50 * 1024 * 1024
        ),
    )(
        chain_ids, row_counts, chain_ids, alignment.reshape(128 * ROWS, C_M),
        norm_gain.reshape(1, C_M), norm_shift.reshape(1, C_M), wt,
        bias.reshape(2, C_H), bias.reshape(2 * C_H, 1),
        out_weight.reshape(C_H, C_H * C_Z), out_bias.reshape(1, C_Z), pair_cotangent[0],
    )
    return (
        upd[None],
        agrad.reshape(1, 128, ROWS, C_M),
        lw,
        tails[1, 0:C_H],
        rw,
        tails[12, 0:C_H],
        dw.reshape(C_H * C_H, C_Z),
        tails[0],
        tails[8:10].reshape(C_M),
        tails[10:12].reshape(C_M),
    )


def solution(mesh):
    return jax.shard_map(
        body,
        mesh=mesh,
        in_specs=(
            P("dp", None, "res", None), P("dp", None), P("dp", None), P(), P(), P(), P(), P(), P(), P(), P(),
            P("dp", "res", None, None),
        ),
        out_specs=(
            P("dp", "res", None, None), P("dp", None, "res", None), P(), P(), P(), P(), P(), P(), P(), P(),
        ),
        check_vma=False,
    )
```

```python
import functools

import jax
import jax.numpy as jnp
from jax import lax
from jax.experimental import pallas as pl
from jax.experimental.pallas import tpu as pltpu
from jax.sharding import PartitionSpec as P

C_M = 256
C_H = 32
C_Z = 128
PAIRED = 64
UNP = 64
MOST = 16
CHAINS = 12
EPSILON = 1e-05
NORM_FLOOR = 0.001

ROWS = 8
SLOTS = PAIRED + MOST
NY, NZ, NDP = 4, 8, 8
NRES = NY * NZ
N = ROWS * NRES
ENT = ROWS * SLOTS
HALF = 640
F32, BF16 = jnp.float32, jnp.bfloat16
MESH = pl.DeviceIdType.MESH

NN = (((1,), (0,)), ((), ()))
NT = (((1,), (1,)), ((), ()))
TN = (((0,), (0,)), ((), ()))


def dot(a, b, dims=NN):
    return lax.dot_general(a, b, dims, preferred_element_type=F32)


def iota(shape, dim):
    return lax.broadcasted_iota(jnp.int32, shape, dim)


def onehot(cond):
    return jnp.where(cond, 1.0, 0.0).astype(BF16)


def kernel(
    chain_h, counts_h, x_h, gain_h, shift_h, lw_h, lb_h, rw_h, rb_h, w_h, ob_h, cot_h,
    upd_h, agrad_h, dw_h, small_h,
    upd_ref, agrad_ref, chain_s, counts_s, chain_v, x_ref, gain_ref, shift_ref, lb_ref, rb_ref, w_ref, obias_ref, cot_ref,
    wt_ref, wf, w2_ref,
    xc, normed, inv_ref, lrow, lt, q_ref, tp, tu, g_ref, gm_ref, v_ref, rx, rp, ru,
    ry1, ry2, vsum, rz, ucat, dwf, dws, a_rx, s1, b_rx, c_rx, s4, d_rx,
    sm, t_rx, e_rx, so, ract,
    in_s, out_s, agz_s, agz_r, agy_s, agy_r, agf_s, agf_r, rs1_s, rs1_r, rs2_s, rs2_r, rsz_s, rsz_r,
    p_s, p_r, bz_s, bz_r, cy_s, cy_r, dz_s, dz_r, ed_s, ed_r,
    td_s, td_r, ur_s, ur_r, wd_s, wd_r,
):
    me = lax.axis_index("res")
    dp = lax.axis_index("dp")
    z, y = me // NY, me % NY

    def zpeer(k):
        return (z + k) % NZ

    def ypeer(k):
        return (y + k) % NY

    def dpeer(k):
        return (dp + k) % NDP

    def rc(src, dst, ss, rs, **where):
        return pltpu.make_async_remote_copy(
            src_ref=src, dst_ref=dst, send_sem=ss, recv_sem=rs,
            device_id=where, device_id_type=MESH,
        )

    fetches = [
        pltpu.make_async_copy(src, dst, in_s.at[n])
        for n, (src, dst) in enumerate((
            (x_h, x_ref), (chain_h, chain_s), (counts_h, counts_s), (chain_h, chain_v), (gain_h, gain_ref),
            (shift_h, shift_ref), (lw_h, wt_ref.at[0:C_H]), (lb_h, lb_ref), (rw_h, wt_ref.at[C_H:2 * C_H]), (rb_h, rb_ref),
            (w_h, w_ref), (ob_h, obias_ref), (cot_h, cot_ref),
        ))
    ]
    for f in fetches:
        f.start()

    barrier = pltpu.get_barrier_semaphore()

    @pl.loop(1, NRES)
    def _(k):
        pl.semaphore_signal(barrier, inc=1, device_id={"res": (me + k) % NRES}, device_id_type=MESH)

    for k in range(1, NDP):
        pl.semaphore_signal(barrier, inc=1, device_id={"dp": dpeer(k)}, device_id_type=MESH)

    for f in fetches[:10]:
        f.wait()
    rb_col = jnp.transpose(jnp.broadcast_to(rb_ref[...], (8, C_H)))[:, 0:1]

    chain, start, count, base = [], [], [], []
    for r in range(ROWS):
        c = chain_s[0, me * ROWS + r]
        st = jnp.int32(0)
        ct = jnp.int32(0)
        for k in range(CHAINS):
            v = counts_s[0, k]
            st = st + jnp.where(c > k, v, 0)
            ct = ct + jnp.where(c == k, v, 0)
        chain.append(c)
        start.append(st)
        count.append(ct)
        base.append(jnp.minimum(st, UNP - MOST))

    def slot_mask(r, shape, dim):
        s = iota(shape, dim)
        row = s - PAIRED + base[r]
        live = (row >= start[r]) & (row < start[r] + count[r])
        return jnp.where((s < PAIRED) | live, 1.0, 0.0)

    ro, co = iota((128, 128), 0), iota((128, 128), 1)
    perm0 = onehot(co == (ro % 16) * ROWS + ro // 16)
    for b in range(PAIRED // 16):
        part = dot(perm0, x_ref[b * 128:(b + 1) * 128, :])
        for r in range(ROWS):
            xc[r * SLOTS + b * 16:r * SLOTS + b * 16 + 16, :] = part[r * 16:(r + 1) * 16]
    ru_i = iota((128, UNP * ROWS), 0)
    base_rows = jnp.zeros((128, UNP * ROWS), jnp.int32)
    for r in range(ROWS):
        base_rows = jnp.where(ru_i // 16 == r, base[r], base_rows)
    pick = onehot(iota((128, UNP * ROWS), 1) == (base_rows + ru_i % 16) * ROWS + ru_i // 16)
    part = dot(pick, x_ref[PAIRED * ROWS:, :])
    for r in range(ROWS):
        xc[r * SLOTS + PAIRED:(r + 1) * SLOTS, :] = part[r * 16:(r + 1) * 16]

    for r in range(ROWS):
        rows = slice(r * SLOTS, (r + 1) * SLOTS)
        floats = xc[rows, :]
        centred = floats - jnp.mean(floats, axis=-1, keepdims=True)
        inverse = lax.rsqrt(jnp.mean(centred * centred, axis=-1, keepdims=True) + EPSILON)
        scaled = centred * inverse
        nrm = (scaled * gain_ref[...] + shift_ref[...]).astype(BF16)
        xc[rows, :] = scaled
        inv_ref[rows, :] = inverse
        normed[rows, :] = nrm
        left = (dot(nrm, wt_ref[0:C_H, :], NT) + lb_ref[...]) * slot_mask(r, (SLOTS, C_H), 0)
        lrow[rows, :] = left.astype(BF16)
        right = (dot(wt_ref[C_H:, :], nrm, NT) + rb_col) * slot_mask(r, (C_H, SLOTS), 1)
        q_ref[r * C_H:(r + 1) * C_H, 0:SLOTS] = right.astype(BF16)
    re, ce = iota((256, 256), 0), iota((256, 256), 1)
    permq = onehot(ce == (re % 8) * 32 + ((re // 8) % 2) * 16 + re // 16)
    mixed = dot(permq, q_ref[:, 0:SLOTS])
    for p in range(8):
        rx[me, :, p * 128:(p + 1) * 128] = jnp.concatenate(
            [mixed[(2 * p + a) * 16:(2 * p + a + 1) * 16, 0:PAIRED] for a in range(2)], axis=1
        ).astype(BF16)
    for q in range(2):
        rx[me, :, 1024 + q * 128:1024 + (q + 1) * 128] = jnp.concatenate(
            [mixed[(8 * q + a) * 16:(8 * q + a + 1) * 16, PAIRED:SLOTS] for a in range(8)], axis=1
        ).astype(BF16)

    pl.semaphore_wait(barrier, NRES + NDP - 2)

    def agz(k):
        return rc(rx.at[me], rx.at[me], agz_s.at[k], agz_r.at[k], res=zpeer(k) * NY + y)

    def agy(d, kz):
        slot = ((z - kz + NZ) % NZ) * NY + y
        return rc(rx.at[slot], rx.at[slot], agy_s.at[d, kz], agy_r.at[d, kz], res=z * NY + ypeer(1 + 2 * d))

    def agf(d, kz):
        slot = ((z - kz + NZ) % NZ) * NY + ypeer(3 - 2 * d)
        part = rx.at[slot, :, d * HALF:(d + 1) * HALF]
        return rc(part, part, agf_s.at[d, kz], agf_r.at[d, kz], res=z * NY + ypeer(1 + 2 * d))

    def spread(*turns):
        for kz in turns:
            if kz:
                agz(kz).wait_recv()
            for d in range(2):
                agy(d, kz).start()

    def forward(*turns):
        for kz in turns:
            for d in range(2):
                agy(d, kz).wait_recv()
                agf(d, kz).start()

    spread(0)
    for k in (1, 7, 2, 6, 3, 5, 4):
        agz(k).start()

    for f in fetches[10:]:
        f.wait()
    wf[...] = w_ref[...].astype(F32)
    for e in range(C_H):
        w2_ref[:, e * 128:(e + 1) * 128] = wf[pl.ds(e, C_H, stride=C_H), :].astype(BF16)

    lt[...] = jnp.transpose(lrow[...].astype(F32)).astype(BF16)

    def t_step(g):
        h, p = g // 8, g % 8
        t = dot(lrow[...], w2_ref[:, pl.ds(pl.multiple_of(g * 256, 256), 256)]).astype(BF16)
        rowp = pl.multiple_of((p * 2 + h) * 128, 128)
        rowu = pl.multiple_of(((p // 4) * 2 + h) * 128 + (p % 4) * 32, 32)
        for i in range(ROWS):
            for a in range(2):
                tp[pl.ds(rowp + a * 64, 64), i * 128:(i + 1) * 128] = t[i * SLOTS:i * SLOTS + PAIRED, a * 128:(a + 1) * 128]
                tu[pl.ds(rowu + a * 16, 16), i * 128:(i + 1) * 128] = t[i * SLOTS + PAIRED:(i + 1) * SLOTS, a * 128:(a + 1) * 128]

    pl.loop(0, 12)(t_step)
    spread(1, 7)
    pl.loop(12, 16)(t_step)
    spread(2, 6)
    forward(0)

    chain_col = jnp.transpose(jnp.broadcast_to(chain_v[...].astype(F32), (128, N)))
    obg = jnp.zeros((8, C_Z), F32)
    inv_own = []
    for i in range(ROWS):
        same = chain_col == chain[i].astype(F32)
        cntf = jnp.full((8, C_Z), count[i].astype(F32))
        inv_own.append((1.0 / (PAIRED + cntf + NORM_FLOOR))[0:1, :])
        raw = cot_ref[i].astype(F32)
        obg = obg + jnp.sum(raw.reshape(N // 8, 8, C_Z), axis=0)
        g = (raw * jnp.where(same, inv_own[i], 1.0 / (PAIRED + NORM_FLOOR))).astype(BF16)
        g_ref[:, i * 128:(i + 1) * 128] = g
        gm_ref[:, i * 128:(i + 1) * 128] = jnp.where(same, g.astype(F32), 0.0).astype(BF16)

    spread(3, 5)
    forward(1, 7)

    def put_v(v, lane):
        both = jnp.concatenate(
            [v[:, 0:128].reshape(NRES, ROWS, 128), v[:, 128:256].reshape(NRES, ROWS, 128)], axis=1
        )
        v_ref[:, :, pl.ds(lane, 128)] = both.astype(BF16)

    def v_step(p):
        put_v(dot(g_ref[...], tp[pl.ds(pl.multiple_of(p * 256, 256), 256), :], NT), pl.multiple_of(p * 128, 128))

    def rs1(d, kz):
        dst = zpeer(kz) * NY + ypeer(2)
        src = v_ref.at[dst, :, d * HALF:(d + 1) * HALF]
        return rc(src, ry1.at[d, kz], rs1_s.at[d, kz], rs1_r.at[d, kz], res=z * NY + ypeer(3 - 2 * d))

    def rs2(d, kz):
        dst = zpeer(kz) * NY + ypeer(3 - 2 * d)
        return rc(v_ref.at[dst], ry2.at[d, kz], rs2_s.at[d, kz], rs2_r.at[d, kz], res=z * NY + ypeer(3 - 2 * d))

    def rsz(k):
        return rc(vsum.at[k], rz.at[k], rsz_s.at[k], rsz_r.at[k], res=zpeer(k) * NY + y)

    def second(*turns):
        for kz in turns:
            for d in range(2):
                slab = zpeer(kz) * NY + ypeer(3 - 2 * d)
                lanes = slice(d * HALF, (d + 1) * HALF)
                rs1(d, kz).wait_recv()
                v_ref[slab, :, lanes] = (v_ref[slab, :, lanes].astype(F32) + ry1[d, kz].astype(F32)).astype(BF16)
                rs2(d, kz).start()

    def third(*turns):
        for kz in turns:
            total = v_ref[zpeer(kz) * NY + y].astype(F32)
            for d in range(2):
                rs2(d, kz).wait_recv()
                total = total + ry2[d, kz].astype(F32)
            if kz:
                vsum[kz] = total.astype(BF16)
                rsz(kz).start()
        return total

    pl.loop(0, 4)(v_step)
    spread(4)
    forward(2, 6)
    pl.loop(4, 8)(v_step)
    forward(3)
    for q in range(2):
        put_v(dot(gm_ref[...], tu[q * 256:(q + 1) * 256, :], NT), 1024 + q * 128)
    forward(5)
    for kz in (4, 3, 5, 2, 6):
        for d in range(2):
            rs1(d, kz).start()
    forward(4)
    for kz in (1, 7, 0):
        for d in range(2):
            rs1(d, kz).start()

    for kz in range(NZ):
        for d in range(2):
            agf(d, kz).wait_recv()

    @pl.loop(0, NRES // 2)
    def _(d):
        a, b = rx[2 * d].astype(F32), rx[2 * d + 1].astype(F32)
        rows = pl.ds(pl.multiple_of(d * 16, 16), 16)
        for h in range(2):
            both = jnp.concatenate([a[h * 8:h * 8 + 8], b[h * 8:h * 8 + 8]], axis=0).astype(BF16)
            for p in range(8):
                rp[rows, p * 256 + h * 128:p * 256 + (h + 1) * 128] = both[:, p * 128:(p + 1) * 128]
            for q in range(2):
                ru[rows, q * 256 + h * 128:q * 256 + (h + 1) * 128] = both[:, 1024 + q * 128:1024 + (q + 1) * 128]

    def u_step(p):
        u = dot(rp[:, pl.ds(pl.multiple_of(p * 256, 256), 256)], g_ref[...], TN).astype(BF16)
        for h in range(2):
            for a in range(2):
                lane = pl.multiple_of((h * 16 + 2 * p + a) * 128, 128)
                for i in range(ROWS):
                    ucat[i * SLOTS:i * SLOTS + PAIRED, pl.ds(lane, 128)] = u[(h * 2 + a) * 64:(h * 2 + a + 1) * 64, i * 128:(i + 1) * 128]

    pl.loop(0, 3)(u_step)
    second(4, 3, 5)
    pl.loop(3, 6)(u_step)
    second(2, 6, 1)
    pl.loop(6, 8)(u_step)
    for q in range(2):
        u = dot(ru[:, q * 256:(q + 1) * 256], gm_ref[...], TN).astype(BF16)
        for h in range(2):
            for a in range(8):
                lane = (h * 16 + q * 8 + a) * 128
                for i in range(ROWS):
                    ucat[i * SLOTS + PAIRED:(i + 1) * SLOTS, lane:lane + 128] = u[(h * 8 + a) * 16:(h * 8 + a + 1) * 16, i * 128:(i + 1) * 128]

    second(7, 0)
    third(4, 3, 5)

    @pl.loop(0, 16)
    def _(g):
        dw = dot(lt[...], ucat[:, pl.ds(pl.multiple_of(g * 256, 256), 256)])
        for a in range(2):
            part = dw[:, a * 128:(a + 1) * 128]
            row = pl.multiple_of((g % 2) * 64 + a * 32, 32)
            dwf[g // 2, pl.ds(row, 32), :] = part
            dws[g // 2, pl.ds(row, 32), :] = part.astype(BF16)

    def pdp(k):
        return rc(dws.at[dpeer(k)], a_rx.at[k], p_s.at[k], p_r.at[k], dp=dpeer(k))

    for k in range(1, NDP):
        pdp(k).start()

    own = third(2, 6, 1, 7, 0)

    def left_step(k, acc):
        cols = pl.ds(pl.multiple_of(k * 512, 512), 512)
        return acc + dot(ucat[:, cols], w2_ref[:, cols], NT)

    lgrad = lax.fori_loop(0, 8, left_step, jnp.zeros((ENT, C_H), F32))

    def td(c, k):
        return rc(sm.at[c, dpeer(k)], t_rx.at[c, k], td_s.at[c, k], td_r.at[c, k], dp=dpeer(k))

    def ur(c, k):
        return rc(e_rx.at[c, me], e_rx.at[c, me], ur_s.at[c], ur_r.at[c], res=(me + k) % NRES)

    def wd(c, k):
        return rc(so.at[c, dp], so.at[c, dp], wd_s.at[c, k], wd_r.at[c, k], dp=dpeer(k))

    rows8 = iota((8, C_Z), 0)

    def small_first(c, gw, tail_rows):
        tail = jnp.zeros((8, C_Z), F32)
        for k, row in enumerate(tail_rows):
            tail = jnp.where(rows8 == k, row, tail)
        main = jnp.concatenate([gw[:, 0:128], gw[:, 128:256]], axis=0).reshape(8, 8, C_Z)
        tails = jnp.broadcast_to(tail.reshape(8, 1, C_Z), (8, 8, C_Z))
        sm[c] = jnp.concatenate([main, tails], axis=1).astype(BF16)
        for k in range(1, NDP):
            td(c, k).start()

    def small_second(c):
        s = sm[c, dp].astype(F32)
        for k in range(1, NDP):
            td(c, k).wait_recv()
            s = s + t_rx[c, k].astype(F32)
        e_rx[c, me] = s.astype(BF16)

        @pl.loop(1, NRES)
        def _(k):
            ur(c, k).start()

    def small_third(c):
        others = e_rx.at[c, 0:NRES - 1]
        rc(others, others, ur_s.at[c], ur_r.at[c], res=(me + 1) % NRES).wait()

        so[c, dp] = (jnp.sum(e_rx[c].astype(F32), axis=0) * (1.0 / N)).astype(BF16)
        for k in range(1, NDP):
            wd(c, k).start()

    gw_l = jnp.zeros((C_H, C_M), F32)
    gb_l = jnp.zeros((1, C_H), F32)
    for r in range(ROWS):
        rows = slice(r * SLOTS, (r + 1) * SLOTS)
        lact = (lgrad[rows] * slot_mask(r, (SLOTS, C_H), 0)).astype(BF16)
        gw_l = gw_l + dot(lact, normed[rows, :], TN)
        gb_l = gb_l + jnp.sum(lact.astype(F32), axis=0, keepdims=True)
        lrow[rows, :] = lact
    small_first(0, gw_l, (
        jnp.sum(obg, axis=0, keepdims=True),
        jnp.concatenate([gb_l, jnp.zeros((1, 96), F32)], axis=1),
    ))

    s = dwf[dp]
    for k in range(1, NDP):
        pdp(k).wait_recv()
        s = s + a_rx[k].astype(F32)
    s1[...] = s.reshape(NZ, 16, C_Z)

    def bz(k):
        return rc(s1.at[zpeer(k)], b_rx.at[k], bz_s.at[k], bz_r.at[k], res=zpeer(k) * NY + y)

    for k in range(1, NZ):
        bz(k).start()

    small_second(0)

    for kz in (4, 3, 5, 2, 6, 1, 7):
        rsz(kz).wait_recv()
        own = own + rz[kz].astype(F32)
    tiles = []
    for e in range(16):
        tiles.append(jnp.concatenate([own[:, e * 64:(e + 1) * 64], own[:, 1024 + e * 16:1024 + (e + 1) * 16]], axis=1))
    back = dot(permq, jnp.concatenate(tiles, axis=0).astype(BF16), TN)

    gw_r = jnp.zeros((C_H, C_M), F32)
    gb_r = jnp.zeros((C_H, 1), F32)
    gain_g = jnp.zeros((1, C_M), F32)
    shift_g = jnp.zeros((1, C_M), F32)
    for r in range(ROWS):
        rows = slice(r * SLOTS, (r + 1) * SLOTS)
        ract_t = (back[r * C_H:(r + 1) * C_H, :] * slot_mask(r, (C_H, SLOTS), 1)).astype(BF16)
        gw_r = gw_r + dot(ract_t, normed[rows, :])
        gb_r = gb_r + jnp.sum(ract_t.astype(F32), axis=1, keepdims=True)
        gn = dot(lrow[rows, :], wt_ref[0:C_H, :]) + dot(ract_t, wt_ref[C_H:, :], TN)
        scaled = xc[rows, :]
        gain_g = gain_g + jnp.sum(gn * scaled, axis=0, keepdims=True)
        shift_g = shift_g + jnp.sum(gn, axis=0, keepdims=True)
        gg = gn * gain_ref[...]
        mean_g = jnp.mean(gg, axis=-1, keepdims=True)
        mean_p = jnp.mean(gg * scaled, axis=-1, keepdims=True)
        ract[rows, :] = (inv_ref[rows, :] * (gg - mean_g - scaled * mean_p)).astype(BF16)
    gbr_row = jnp.transpose(jnp.broadcast_to(gb_r, (C_H, 128)))[0:1, :]
    small_first(1, gw_r, (
        gain_g[:, 0:128], gain_g[:, 128:256], shift_g[:, 0:128], shift_g[:, 128:256],
        jnp.concatenate([gbr_row, jnp.zeros((1, 96), F32)], axis=1),
    ))

    s = s1[z]
    for k in range(1, NZ):
        bz(k).wait_recv()
        s = s + b_rx[k]
    c_rx[y] = s

    def cy(k):
        return rc(c_rx.at[y], c_rx.at[y], cy_s.at[k], cy_r.at[k], res=z * NY + ypeer(k))

    for k in range(1, NY):
        cy(k).start()

    small_second(1)

    for k in range(1, NY):
        cy(k).wait_recv()
    s4[z] = ((c_rx[0] + c_rx[1] + c_rx[2] + c_rx[3]) * (1.0 / N)).astype(BF16)

    def dz(k):
        return rc(s4.at[z], s4.at[z], dz_s.at[k], dz_r.at[k], res=zpeer(k) * NY + y)

    for k in range(1, NZ):
        dz(k).start()

    small_third(0)

    @pl.loop(0, 4)
    def _(g):
        cols = pl.ds(pl.multiple_of(g * 256, 256), 256)
        main = dot(rp[...], tp[:, cols])
        side = dot(ru[...], tu[:, cols])
        for a in range(2):
            i = 2 * g + a
            ch = jnp.int32(0)
            iv = jnp.zeros((1, C_Z), F32)
            for r in range(ROWS):
                ch = jnp.where(i == r, chain[r], ch)
                iv = jnp.where(i == r, inv_own[r], iv)
            same = chain_col == ch.astype(F32)
            m, s = main[:, a * 128:(a + 1) * 128], side[:, a * 128:(a + 1) * 128]
            out = jnp.where(same, (m + s) * iv, m * (1.0 / (PAIRED + NORM_FLOOR))) + obias_ref[...]
            upd_ref[i] = out.astype(BF16)

    for b in range(PAIRED // 16):
        src = jnp.concatenate([ract[r * SLOTS + b * 16:r * SLOTS + b * 16 + 16, :] for r in range(ROWS)], axis=0)
        agrad_ref[b * 128:(b + 1) * 128, :] = dot(perm0, src, TN).astype(BF16)
    src = jnp.concatenate([ract[r * SLOTS + PAIRED:(r + 1) * SLOTS, :] for r in range(ROWS)], axis=0)
    agrad_ref[PAIRED * ROWS:, :] = dot(pick, src, TN).astype(BF16)

    upd_out = pltpu.make_async_copy(upd_ref, upd_h, out_s.at[0])
    upd_out.start()

    for k in range(1, NZ):
        dz(k).wait_recv()
    d_rx[dp] = s4[...].reshape(128, C_Z)

    def ed(k):
        return rc(d_rx.at[dp], d_rx.at[dp], ed_s.at[k], ed_r.at[k], dp=dpeer(k))

    for k in range(1, NDP):
        ed(k).start()

    small_third(1)
    agrad_out = pltpu.make_async_copy(agrad_ref, agrad_h, out_s.at[1])
    agrad_out.start()
    for kz in range(NZ):
        for d in range(2):
            for c in (agy, agf, rs1, rs2):
                c(d, kz).wait_send()
    for k in range(1, NZ):
        for c in (agz, rsz, bz, dz):
            c(k).wait_send()
    for k in range(1, NDP):
        pdp(k).wait_send()
        td(0, k).wait_send()
        td(1, k).wait_send()
        wd(0, k).wait_send()
    for k in range(1, NY):
        cy(k).wait_send()

    for k in range(1, NDP):
        wd(0, k).wait_recv()
    small0_out = pltpu.make_async_copy(so.at[0], small_h.at[0], out_s.at[2])
    small0_out.start()
    for k in range(1, NDP):
        ed(k).wait_recv()
    dw_out = pltpu.make_async_copy(d_rx, dw_h, out_s.at[3])
    dw_out.start()
    for k in range(1, NDP):
        wd(1, k).wait_recv()
    small1_out = pltpu.make_async_copy(so.at[1], small_h.at[1], out_s.at[4])
    small1_out.start()
    for k in range(1, NDP):
        ed(k).wait_send()
        wd(1, k).wait_send()
    for c in (upd_out, agrad_out, small0_out, dw_out, small1_out):
        c.wait()


def finish(
    upd_i, agrad_i, dw_i, small_i,
    upd_h, agrad_h, lw_h, lb_h, rw_h, rb_h, dw_h, ob_h, gain_h, shift_h,
    upd_v, agrad_v, dw_v, small_v, dw_f, lw_f, rw_f, lb_f, rb_f, ob_f, gain_f, shift_f, sem,
):
    copies = []

    def send(src, dst):
        copies.append(pltpu.make_async_copy(src, dst, sem.at[len(copies)]))
        copies[-1].start()

    fetches = [
        pltpu.make_async_copy(src, dst, sem.at[10 + n])
        for n, (src, dst) in enumerate(((dw_i, dw_v), (small_i, small_v), (upd_i, upd_v), (agrad_i, agrad_v)))
    ]
    for f in fetches:
        f.start()
    fetches[0].wait()
    for d in range(NDP):
        for a in range(4):
            dw_f[:, d * 4 + a, :] = dw_v[d, a * 32:(a + 1) * 32, :].astype(F32)
    send(dw_f, dw_h)
    fetches[2].wait()
    send(upd_v, upd_h)
    fetches[3].wait()
    send(agrad_v, agrad_h)
    fetches[1].wait()

    def tail(c, k):
        return small_v[c, k].astype(F32)[8:9]

    for c, (buf, out) in enumerate(((lw_f, lw_h), (rw_f, rw_h))):
        for half in range(2):
            rows = [small_v[c, half * 4 + d].astype(F32)[0:8] for d in range(4)]
            buf[:, half * 128:(half + 1) * 128] = jnp.concatenate(rows, axis=0)
        send(buf, out)
    ob_f[...] = tail(0, 0)
    lb_f[...] = tail(0, 1)[:, 0:C_H]
    rb_f[...] = tail(1, 4)[:, 0:C_H]
    gain_f[...] = jnp.concatenate([tail(1, 0), tail(1, 1)], axis=1)
    shift_f[...] = jnp.concatenate([tail(1, 2), tail(1, 3)], axis=1)
    for buf, out in ((ob_f, ob_h), (lb_f, lb_h), (rb_f, rb_h), (gain_f, gain_h), (shift_f, shift_h)):
        send(buf, out)
    for c in copies:
        c.wait()


def body(
    alignment, chain_ids, row_counts, norm_gain, norm_shift, left_weight, left_bias,
    right_weight, right_bias, out_weight, out_bias, pair_cotangent,
):
    sems = lambda *shape: pltpu.SemaphoreType.DMA(shape)
    vmem = pltpu.VMEM
    scratch = [
        vmem((ROWS, N, C_Z), BF16), vmem((128 * ROWS, C_M), BF16), pltpu.SMEM((1, N), jnp.int32), pltpu.SMEM((1, CHAINS), jnp.int32), vmem((1, N), jnp.int32),
        vmem((128 * ROWS, C_M), BF16), vmem((1, C_M), F32), vmem((1, C_M), F32), vmem((1, C_H), F32),
        vmem((1, C_H), F32), vmem((C_H * C_H, C_Z), BF16), vmem((1, C_Z), F32), vmem((ROWS, N, C_Z), BF16),
        vmem((2 * C_H, C_M), BF16), vmem((C_H * C_H, C_Z), F32), vmem((C_H, C_H * C_Z), BF16),
        vmem((ENT, C_M), F32), vmem((ENT, C_M), BF16), vmem((ENT, 1), F32),
        vmem((ENT, C_H), BF16), vmem((C_H, ENT), BF16), vmem((256, 128), BF16),
        vmem((2048, 1024), BF16), vmem((512, 1024), BF16), vmem((N, 1024), BF16), vmem((N, 1024), BF16),
        vmem((NRES, 16, 1280), BF16), vmem((NRES, 16, 1280), BF16), vmem((N, 2048), BF16), vmem((N, 512), BF16),
        vmem((2, NZ, 16, HALF), BF16), vmem((2, NZ, 16, 1280), BF16), vmem((NZ, 16, 1280), BF16), vmem((NZ, 16, 1280), BF16),
        vmem((ENT, 4096), BF16),
        vmem((NDP, 128, C_Z), F32), vmem((NDP, 128, C_Z), BF16), vmem((NDP, 128, C_Z), BF16),
        vmem((NZ, 16, C_Z), F32), vmem((NZ, 16, C_Z), F32), vmem((NY, 16, C_Z), F32),
        vmem((NZ, 16, C_Z), BF16), vmem((NDP, 128, C_Z), BF16),
        vmem((2, NDP, 16, C_Z), BF16), vmem((2, NDP, 16, C_Z), BF16), vmem((2, NRES, 16, C_Z), BF16), vmem((2, NDP, 16, C_Z), BF16),
        vmem((ENT, C_M), BF16),
        sems(13), sems(5), sems(NZ), sems(NZ), sems(2, NZ), sems(2, NZ), sems(2, NZ), sems(2, NZ),
        sems(2, NZ), sems(2, NZ), sems(2, NZ), sems(2, NZ), sems(NZ), sems(NZ),
        sems(NDP), sems(NDP), sems(NZ), sems(NZ), sems(NY), sems(NY), sems(NZ), sems(NZ), sems(NDP), sems(NDP),
        sems(2, NDP), sems(2, NDP), sems(2), sems(2), sems(2, NDP), sems(2, NDP),
    ]
    hbm = pl.BlockSpec(memory_space=pltpu.HBM)
    upd, agrad, dw, small = pl.pallas_call(
        kernel,
        out_shape=(
            jax.ShapeDtypeStruct((ROWS, N, C_Z), BF16),
            jax.ShapeDtypeStruct((128 * ROWS, C_M), BF16),
            jax.ShapeDtypeStruct((NDP, 128, C_Z), BF16),
            jax.ShapeDtypeStruct((2, NDP, 16, C_Z), BF16),
        ),
        in_specs=[hbm] * 12,
        out_specs=(hbm,) * 4,
        scratch_shapes=scratch,
        compiler_params=pltpu.CompilerParams(
            collective_id=0, has_side_effects=True, vmem_limit_bytes=56 * 1024 * 1024
        ),
    )(
        chain_ids, row_counts, alignment.reshape(128 * ROWS, C_M),
        norm_gain.reshape(1, C_M), norm_shift.reshape(1, C_M), left_weight.T, left_bias.reshape(1, C_H),
        right_weight.T, right_bias.reshape(1, C_H), out_weight, out_bias.reshape(1, C_Z), pair_cotangent[0],
    )
    outs = (
        ((ROWS, N, C_Z), BF16), ((128 * ROWS, C_M), BF16), ((C_H, C_M), F32), ((1, C_H), F32), ((C_H, C_M), F32),
        ((1, C_H), F32), ((C_H, C_H, C_Z), F32), ((1, C_Z), F32), ((1, C_M), F32), ((1, C_M), F32),
    )
    upd, agrad, lw, lb, rw, rb, dw, ob, gain, shift = pl.pallas_call(
        finish,
        out_shape=tuple(jax.ShapeDtypeStruct(*o) for o in outs),
        in_specs=[hbm] * 4,
        out_specs=(hbm,) * 10,
        scratch_shapes=[
            vmem((ROWS, N, C_Z), BF16), vmem((128 * ROWS, C_M), BF16),
            vmem((NDP, 128, C_Z), BF16), vmem((2, NDP, 16, C_Z), BF16), vmem((C_H, C_H, C_Z), F32), vmem((C_H, C_M), F32), vmem((C_H, C_M), F32), vmem((1, C_H), F32), vmem((1, C_H), F32),
            vmem((1, C_Z), F32), vmem((1, C_M), F32), vmem((1, C_M), F32), sems(14),
        ],
        compiler_params=pltpu.CompilerParams(vmem_limit_bytes=56 * 1024 * 1024),
    )(upd, agrad, dw, small)
    return (
        upd[None],
        agrad.reshape(1, 128, ROWS, C_M),
        lw.T,
        lb.reshape(C_H),
        rw.T,
        rb.reshape(C_H),
        dw.reshape(C_H * C_H, C_Z),
        ob.reshape(C_Z),
        gain.reshape(C_M),
        shift.reshape(C_M),
    )


def solution(mesh):
    return jax.shard_map(
        body,
        mesh=mesh,
        in_specs=(
            P("dp", None, "res", None), P("dp", None), P("dp", None), P(), P(), P(), P(), P(), P(), P(), P(),
            P("dp", "res", None, None),
        ),
        out_specs=(
            P("dp", "res", None, None), P("dp", None, "res", None), P(), P(), P(), P(), P(), P(), P(), P(),
        ),
        check_vma=False,
    )
```

```python
import functools

import jax
import jax.numpy as jnp
from jax import lax
from jax.experimental import pallas as pl
from jax.experimental.pallas import tpu as pltpu
from jax.sharding import PartitionSpec as P

C_M = 256
C_H = 32
C_Z = 128
PAIRED = 64
UNP = 64
MOST = 16
CHAINS = 12
EPSILON = 1e-05
NORM_FLOOR = 0.001

ROWS = 8
SLOTS = PAIRED + MOST
NY, NZ, NDP = 4, 8, 8
NRES = NY * NZ
N = ROWS * NRES
ENT = ROWS * SLOTS
HALF = 640
F32, BF16 = jnp.float32, jnp.bfloat16
MESH = pl.DeviceIdType.MESH

NN = (((1,), (0,)), ((), ()))
NT = (((1,), (1,)), ((), ()))
TN = (((0,), (0,)), ((), ()))


def dot(a, b, dims=NN):
    return lax.dot_general(a, b, dims, preferred_element_type=F32)


def iota(shape, dim):
    return lax.broadcasted_iota(jnp.int32, shape, dim)


def onehot(cond):
    return jnp.where(cond, 1.0, 0.0).astype(BF16)


def kernel(
    chain_h, counts_h, x_h, gain_h, shift_h, lw_h, lb_h, rw_h, rb_h, w_h, ob_h, cot_h,
    upd_h, agrad_h, dw_h, small_h,
    upd_ref, agrad_ref, chain_s, counts_s, chain_v, x_ref, gain_ref, shift_ref, lb_ref, rb_ref, w_ref, obias_ref, cot_ref,
    wt_ref, wf, w2_ref,
    xc, normed, inv_ref, lrow, lt, q_ref, tp, tu, g_ref, gm_ref, v_ref, rx, rp, ru,
    ry1, ry2, vsum, rz, ucat, dwf, dws, a_rx, c_rx, d_rx,
    sm, t_rx, e_rx, f_rx, so, ract,
    in_s, out_s, agz_s, agz_r, agy_s, agy_r, agf_s, agf_r, rs1_s, rs1_r, rs2_s, rs2_r, rsz_s, rsz_r,
    p_s, p_r, cz_s, cz_r, ed_s, ed_r,
    td_s, td_r, uy_s, uy_r, uz_s, uz_r, wd_s, wd_r,
):
    me = lax.axis_index("res")
    dp = lax.axis_index("dp")
    z, y = me // NY, me % NY

    def zpeer(k):
        return (z + k) % NZ

    def ypeer(k):
        return (y + k) % NY

    def dpeer(k):
        return (dp + k) % NDP

    def rc(src, dst, ss, rs, **where):
        return pltpu.make_async_remote_copy(
            src_ref=src, dst_ref=dst, send_sem=ss, recv_sem=rs,
            device_id=where, device_id_type=MESH,
        )

    fetches = [
        pltpu.make_async_copy(src, dst, in_s.at[n])
        for n, (src, dst) in enumerate((
            (x_h, x_ref), (chain_h, chain_s), (counts_h, counts_s), (chain_h, chain_v), (gain_h, gain_ref),
            (shift_h, shift_ref), (lw_h, wt_ref.at[0:C_H]), (lb_h, lb_ref), (rw_h, wt_ref.at[C_H:2 * C_H]), (rb_h, rb_ref),
            (w_h, w_ref), (ob_h, obias_ref), (cot_h, cot_ref),
        ))
    ]
    for f in fetches:
        f.start()

    barrier = pltpu.get_barrier_semaphore()

    @pl.loop(1, NRES)
    def _(k):
        pl.semaphore_signal(barrier, inc=1, device_id={"res": (me + k) % NRES}, device_id_type=MESH)

    owner = dp * NY + y

    def opeer(k):
        o = (owner + k) % C_H
        return {"dp": o // NY, "res": z * NY + o % NY}

    @pl.loop(1, NDP)
    def _(k):
        for j in range(NY):
            pl.semaphore_signal(
                barrier, inc=1, device_id={"dp": dpeer(k), "res": z * NY + ypeer(j)}, device_id_type=MESH
            )

    for f in fetches[:10]:
        f.wait()
    rb_col = jnp.transpose(jnp.broadcast_to(rb_ref[...], (8, C_H)))[:, 0:1]

    chain, start, count, base = [], [], [], []
    for r in range(ROWS):
        c = chain_s[0, me * ROWS + r]
        st = jnp.int32(0)
        ct = jnp.int32(0)
        for k in range(CHAINS):
            v = counts_s[0, k]
            st = st + jnp.where(c > k, v, 0)
            ct = ct + jnp.where(c == k, v, 0)
        chain.append(c)
        start.append(st)
        count.append(ct)
        base.append(jnp.minimum(st, UNP - MOST))

    def slot_mask(r, shape, dim):
        s = iota(shape, dim)
        row = s - PAIRED + base[r]
        live = (row >= start[r]) & (row < start[r] + count[r])
        return jnp.where((s < PAIRED) | live, 1.0, 0.0)

    ro, co = iota((128, 128), 0), iota((128, 128), 1)
    perm0 = onehot(co == (ro % 16) * ROWS + ro // 16)
    for b in range(PAIRED // 16):
        part = dot(perm0, x_ref[b * 128:(b + 1) * 128, :])
        for r in range(ROWS):
            xc[r * SLOTS + b * 16:r * SLOTS + b * 16 + 16, :] = part[r * 16:(r + 1) * 16]
    ru_i = iota((128, UNP * ROWS), 0)
    base_rows = jnp.zeros((128, UNP * ROWS), jnp.int32)
    for r in range(ROWS):
        base_rows = jnp.where(ru_i // 16 == r, base[r], base_rows)
    pick = onehot(iota((128, UNP * ROWS), 1) == (base_rows + ru_i % 16) * ROWS + ru_i // 16)
    part = dot(pick, x_ref[PAIRED * ROWS:, :])
    for r in range(ROWS):
        xc[r * SLOTS + PAIRED:(r + 1) * SLOTS, :] = part[r * 16:(r + 1) * 16]

    for r in range(ROWS):
        rows = slice(r * SLOTS, (r + 1) * SLOTS)
        floats = xc[rows, :]
        centred = floats - jnp.mean(floats, axis=-1, keepdims=True)
        inverse = lax.rsqrt(jnp.mean(centred * centred, axis=-1, keepdims=True) + EPSILON)
        scaled = centred * inverse
        nrm = (scaled * gain_ref[...] + shift_ref[...]).astype(BF16)
        xc[rows, :] = scaled
        inv_ref[rows, :] = inverse
        normed[rows, :] = nrm
        left = (dot(nrm, wt_ref[0:C_H, :], NT) + lb_ref[...]) * slot_mask(r, (SLOTS, C_H), 0)
        lrow[rows, :] = left.astype(BF16)
        right = (dot(wt_ref[C_H:, :], nrm, NT) + rb_col) * slot_mask(r, (C_H, SLOTS), 1)
        q_ref[r * C_H:(r + 1) * C_H, 0:SLOTS] = right.astype(BF16)
    re, ce = iota((256, 256), 0), iota((256, 256), 1)
    permq = onehot(ce == (re % 8) * 32 + ((re // 8) % 2) * 16 + re // 16)
    mixed = dot(permq, q_ref[:, 0:SLOTS])
    for p in range(8):
        rx[me, :, p * 128:(p + 1) * 128] = jnp.concatenate(
            [mixed[(2 * p + a) * 16:(2 * p + a + 1) * 16, 0:PAIRED] for a in range(2)], axis=1
        ).astype(BF16)
    for q in range(2):
        rx[me, :, 1024 + q * 128:1024 + (q + 1) * 128] = jnp.concatenate(
            [mixed[(8 * q + a) * 16:(8 * q + a + 1) * 16, PAIRED:SLOTS] for a in range(8)], axis=1
        ).astype(BF16)

    pl.semaphore_wait(barrier, NRES - 1 + NY * (NDP - 1))

    def agz(k):
        return rc(rx.at[me], rx.at[me], agz_s.at[k], agz_r.at[k], res=zpeer(k) * NY + y)

    def agy(d, kz):
        slot = ((z - kz + NZ) % NZ) * NY + y
        return rc(rx.at[slot], rx.at[slot], agy_s.at[d, kz], agy_r.at[d, kz], res=z * NY + ypeer(1 + 2 * d))

    def agf(d, kz):
        slot = ((z - kz + NZ) % NZ) * NY + ypeer(3 - 2 * d)
        part = rx.at[slot, :, d * HALF:(d + 1) * HALF]
        return rc(part, part, agf_s.at[d, kz], agf_r.at[d, kz], res=z * NY + ypeer(1 + 2 * d))

    def spread(*turns):
        for kz in turns:
            if kz:
                agz(kz).wait_recv()
            for d in range(2):
                agy(d, kz).start()

    def forward(*turns):
        for kz in turns:
            for d in range(2):
                agy(d, kz).wait_recv()
                agf(d, kz).start()

    spread(0)
    for k in (1, 7, 2, 6, 3, 5, 4):
        agz(k).start()

    for f in fetches[10:]:
        f.wait()
    wf[...] = w_ref[...].astype(F32)
    for e in range(C_H):
        w2_ref[:, e * 128:(e + 1) * 128] = wf[pl.ds(e, C_H, stride=C_H), :].astype(BF16)

    lt[...] = jnp.transpose(lrow[...].astype(F32)).astype(BF16)

    def t_step(g):
        h, p = g // 8, g % 8
        t = dot(lrow[...], w2_ref[:, pl.ds(pl.multiple_of(g * 256, 256), 256)]).astype(BF16)
        rowp = pl.multiple_of((p * 2 + h) * 128, 128)
        rowu = pl.multiple_of(((p // 4) * 2 + h) * 128 + (p % 4) * 32, 32)
        for i in range(ROWS):
            for a in range(2):
                tp[pl.ds(rowp + a * 64, 64), i * 128:(i + 1) * 128] = t[i * SLOTS:i * SLOTS + PAIRED, a * 128:(a + 1) * 128]
                tu[pl.ds(rowu + a * 16, 16), i * 128:(i + 1) * 128] = t[i * SLOTS + PAIRED:(i + 1) * SLOTS, a * 128:(a + 1) * 128]

    pl.loop(0, 12, unroll=2)(t_step)
    spread(1, 7)
    pl.loop(12, 16, unroll=2)(t_step)
    chain_col = jnp.transpose(jnp.broadcast_to(chain_v[...].astype(F32), (128, N)))
    obg = jnp.zeros((8, C_Z), F32)
    inv_own = []
    for i in range(ROWS):
        same = chain_col == chain[i].astype(F32)
        cntf = jnp.full((8, C_Z), count[i].astype(F32))
        inv_own.append((1.0 / (PAIRED + cntf + NORM_FLOOR))[0:1, :])
        raw = cot_ref[i].astype(F32)
        obg = obg + jnp.sum(raw.reshape(N // 8, 8, C_Z), axis=0)
        g = (raw * jnp.where(same, inv_own[i], 1.0 / (PAIRED + NORM_FLOOR))).astype(BF16)
        g_ref[:, i * 128:(i + 1) * 128] = g
        gm_ref[:, i * 128:(i + 1) * 128] = jnp.where(same, g.astype(F32), 0.0).astype(BF16)

    def put_v(v, lane):
        both = jnp.concatenate(
            [v[:, 0:128].reshape(NRES, ROWS, 128), v[:, 128:256].reshape(NRES, ROWS, 128)], axis=1
        )
        v_ref[:, :, pl.ds(lane, 128)] = both.astype(BF16)

    def v_step(p):
        put_v(dot(g_ref[...], tp[pl.ds(pl.multiple_of(p * 256, 256), 256), :], NT), pl.multiple_of(p * 128, 128))

    def rs1(d, kz):
        dst = zpeer(kz) * NY + ypeer(2)
        src = v_ref.at[dst, :, d * HALF:(d + 1) * HALF]
        return rc(src, ry1.at[d, kz], rs1_s.at[d, kz], rs1_r.at[d, kz], res=z * NY + ypeer(3 - 2 * d))

    def rs2(d, kz):
        dst = zpeer(kz) * NY + ypeer(3 - 2 * d)
        return rc(v_ref.at[dst], ry2.at[d, kz], rs2_s.at[d, kz], rs2_r.at[d, kz], res=z * NY + ypeer(3 - 2 * d))

    def rsz(k):
        return rc(vsum.at[k], rz.at[k], rsz_s.at[k], rsz_r.at[k], res=zpeer(k) * NY + y)

    def second(*turns):
        for kz in turns:
            for d in range(2):
                slab = zpeer(kz) * NY + ypeer(3 - 2 * d)
                lanes = slice(d * HALF, (d + 1) * HALF)
                rs1(d, kz).wait_recv()
                v_ref[slab, :, lanes] = (v_ref[slab, :, lanes].astype(F32) + ry1[d, kz].astype(F32)).astype(BF16)
                rs2(d, kz).start()

    def third(*turns):
        for kz in turns:
            total = v_ref[zpeer(kz) * NY + y].astype(F32)
            for d in range(2):
                rs2(d, kz).wait_recv()
                total = total + ry2[d, kz].astype(F32)
            if kz:
                vsum[kz] = total.astype(BF16)
                rsz(kz).start()
        return total

    def first(*turns):
        for kz in turns:
            for d in range(2):
                rs1(d, kz).start()

    pl.loop(0, 4, unroll=2)(v_step)
    spread(2, 6)
    forward(0)
    pl.loop(4, 8, unroll=2)(v_step)
    for q in range(2):
        put_v(dot(gm_ref[...], tu[q * 256:(q + 1) * 256, :], NT), 1024 + q * 128)
    first(4, 3, 5, 2)
    spread(3, 5)
    forward(1, 7)
    first(6, 1, 7, 0)
    spread(4)
    forward(2, 6)
    second(4)
    forward(3, 5)
    second(3, 5)
    forward(4)
    second(2, 6)

    for kz in range(NZ):
        for d in range(2):
            agf(d, kz).wait_recv()

    @pl.loop(0, NRES // 2)
    def _(d):
        a, b = rx[2 * d].astype(F32), rx[2 * d + 1].astype(F32)
        rows = pl.ds(pl.multiple_of(d * 16, 16), 16)
        for h in range(2):
            both = jnp.concatenate([a[h * 8:h * 8 + 8], b[h * 8:h * 8 + 8]], axis=0).astype(BF16)
            for p in range(8):
                rp[rows, p * 256 + h * 128:p * 256 + (h + 1) * 128] = both[:, p * 128:(p + 1) * 128]
            for q in range(2):
                ru[rows, q * 256 + h * 128:q * 256 + (h + 1) * 128] = both[:, 1024 + q * 128:1024 + (q + 1) * 128]

    def u_step(p):
        u = dot(rp[:, pl.ds(pl.multiple_of(p * 256, 256), 256)], g_ref[...], TN).astype(BF16)
        for h in range(2):
            for a in range(2):
                lane = pl.multiple_of((h * 16 + 2 * p + a) * 128, 128)
                for i in range(ROWS):
                    ucat[i * SLOTS:i * SLOTS + PAIRED, pl.ds(lane, 128)] = u[(h * 2 + a) * 64:(h * 2 + a + 1) * 64, i * 128:(i + 1) * 128]

    def u_side(q):
        u = dot(ru[:, q * 256:(q + 1) * 256], gm_ref[...], TN).astype(BF16)
        for h in range(2):
            for a in range(8):
                lane = (h * 16 + q * 8 + a) * 128
                for i in range(ROWS):
                    ucat[i * SLOTS + PAIRED:(i + 1) * SLOTS, lane:lane + 128] = u[(h * 8 + a) * 16:(h * 8 + a + 1) * 16, i * 128:(i + 1) * 128]

    def pd(e):
        k = (e - owner + C_H) % C_H
        return rc(dws.at[e], a_rx.at[k - 1], p_s.at[0], p_r.at[0], **opeer(k))

    def dw_step(g):
        dw = dot(lt[...], ucat[:, g * 256:(g + 1) * 256])
        for a in range(2):
            part = dw[:, a * 128:(a + 1) * 128]
            dwf[2 * g + a] = part
            dws[2 * g + a] = part.astype(BF16)

    def dw_send(first):
        @pl.loop(first, first + 8)
        def _(e):
            @pl.when(e != owner)
            def _():
                pd(e).start()

    pl.loop(0, 4, unroll=2)(u_step)
    u_side(0)
    second(1, 7, 0)
    for g in (0, 1, 2, 3, 8, 9, 10, 11):
        dw_step(g)
    dw_send(0)
    dw_send(16)
    third(4, 3, 5)
    pl.loop(4, 8, unroll=2)(u_step)
    u_side(1)
    third(2, 6)
    for g in (4, 5, 6, 7, 12, 13, 14, 15):
        dw_step(g)
    dw_send(8)
    dw_send(24)
    own = third(1, 7, 0)

    def left_step(k, acc):
        cols = pl.ds(pl.multiple_of(k * 512, 512), 512)
        return acc + dot(ucat[:, cols], w2_ref[:, cols], NT)

    lgrad = lax.fori_loop(0, 8, left_step, jnp.zeros((ENT, C_H), F32), unroll=2)

    def td(k):
        return rc(sm.at[dpeer(k)], t_rx.at[k - 1], td_s.at[0], td_r.at[0], dp=dpeer(k))

    def uy(k):
        return rc(e_rx.at[y], e_rx.at[y], uy_s.at[0], uy_r.at[0], res=z * NY + ypeer(k))

    def uz(k):
        return rc(f_rx.at[z], f_rx.at[z], uz_s.at[0], uz_r.at[0], res=zpeer(k) * NY + y)

    def wd(k):
        return rc(so.at[dp], so.at[dp], wd_s.at[0], wd_r.at[0], dp=dpeer(k))

    rows8 = iota((8, C_Z), 0)

    def small_put(c, gw, tail_rows):
        tail = jnp.zeros((8, C_Z), F32)
        for k, row in enumerate(tail_rows):
            tail = jnp.where(rows8 == k, row, tail)
        main = jnp.concatenate([gw[:, 0:128], gw[:, 128:256]], axis=0).reshape(8, 8, C_Z)
        tails = jnp.broadcast_to(tail.reshape(8, 1, C_Z), (8, 8, C_Z))
        sm[:, c * 16:(c + 1) * 16, :] = jnp.concatenate([main, tails], axis=1).astype(BF16)

    def drain(ref, send, recv, count):
        some = ref.at[0:count]
        rc(some, some, send.at[0], recv.at[0], dp=dpeer(1)).wait()

    def total(ref):
        return jnp.sum(ref[...].astype(F32), axis=0)

    gw_l = jnp.zeros((C_H, C_M), F32)
    gb_l = jnp.zeros((1, C_H), F32)
    for r in range(ROWS):
        rows = slice(r * SLOTS, (r + 1) * SLOTS)
        lact = (lgrad[rows] * slot_mask(r, (SLOTS, C_H), 0)).astype(BF16)
        gw_l = gw_l + dot(lact, normed[rows, :], TN)
        gb_l = gb_l + jnp.sum(lact.astype(F32), axis=0, keepdims=True)
        lrow[rows, :] = lact
    small_put(0, gw_l, (
        jnp.sum(obg, axis=0, keepdims=True),
        jnp.concatenate([gb_l, jnp.zeros((1, 96), F32)], axis=1),
    ))

    for kz in (4, 3, 5, 2, 6, 1, 7):
        rsz(kz).wait_recv()
        own = own + rz[kz].astype(F32)
    tiles = []
    for e in range(16):
        tiles.append(jnp.concatenate([own[:, e * 64:(e + 1) * 64], own[:, 1024 + e * 16:1024 + (e + 1) * 16]], axis=1))
    back = dot(permq, jnp.concatenate(tiles, axis=0).astype(BF16), TN)

    gw_r = jnp.zeros((C_H, C_M), F32)
    gb_r = jnp.zeros((C_H, 1), F32)
    gain_g = jnp.zeros((1, C_M), F32)
    shift_g = jnp.zeros((1, C_M), F32)
    for r in range(ROWS):
        rows = slice(r * SLOTS, (r + 1) * SLOTS)
        ract_t = (back[r * C_H:(r + 1) * C_H, :] * slot_mask(r, (C_H, SLOTS), 1)).astype(BF16)
        gw_r = gw_r + dot(ract_t, normed[rows, :])
        gb_r = gb_r + jnp.sum(ract_t.astype(F32), axis=1, keepdims=True)
        gn = dot(lrow[rows, :], wt_ref[0:C_H, :]) + dot(ract_t, wt_ref[C_H:, :], TN)
        scaled = xc[rows, :]
        gain_g = gain_g + jnp.sum(gn * scaled, axis=0, keepdims=True)
        shift_g = shift_g + jnp.sum(gn, axis=0, keepdims=True)
        gg = gn * gain_ref[...]
        mean_g = jnp.mean(gg, axis=-1, keepdims=True)
        mean_p = jnp.mean(gg * scaled, axis=-1, keepdims=True)
        ract[rows, :] = (inv_ref[rows, :] * (gg - mean_g - scaled * mean_p)).astype(BF16)
    gbr_row = jnp.transpose(jnp.broadcast_to(gb_r, (C_H, 128)))[0:1, :]
    small_put(1, gw_r, (
        gain_g[:, 0:128], gain_g[:, 128:256], shift_g[:, 0:128], shift_g[:, 128:256],
        jnp.concatenate([gbr_row, jnp.zeros((1, 96), F32)], axis=1),
    ))

    for k in range(1, NDP):
        td(k).start()

    drain(a_rx, p_s, p_r, C_H - 1)

    def add(k, t):
        return t + a_rx[k].astype(F32)

    c_rx[z] = lax.fori_loop(0, C_H - 1, add, dwf[owner], unroll=True).astype(BF16)

    def cz(k):
        return rc(c_rx.at[z], c_rx.at[z], cz_s.at[0], cz_r.at[0], res=zpeer(k) * NY + y)

    for k in range(1, NZ):
        cz(k).start()

    drain(t_rx, td_s, td_r, NDP - 1)
    e_rx[y] = (sm[dp].astype(F32) + total(t_rx)).astype(BF16)
    for k in range(1, NY):
        uy(k).start()

    drain(c_rx, cz_s, cz_r, NZ - 1)
    d_rx[owner] = (total(c_rx) * (1.0 / N)).astype(BF16)

    def ed(k):
        return rc(d_rx.at[owner], d_rx.at[owner], ed_s.at[0], ed_r.at[0], **opeer(k))

    @pl.loop(1, C_H)
    def _(k):
        ed(k).start()

    drain(e_rx, uy_s, uy_r, NY - 1)
    f_rx[z] = total(e_rx).astype(BF16)
    for k in range(1, NZ):
        uz(k).start()

    @pl.loop(0, 4)
    def _(g):
        cols = pl.ds(pl.multiple_of(g * 256, 256), 256)
        main = dot(rp[...], tp[:, cols])
        side = dot(ru[...], tu[:, cols])
        for a in range(2):
            i = 2 * g + a
            ch = jnp.int32(0)
            iv = jnp.zeros((1, C_Z), F32)
            for r in range(ROWS):
                ch = jnp.where(i == r, chain[r], ch)
                iv = jnp.where(i == r, inv_own[r], iv)
            same = chain_col == ch.astype(F32)
            m, s = main[:, a * 128:(a + 1) * 128], side[:, a * 128:(a + 1) * 128]
            out = jnp.where(same, (m + s) * iv, m * (1.0 / (PAIRED + NORM_FLOOR))) + obias_ref[...]
            upd_ref[i] = out.astype(BF16)

    for b in range(PAIRED // 16):
        src = jnp.concatenate([ract[r * SLOTS + b * 16:r * SLOTS + b * 16 + 16, :] for r in range(ROWS)], axis=0)
        agrad_ref[b * 128:(b + 1) * 128, :] = dot(perm0, src, TN).astype(BF16)
    src = jnp.concatenate([ract[r * SLOTS + PAIRED:(r + 1) * SLOTS, :] for r in range(ROWS)], axis=0)
    agrad_ref[PAIRED * ROWS:, :] = dot(pick, src, TN).astype(BF16)

    upd_out = pltpu.make_async_copy(upd_ref, upd_h, out_s.at[0])
    upd_out.start()

    agrad_out = pltpu.make_async_copy(agrad_ref, agrad_h, out_s.at[1])
    agrad_out.start()

    drain(f_rx, uz_s, uz_r, NZ - 1)
    so[dp] = (total(f_rx) * (1.0 / N)).astype(BF16)
    for k in range(1, NDP):
        wd(k).start()

    for kz in range(NZ):
        for d in range(2):
            for c in (agy, agf, rs1, rs2):
                c(d, kz).wait_send()
    for k in range(1, NZ):
        agz(k).wait_send()
        rsz(k).wait_send()

    drain(d_rx, ed_s, ed_r, C_H - 1)
    dw_out = pltpu.make_async_copy(d_rx, dw_h, out_s.at[2])
    dw_out.start()
    drain(so, wd_s, wd_r, NDP - 1)
    small_out = pltpu.make_async_copy(so, small_h, out_s.at[3])
    small_out.start()
    for c in (upd_out, agrad_out, dw_out, small_out):
        c.wait()


def finish(
    upd_i, agrad_i, dw_i, small_i,
    upd_h, agrad_h, lw_h, lb_h, rw_h, rb_h, dw_h, ob_h, gain_h, shift_h,
    upd_v, agrad_v, dw_v, small_v, dw_f, lw_f, rw_f, lb_f, rb_f, ob_f, gain_f, shift_f, sem,
):
    copies = []

    def send(src, dst):
        copies.append(pltpu.make_async_copy(src, dst, sem.at[len(copies)]))
        copies[-1].start()

    fetches = [
        pltpu.make_async_copy(src, dst, sem.at[10 + n])
        for n, (src, dst) in enumerate(((dw_i, dw_v), (small_i, small_v), (upd_i, upd_v), (agrad_i, agrad_v)))
    ]
    for f in fetches:
        f.start()
    fetches[0].wait()
    for d in range(NDP):
        for a in range(4):
            dw_f[:, d * 4 + a, :] = dw_v[d * 4 + a].astype(F32)
    send(dw_f, dw_h)
    fetches[2].wait()
    send(upd_v, upd_h)
    fetches[3].wait()
    send(agrad_v, agrad_h)
    fetches[1].wait()

    def tail(c, k):
        return small_v[k].astype(F32)[c * 16 + 8:c * 16 + 9]

    for c, (buf, out) in enumerate(((lw_f, lw_h), (rw_f, rw_h))):
        for half in range(2):
            rows = [small_v[half * 4 + d].astype(F32)[c * 16:c * 16 + 8] for d in range(4)]
            buf[:, half * 128:(half + 1) * 128] = jnp.concatenate(rows, axis=0)
        send(buf, out)
    ob_f[...] = tail(0, 0)
    lb_f[...] = tail(0, 1)[:, 0:C_H]
    rb_f[...] = tail(1, 4)[:, 0:C_H]
    gain_f[...] = jnp.concatenate([tail(1, 0), tail(1, 1)], axis=1)
    shift_f[...] = jnp.concatenate([tail(1, 2), tail(1, 3)], axis=1)
    for buf, out in ((ob_f, ob_h), (lb_f, lb_h), (rb_f, rb_h), (gain_f, gain_h), (shift_f, shift_h)):
        send(buf, out)
    for c in copies:
        c.wait()


def body(
    alignment, chain_ids, row_counts, norm_gain, norm_shift, left_weight, left_bias,
    right_weight, right_bias, out_weight, out_bias, pair_cotangent,
):
    sems = lambda *shape: pltpu.SemaphoreType.DMA(shape)
    vmem = pltpu.VMEM
    scratch = [
        vmem((ROWS, N, C_Z), BF16), vmem((128 * ROWS, C_M), BF16), pltpu.SMEM((1, N), jnp.int32), pltpu.SMEM((1, CHAINS), jnp.int32), vmem((1, N), jnp.int32),
        vmem((128 * ROWS, C_M), BF16), vmem((1, C_M), F32), vmem((1, C_M), F32), vmem((1, C_H), F32),
        vmem((1, C_H), F32), vmem((C_H * C_H, C_Z), BF16), vmem((1, C_Z), F32), vmem((ROWS, N, C_Z), BF16),
        vmem((2 * C_H, C_M), BF16), vmem((C_H * C_H, C_Z), F32), vmem((C_H, C_H * C_Z), BF16),
        vmem((ENT, C_M), F32), vmem((ENT, C_M), BF16), vmem((ENT, 1), F32),
        vmem((ENT, C_H), BF16), vmem((C_H, ENT), BF16), vmem((256, 128), BF16),
        vmem((2048, 1024), BF16), vmem((512, 1024), BF16), vmem((N, 1024), BF16), vmem((N, 1024), BF16),
        vmem((NRES, 16, 1280), BF16), vmem((NRES, 16, 1280), BF16), vmem((N, 2048), BF16), vmem((N, 512), BF16),
        vmem((2, NZ, 16, HALF), BF16), vmem((2, NZ, 16, 1280), BF16), vmem((NZ, 16, 1280), BF16), vmem((NZ, 16, 1280), BF16),
        vmem((ENT, 4096), BF16),
        vmem((C_H, C_H, C_Z), F32), vmem((C_H, C_H, C_Z), BF16), vmem((C_H - 1, C_H, C_Z), BF16),
        vmem((NZ, C_H, C_Z), BF16), vmem((C_H, C_H, C_Z), BF16),
        vmem((NDP, 32, C_Z), BF16), vmem((NDP - 1, 32, C_Z), BF16), vmem((NY, 32, C_Z), BF16), vmem((NZ, 32, C_Z), BF16), vmem((NDP, 32, C_Z), BF16),
        vmem((ENT, C_M), BF16),
        sems(13), sems(4), sems(NZ), sems(NZ), sems(2, NZ), sems(2, NZ), sems(2, NZ), sems(2, NZ),
        sems(2, NZ), sems(2, NZ), sems(2, NZ), sems(2, NZ), sems(NZ), sems(NZ),
        sems(1), sems(1), sems(1), sems(1), sems(1), sems(1),
        sems(1), sems(1), sems(1), sems(1), sems(1), sems(1), sems(1), sems(1),
    ]
    hbm = pl.BlockSpec(memory_space=pltpu.HBM)
    upd, agrad, dw, small = pl.pallas_call(
        kernel,
        out_shape=(
            jax.ShapeDtypeStruct((ROWS, N, C_Z), BF16),
            jax.ShapeDtypeStruct((128 * ROWS, C_M), BF16),
            jax.ShapeDtypeStruct((C_H, C_H, C_Z), BF16),
            jax.ShapeDtypeStruct((NDP, 32, C_Z), BF16),
        ),
        in_specs=[hbm] * 12,
        out_specs=(hbm,) * 4,
        scratch_shapes=scratch,
        compiler_params=pltpu.CompilerParams(
            collective_id=0, has_side_effects=True, vmem_limit_bytes=56 * 1024 * 1024
        ),
    )(
        chain_ids, row_counts, alignment.reshape(128 * ROWS, C_M),
        norm_gain.reshape(1, C_M), norm_shift.reshape(1, C_M), left_weight.T, left_bias.reshape(1, C_H),
        right_weight.T, right_bias.reshape(1, C_H), out_weight, out_bias.reshape(1, C_Z), pair_cotangent[0],
    )
    outs = (
        ((ROWS, N, C_Z), BF16), ((128 * ROWS, C_M), BF16), ((C_H, C_M), F32), ((1, C_H), F32), ((C_H, C_M), F32),
        ((1, C_H), F32), ((C_H, C_H, C_Z), F32), ((1, C_Z), F32), ((1, C_M), F32), ((1, C_M), F32),
    )
    upd, agrad, lw, lb, rw, rb, dw, ob, gain, shift = pl.pallas_call(
        finish,
        out_shape=tuple(jax.ShapeDtypeStruct(*o) for o in outs),
        in_specs=[hbm] * 4,
        out_specs=(hbm,) * 10,
        scratch_shapes=[
            vmem((ROWS, N, C_Z), BF16), vmem((128 * ROWS, C_M), BF16),
            vmem((C_H, C_H, C_Z), BF16), vmem((NDP, 32, C_Z), BF16), vmem((C_H, C_H, C_Z), F32), vmem((C_H, C_M), F32), vmem((C_H, C_M), F32), vmem((1, C_H), F32), vmem((1, C_H), F32),
            vmem((1, C_Z), F32), vmem((1, C_M), F32), vmem((1, C_M), F32), sems(14),
        ],
        compiler_params=pltpu.CompilerParams(vmem_limit_bytes=56 * 1024 * 1024),
    )(upd, agrad, dw, small)
    return (
        upd[None],
        agrad.reshape(1, 128, ROWS, C_M),
        lw.T,
        lb.reshape(C_H),
        rw.T,
        rb.reshape(C_H),
        dw.reshape(C_H * C_H, C_Z),
        ob.reshape(C_Z),
        gain.reshape(C_M),
        shift.reshape(C_M),
    )


def solution(mesh):
    return jax.shard_map(
        body,
        mesh=mesh,
        in_specs=(
            P("dp", None, "res", None), P("dp", None), P("dp", None), P(), P(), P(), P(), P(), P(), P(), P(),
            P("dp", "res", None, None),
        ),
        out_specs=(
            P("dp", "res", None, None), P("dp", None, "res", None), P(), P(), P(), P(), P(), P(), P(), P(),
        ),
        check_vma=False,
    )
```

```python
import functools

import jax
import jax.numpy as jnp
from jax import lax
from jax.experimental import pallas as pl
from jax.experimental.pallas import tpu as pltpu
from jax.sharding import PartitionSpec as P

C_M = 256
C_H = 32
C_Z = 128
PAIRED = 64
UNP = 64
MOST = 16
CHAINS = 12
EPSILON = 1e-05
NORM_FLOOR = 0.001

ROWS = 8
SLOTS = PAIRED + MOST
NY, NZ, NDP = 4, 8, 8
NRES = NY * NZ
N = ROWS * NRES
ENT = ROWS * SLOTS
MAIN = 1024
HALF = MAIN // 2
F32, BF16 = jnp.float32, jnp.bfloat16
MESH = pl.DeviceIdType.MESH

NN = (((1,), (0,)), ((), ()))
NT = (((1,), (1,)), ((), ()))
TN = (((0,), (0,)), ((), ()))


def dot(a, b, dims=NN):
    return lax.dot_general(a, b, dims, preferred_element_type=F32)


def iota(shape, dim):
    return lax.broadcasted_iota(jnp.int32, shape, dim)


def onehot(cond):
    return jnp.where(cond, 1.0, 0.0).astype(BF16)


def kernel(
    chain_h, counts_h, x_h, gain_h, shift_h, lw_h, lb_h, rw_h, rb_h, w_h, ob_h, cot_h,
    upd_h, agrad_h, dw_h, small_h,
    upd_ref, agrad_ref, chain_s, counts_s, chain_v, x_ref, gain_ref, shift_ref, lb_ref, rb_ref, w_ref, obias_ref, cot_ref,
    wt_ref, wf, w2_ref,
    xc, normed, inv_ref, lrow, lt, q_ref, tp, tu, g_ref, gm_ref, v_ref, rx, rp, ru,
    ry1, ry2, vsum, rz, rbz, sbf, sb, rby, ucat, dwf, dws, a_rx, c_rx, d_rx,
    sm, t_rx, e_rx, f_rx, so, ract,
    in_s, out_s, bgy_s, bgy_r, bgz_s, bgz_r, bsz_s, bsz_r, bsy_s, bsy_r, agz_s, agz_r, agy_s, agy_r, agf_s, agf_r, rs1_s, rs1_r, rs2_s, rs2_r, rsz_s, rsz_r,
    p_s, p_r, cz_s, cz_r, ed_s, ed_r,
    td_s, td_r, uy_s, uy_r, uz_s, uz_r, wd_s, wd_r,
):
    me = lax.axis_index("res")
    dp = lax.axis_index("dp")
    z, y = me // NY, me % NY

    def zpeer(k):
        return (z + k) % NZ

    def ypeer(k):
        return (y + k) % NY

    def dpeer(k):
        return (dp + k) % NDP

    def rc(src, dst, ss, rs, **where):
        return pltpu.make_async_remote_copy(
            src_ref=src, dst_ref=dst, send_sem=ss, recv_sem=rs,
            device_id=where, device_id_type=MESH,
        )

    fetches = [
        pltpu.make_async_copy(src, dst, in_s.at[n])
        for n, (src, dst) in enumerate((
            (x_h, x_ref), (chain_h, chain_s), (counts_h, counts_s), (chain_h, chain_v), (gain_h, gain_ref),
            (shift_h, shift_ref), (lw_h, wt_ref.at[0:C_H]), (lb_h, lb_ref), (rw_h, wt_ref.at[C_H:2 * C_H]), (rb_h, rb_ref),
            (w_h, w_ref), (ob_h, obias_ref), (cot_h, cot_ref),
        ))
    ]
    for f in fetches:
        f.start()

    barrier = pltpu.get_barrier_semaphore()

    @pl.loop(1, NRES)
    def _(k):
        pl.semaphore_signal(barrier, inc=1, device_id={"res": (me + k) % NRES}, device_id_type=MESH)

    owner = dp * NY + y

    def opeer(k):
        o = (owner + k) % C_H
        return {"dp": o // NY, "res": z * NY + o % NY}

    @pl.loop(1, NDP)
    def _(k):
        for j in range(NY):
            pl.semaphore_signal(
                barrier, inc=1, device_id={"dp": dpeer(k), "res": z * NY + ypeer(j)}, device_id_type=MESH
            )

    for f in fetches[:10]:
        f.wait()
    rb_col = jnp.transpose(jnp.broadcast_to(rb_ref[...], (8, C_H)))[:, 0:1]

    chain, start, count, base = [], [], [], []
    for r in range(ROWS):
        c = chain_s[0, me * ROWS + r]
        st = jnp.int32(0)
        ct = jnp.int32(0)
        for k in range(CHAINS):
            v = counts_s[0, k]
            st = st + jnp.where(c > k, v, 0)
            ct = ct + jnp.where(c == k, v, 0)
        chain.append(c)
        start.append(st)
        count.append(ct)
        base.append(jnp.minimum(st, UNP - MOST))

    def slot_mask(r, shape, dim):
        s = iota(shape, dim)
        row = s - PAIRED + base[r]
        live = (row >= start[r]) & (row < start[r] + count[r])
        return jnp.where((s < PAIRED) | live, 1.0, 0.0)

    ro, co = iota((128, 128), 0), iota((128, 128), 1)
    perm0 = onehot(co == (ro % 16) * ROWS + ro // 16)
    for b in range(PAIRED // 16):
        part = dot(perm0, x_ref[b * 128:(b + 1) * 128, :])
        for r in range(ROWS):
            xc[r * SLOTS + b * 16:r * SLOTS + b * 16 + 16, :] = part[r * 16:(r + 1) * 16]
    ru_i = iota((128, UNP * ROWS), 0)
    base_rows = jnp.zeros((128, UNP * ROWS), jnp.int32)
    for r in range(ROWS):
        base_rows = jnp.where(ru_i // 16 == r, base[r], base_rows)
    pick = onehot(iota((128, UNP * ROWS), 1) == (base_rows + ru_i % 16) * ROWS + ru_i // 16)
    part = dot(pick, x_ref[PAIRED * ROWS:, :])
    for r in range(ROWS):
        xc[r * SLOTS + PAIRED:(r + 1) * SLOTS, :] = part[r * 16:(r + 1) * 16]

    for r in range(ROWS):
        rows = slice(r * SLOTS, (r + 1) * SLOTS)
        floats = xc[rows, :]
        centred = floats - jnp.mean(floats, axis=-1, keepdims=True)
        inverse = lax.rsqrt(jnp.mean(centred * centred, axis=-1, keepdims=True) + EPSILON)
        scaled = centred * inverse
        nrm = (scaled * gain_ref[...] + shift_ref[...]).astype(BF16)
        xc[rows, :] = scaled
        inv_ref[rows, :] = inverse
        normed[rows, :] = nrm
        left = (dot(nrm, wt_ref[0:C_H, :], NT) + lb_ref[...]) * slot_mask(r, (SLOTS, C_H), 0)
        lrow[rows, :] = left.astype(BF16)
        right = (dot(wt_ref[C_H:, :], nrm, NT) + rb_col) * slot_mask(r, (C_H, SLOTS), 1)
        q_ref[r * C_H:(r + 1) * C_H, 0:SLOTS] = right.astype(BF16)
    re, ce = iota((256, 256), 0), iota((256, 256), 1)
    permq = onehot(ce == (re % 8) * 32 + ((re // 8) % 2) * 16 + re // 16)
    mixed = dot(permq, q_ref[:, 0:SLOTS])
    for p in range(8):
        rx[me, :, p * 128:(p + 1) * 128] = jnp.concatenate(
            [mixed[(2 * p + a) * 16:(2 * p + a + 1) * 16, 0:PAIRED] for a in range(2)], axis=1
        ).astype(BF16)
    for q in range(2):
        rx[me, :, 1024 + q * 128:1024 + (q + 1) * 128] = jnp.concatenate(
            [mixed[(8 * q + a) * 16:(8 * q + a + 1) * 16, PAIRED:SLOTS] for a in range(8)], axis=1
        ).astype(BF16)

    pl.semaphore_wait(barrier, NRES - 1 + NY * (NDP - 1))

    def agz(k):
        part = rx.at[me, :, 0:MAIN]
        return rc(part, part, agz_s.at[0], agz_r.at[k], res=zpeer(k) * NY + y)

    def agy(d, kz):
        slot = ((z - kz + NZ) % NZ) * NY + y
        part = rx.at[slot, :, 0:MAIN]
        return rc(part, part, agy_s.at[0], agy_r.at[d, kz], res=z * NY + ypeer(1 + 2 * d))

    def agf(d, kz):
        slot = ((z - kz + NZ) % NZ) * NY + ypeer(3 - 2 * d)
        part = rx.at[slot, :, d * HALF:(d + 1) * HALF]
        return rc(part, part, agf_s.at[0], agf_r.at[0], res=z * NY + ypeer(1 + 2 * d))

    def bgy(k):
        part = rx.at[me, :, MAIN:]
        return rc(part, part, bgy_s.at[0], bgy_r.at[0], res=z * NY + ypeer(k))

    def bgz(k):
        part = rx.at[pl.ds(z * NY, NY), :, MAIN:]
        return rc(part, part, bgz_s.at[0], bgz_r.at[0], res=zpeer(k) * NY + y)

    def drain(ref, send, recv, count):
        some = ref.at[0:count]
        rc(some, some, send.at[0], recv.at[0], dp=dpeer(1)).wait()

    def spread(*turns):
        for kz in turns:
            if kz:
                agz(kz).wait_recv()
            for d in range(2):
                agy(d, kz).start()

    def forward(*turns):
        for kz in turns:
            for d in range(2):
                agy(d, kz).wait_recv()
                agf(d, kz).start()

    for k in range(1, NY):
        bgy(k).start()
    for k in (1, 7, 2, 6, 3, 5, 4):
        agz(k).start()
    spread(0)

    for f in fetches[10:]:
        f.wait()
    wf[...] = w_ref[...].astype(F32)
    for e in range(C_H):
        w2_ref[:, e * 128:(e + 1) * 128] = wf[pl.ds(e, C_H, stride=C_H), :].astype(BF16)

    lt[...] = jnp.transpose(lrow[...].astype(F32)).astype(BF16)

    def t_step(g):
        h, p = g // 8, g % 8
        t = dot(lrow[...], w2_ref[:, pl.ds(pl.multiple_of(g * 256, 256), 256)]).astype(BF16)
        rowp = pl.multiple_of((p * 2 + h) * 128, 128)
        rowu = pl.multiple_of(((p // 4) * 2 + h) * 128 + (p % 4) * 32, 32)
        for i in range(ROWS):
            for a in range(2):
                tp[pl.ds(rowp + a * 64, 64), i * 128:(i + 1) * 128] = t[i * SLOTS:i * SLOTS + PAIRED, a * 128:(a + 1) * 128]
                tu[pl.ds(rowu + a * 16, 16), i * 128:(i + 1) * 128] = t[i * SLOTS + PAIRED:(i + 1) * SLOTS, a * 128:(a + 1) * 128]

    pl.loop(0, 12, unroll=2)(t_step)
    spread(1, 7)
    pl.loop(12, 16, unroll=2)(t_step)
    spread(2, 6)
    drain(rx.at[:, :, MAIN:], bgy_s, bgy_r, NY - 1)
    for k in range(1, NZ):
        bgz(k).start()
    forward(0)
    chain_col = jnp.transpose(jnp.broadcast_to(chain_v[...].astype(F32), (128, N)))
    obg = jnp.zeros((8, C_Z), F32)
    inv_own = []
    for i in range(ROWS):
        same = chain_col == chain[i].astype(F32)
        cntf = jnp.full((8, C_Z), count[i].astype(F32))
        inv_own.append((1.0 / (PAIRED + cntf + NORM_FLOOR))[0:1, :])
        raw = cot_ref[i].astype(F32)
        obg = obg + jnp.sum(raw.reshape(N // 8, 8, C_Z), axis=0)
        g = (raw * jnp.where(same, inv_own[i], 1.0 / (PAIRED + NORM_FLOOR))).astype(BF16)
        g_ref[:, i * 128:(i + 1) * 128] = g
        gm_ref[:, i * 128:(i + 1) * 128] = jnp.where(same, g.astype(F32), 0.0).astype(BF16)

    spread(3, 5)
    forward(1, 7)

    def put_v(v, lane):
        both = jnp.concatenate(
            [v[:, 0:128].reshape(NRES, ROWS, 128), v[:, 128:256].reshape(NRES, ROWS, 128)], axis=1
        )
        v_ref[:, :, pl.ds(lane, 128)] = both.astype(BF16)

    def v_step(p):
        put_v(dot(g_ref[...], tp[pl.ds(pl.multiple_of(p * 256, 256), 256), :], NT), pl.multiple_of(p * 128, 128))

    def rs1(d, kz):
        dst = zpeer(kz) * NY + ypeer(2)
        src = v_ref.at[dst, :, d * HALF:(d + 1) * HALF]
        return rc(src, ry1.at[d, kz], rs1_s.at[0], rs1_r.at[d, kz], res=z * NY + ypeer(3 - 2 * d))

    def rs2(d, kz):
        dst = zpeer(kz) * NY + ypeer(3 - 2 * d)
        return rc(v_ref.at[dst, :, 0:MAIN], ry2.at[d, kz], rs2_s.at[0], rs2_r.at[d, kz], res=z * NY + ypeer(3 - 2 * d))

    def rsz(k):
        return rc(vsum.at[k - 1], rz.at[k - 1], rsz_s.at[0], rsz_r.at[0], res=zpeer(k) * NY + y)

    def bsz(k):
        src = v_ref.at[pl.ds(zpeer(k) * NY, NY), :, MAIN:]
        return rc(src, rbz.at[k - 1], bsz_s.at[0], bsz_r.at[0], res=zpeer(k) * NY + y)

    def bsy(k):
        return rc(sb.at[ypeer(k)], rby.at[k - 1], bsy_s.at[0], bsy_r.at[0], res=z * NY + ypeer(k))

    def side_sums():
        drain(rbz, bsz_s, bsz_r, NZ - 1)
        sbf[...] = v_ref[pl.ds(z * NY, NY), :, MAIN:].astype(F32) + jnp.sum(rbz[...].astype(F32), axis=0)
        sb[...] = sbf[...].astype(BF16)
        for k in range(1, NY):
            bsy(k).start()

    def second(*turns):
        for kz in turns:
            for d in range(2):
                slab = zpeer(kz) * NY + ypeer(3 - 2 * d)
                lanes = slice(d * HALF, (d + 1) * HALF)
                rs1(d, kz).wait_recv()
                v_ref[slab, :, lanes] = (v_ref[slab, :, lanes].astype(F32) + ry1[d, kz].astype(F32)).astype(BF16)
                rs2(d, kz).start()

    def third(*turns):
        for kz in turns:
            total = v_ref[zpeer(kz) * NY + y, :, 0:MAIN].astype(F32)
            for d in range(2):
                rs2(d, kz).wait_recv()
                total = total + ry2[d, kz].astype(F32)
            if kz:
                vsum[kz - 1] = total.astype(BF16)
                rsz(kz).start()
        return total

    def first(*turns):
        for kz in turns:
            for d in range(2):
                rs1(d, kz).start()

    for q in range(2):
        put_v(dot(gm_ref[...], tu[q * 256:(q + 1) * 256, :], NT), MAIN + q * 128)
    pl.loop(0, 4, unroll=2)(v_step)
    spread(4)
    for k in range(1, NZ):
        bsz(k).start()
    forward(2, 6)
    pl.loop(4, 8, unroll=2)(v_step)
    forward(3)
    forward(5)
    first(4, 3, 5, 2, 6)
    forward(4)
    first(1, 7, 0)
    drain(rx.at[:, :, 0:HALF], agf_s, agf_r, 2 * NZ)
    second(4, 3, 5, 2, 6, 1, 7, 0)
    drain(rx.at[:, :, MAIN:], bgz_s, bgz_r, NY * (NZ - 1))

    @pl.loop(0, NRES // 2)
    def _(d):
        a, b = rx[2 * d].astype(F32), rx[2 * d + 1].astype(F32)
        rows = pl.ds(pl.multiple_of(d * 16, 16), 16)
        for h in range(2):
            both = jnp.concatenate([a[h * 8:h * 8 + 8], b[h * 8:h * 8 + 8]], axis=0).astype(BF16)
            for p in range(8):
                rp[rows, p * 256 + h * 128:p * 256 + (h + 1) * 128] = both[:, p * 128:(p + 1) * 128]
            for q in range(2):
                ru[rows, q * 256 + h * 128:q * 256 + (h + 1) * 128] = both[:, 1024 + q * 128:1024 + (q + 1) * 128]

    def u_step(p):
        u = dot(rp[:, pl.ds(pl.multiple_of(p * 256, 256), 256)], g_ref[...], TN).astype(BF16)
        for h in range(2):
            for a in range(2):
                lane = pl.multiple_of((h * 16 + 2 * p + a) * 128, 128)
                for i in range(ROWS):
                    ucat[i * SLOTS:i * SLOTS + PAIRED, pl.ds(lane, 128)] = u[(h * 2 + a) * 64:(h * 2 + a + 1) * 64, i * 128:(i + 1) * 128]

    def u_side(q):
        u = dot(ru[:, q * 256:(q + 1) * 256], gm_ref[...], TN).astype(BF16)
        for h in range(2):
            for a in range(8):
                lane = (h * 16 + q * 8 + a) * 128
                for i in range(ROWS):
                    ucat[i * SLOTS + PAIRED:(i + 1) * SLOTS, lane:lane + 128] = u[(h * 8 + a) * 16:(h * 8 + a + 1) * 16, i * 128:(i + 1) * 128]

    def pd(e):
        k = (e - owner + C_H) % C_H
        return rc(dws.at[e], a_rx.at[k - 1], p_s.at[0], p_r.at[0], **opeer(k))

    def dw_step(g):
        dw = dot(lt[...], ucat[:, g * 256:(g + 1) * 256])
        for a in range(2):
            part = dw[:, a * 128:(a + 1) * 128]
            dwf[2 * g + a] = part
            dws[2 * g + a] = part.astype(BF16)

    def dw_send(first):
        @pl.loop(first, first + 8)
        def _(e):
            @pl.when(e != owner)
            def _():
                pd(e).start()

    pl.loop(0, 4, unroll=2)(u_step)
    u_side(0)
    for g in (0, 1, 2, 3, 8, 9, 10, 11):
        dw_step(g)
    dw_send(0)
    dw_send(16)
    pl.loop(4, 8, unroll=2)(u_step)
    third(4, 3, 5)
    side_sums()
    u_side(1)
    for g in (4, 5, 6, 7, 12, 13, 14, 15):
        dw_step(g)
    dw_send(8)
    dw_send(24)
    own = third(2, 6, 1, 7, 0)

    def left_step(k, acc):
        cols = pl.ds(pl.multiple_of(k * 512, 512), 512)
        return acc + dot(ucat[:, cols], w2_ref[:, cols], NT)

    lgrad = lax.fori_loop(0, 8, left_step, jnp.zeros((ENT, C_H), F32), unroll=2)

    def td(k):
        return rc(sm.at[dpeer(k)], t_rx.at[k - 1], td_s.at[0], td_r.at[0], dp=dpeer(k))

    def uy(k):
        return rc(e_rx.at[y], e_rx.at[y], uy_s.at[0], uy_r.at[0], res=z * NY + ypeer(k))

    def uz(k):
        return rc(f_rx.at[z], f_rx.at[z], uz_s.at[0], uz_r.at[0], res=zpeer(k) * NY + y)

    def wd(k):
        return rc(so.at[dp], so.at[dp], wd_s.at[0], wd_r.at[0], dp=dpeer(k))

    rows8 = iota((8, C_Z), 0)

    def small_put(c, gw, tail_rows):
        tail = jnp.zeros((8, C_Z), F32)
        for k, row in enumerate(tail_rows):
            tail = jnp.where(rows8 == k, row, tail)
        main = jnp.concatenate([gw[:, 0:128], gw[:, 128:256]], axis=0).reshape(8, 8, C_Z)
        tails = jnp.broadcast_to(tail.reshape(8, 1, C_Z), (8, 8, C_Z))
        sm[:, c * 16:(c + 1) * 16, :] = jnp.concatenate([main, tails], axis=1).astype(BF16)

    def total(ref):
        return jnp.sum(ref[...].astype(F32), axis=0)

    gw_l = jnp.zeros((C_H, C_M), F32)
    gb_l = jnp.zeros((1, C_H), F32)
    for r in range(ROWS):
        rows = slice(r * SLOTS, (r + 1) * SLOTS)
        lact = (lgrad[rows] * slot_mask(r, (SLOTS, C_H), 0)).astype(BF16)
        gw_l = gw_l + dot(lact, normed[rows, :], TN)
        gb_l = gb_l + jnp.sum(lact.astype(F32), axis=0, keepdims=True)
        lrow[rows, :] = lact
    small_put(0, gw_l, (
        jnp.sum(obg, axis=0, keepdims=True),
        jnp.concatenate([gb_l, jnp.zeros((1, 96), F32)], axis=1),
    ))

    drain(rz, rsz_s, rsz_r, NZ - 1)
    drain(rby, bsy_s, bsy_r, NY - 1)
    own = jnp.concatenate(
        [own + jnp.sum(rz[...].astype(F32), axis=0), sbf[y] + jnp.sum(rby[...].astype(F32), axis=0)], axis=1
    )
    tiles = []
    for e in range(16):
        tiles.append(jnp.concatenate([own[:, e * 64:(e + 1) * 64], own[:, 1024 + e * 16:1024 + (e + 1) * 16]], axis=1))
    back = dot(permq, jnp.concatenate(tiles, axis=0).astype(BF16), TN)

    gw_r = jnp.zeros((C_H, C_M), F32)
    gb_r = jnp.zeros((C_H, 1), F32)
    gain_g = jnp.zeros((1, C_M), F32)
    shift_g = jnp.zeros((1, C_M), F32)
    for r in range(ROWS):
        rows = slice(r * SLOTS, (r + 1) * SLOTS)
        ract_t = (back[r * C_H:(r + 1) * C_H, :] * slot_mask(r, (C_H, SLOTS), 1)).astype(BF16)
        gw_r = gw_r + dot(ract_t, normed[rows, :])
        gb_r = gb_r + jnp.sum(ract_t.astype(F32), axis=1, keepdims=True)
        gn = dot(lrow[rows, :], wt_ref[0:C_H, :]) + dot(ract_t, wt_ref[C_H:, :], TN)
        scaled = xc[rows, :]
        gain_g = gain_g + jnp.sum(gn * scaled, axis=0, keepdims=True)
        shift_g = shift_g + jnp.sum(gn, axis=0, keepdims=True)
        gg = gn * gain_ref[...]
        mean_g = jnp.mean(gg, axis=-1, keepdims=True)
        mean_p = jnp.mean(gg * scaled, axis=-1, keepdims=True)
        ract[rows, :] = (inv_ref[rows, :] * (gg - mean_g - scaled * mean_p)).astype(BF16)
    gbr_row = jnp.transpose(jnp.broadcast_to(gb_r, (C_H, 128)))[0:1, :]
    small_put(1, gw_r, (
        gain_g[:, 0:128], gain_g[:, 128:256], shift_g[:, 0:128], shift_g[:, 128:256],
        jnp.concatenate([gbr_row, jnp.zeros((1, 96), F32)], axis=1),
    ))

    for k in range(1, NDP):
        td(k).start()

    drain(a_rx, p_s, p_r, C_H - 1)

    def add(k, t):
        return t + a_rx[k].astype(F32)

    c_rx[z] = lax.fori_loop(0, C_H - 1, add, dwf[owner], unroll=True).astype(BF16)

    def cz(k):
        return rc(c_rx.at[z], c_rx.at[z], cz_s.at[0], cz_r.at[0], res=zpeer(k) * NY + y)

    for k in range(1, NZ):
        cz(k).start()

    drain(t_rx, td_s, td_r, NDP - 1)
    e_rx[y] = (sm[dp].astype(F32) + total(t_rx)).astype(BF16)
    for k in range(1, NY):
        uy(k).start()

    drain(c_rx, cz_s, cz_r, NZ - 1)
    d_rx[owner] = (total(c_rx) * (1.0 / N)).astype(BF16)

    def ed(k):
        return rc(d_rx.at[owner], d_rx.at[owner], ed_s.at[0], ed_r.at[0], **opeer(k))

    @pl.loop(1, C_H)
    def _(k):
        ed(k).start()

    drain(e_rx, uy_s, uy_r, NY - 1)
    f_rx[z] = total(e_rx).astype(BF16)
    for k in range(1, NZ):
        uz(k).start()

    @pl.loop(0, 4)
    def _(g):
        cols = pl.ds(pl.multiple_of(g * 256, 256), 256)
        main = dot(rp[...], tp[:, cols])
        side = dot(ru[...], tu[:, cols])
        for a in range(2):
            i = 2 * g + a
            ch = jnp.int32(0)
            iv = jnp.zeros((1, C_Z), F32)
            for r in range(ROWS):
                ch = jnp.where(i == r, chain[r], ch)
                iv = jnp.where(i == r, inv_own[r], iv)
            same = chain_col == ch.astype(F32)
            m, s = main[:, a * 128:(a + 1) * 128], side[:, a * 128:(a + 1) * 128]
            out = jnp.where(same, (m + s) * iv, m * (1.0 / (PAIRED + NORM_FLOOR))) + obias_ref[...]
            upd_ref[i] = out.astype(BF16)

    for b in range(PAIRED // 16):
        src = jnp.concatenate([ract[r * SLOTS + b * 16:r * SLOTS + b * 16 + 16, :] for r in range(ROWS)], axis=0)
        agrad_ref[b * 128:(b + 1) * 128, :] = dot(perm0, src, TN).astype(BF16)
    src = jnp.concatenate([ract[r * SLOTS + PAIRED:(r + 1) * SLOTS, :] for r in range(ROWS)], axis=0)
    agrad_ref[PAIRED * ROWS:, :] = dot(pick, src, TN).astype(BF16)

    upd_out = pltpu.make_async_copy(upd_ref, upd_h, out_s.at[0])
    upd_out.start()

    agrad_out = pltpu.make_async_copy(agrad_ref, agrad_h, out_s.at[1])
    agrad_out.start()

    drain(f_rx, uz_s, uz_r, NZ - 1)
    so[dp] = (total(f_rx) * (1.0 / N)).astype(BF16)
    for k in range(1, NDP):
        wd(k).start()

    def sent(ref, sem):
        rc(ref, ref, sem.at[0], sem.at[0], dp=dpeer(1)).wait_send()

    sent(rx.at[0:NZ - 1, :, 0:MAIN], agz_s)
    sent(rx.at[0:2 * NZ, :, 0:MAIN], agy_s)
    sent(v_ref.at[0:2 * NZ, :, 0:HALF], rs1_s)
    sent(v_ref.at[0:2 * NZ, :, 0:MAIN], rs2_s)

    drain(d_rx, ed_s, ed_r, C_H - 1)
    dw_out = pltpu.make_async_copy(d_rx, dw_h, out_s.at[2])
    dw_out.start()
    drain(so, wd_s, wd_r, NDP - 1)
    small_out = pltpu.make_async_copy(so, small_h, out_s.at[3])
    small_out.start()
    for c in (upd_out, agrad_out, dw_out, small_out):
        c.wait()


def finish(
    upd_i, agrad_i, dw_i, small_i,
    upd_h, agrad_h, lw_h, lb_h, rw_h, rb_h, dw_h, ob_h, gain_h, shift_h,
    upd_v, agrad_v, dw_v, small_v, dw_f, lw_f, rw_f, lb_f, rb_f, ob_f, gain_f, shift_f, sem,
):
    copies = []

    def send(src, dst):
        copies.append(pltpu.make_async_copy(src, dst, sem.at[len(copies)]))
        copies[-1].start()

    fetches = [
        pltpu.make_async_copy(src, dst, sem.at[10 + n])
        for n, (src, dst) in enumerate(((dw_i, dw_v), (small_i, small_v), (upd_i, upd_v), (agrad_i, agrad_v)))
    ]
    for f in fetches:
        f.start()
    fetches[0].wait()
    for d in range(NDP):
        for a in range(4):
            dw_f[:, d * 4 + a, :] = dw_v[d * 4 + a].astype(F32)
    send(dw_f, dw_h)
    fetches[2].wait()
    send(upd_v, upd_h)
    fetches[3].wait()
    send(agrad_v, agrad_h)
    fetches[1].wait()

    def tail(c, k):
        return small_v[k].astype(F32)[c * 16 + 8:c * 16 + 9]

    for c, (buf, out) in enumerate(((lw_f, lw_h), (rw_f, rw_h))):
        for half in range(2):
            rows = [small_v[half * 4 + d].astype(F32)[c * 16:c * 16 + 8] for d in range(4)]
            buf[:, half * 128:(half + 1) * 128] = jnp.concatenate(rows, axis=0)
        send(buf, out)
    ob_f[...] = tail(0, 0)
    lb_f[...] = tail(0, 1)[:, 0:C_H]
    rb_f[...] = tail(1, 4)[:, 0:C_H]
    gain_f[...] = jnp.concatenate([tail(1, 0), tail(1, 1)], axis=1)
    shift_f[...] = jnp.concatenate([tail(1, 2), tail(1, 3)], axis=1)
    for buf, out in ((ob_f, ob_h), (lb_f, lb_h), (rb_f, rb_h), (gain_f, gain_h), (shift_f, shift_h)):
        send(buf, out)
    for c in copies:
        c.wait()


def body(
    alignment, chain_ids, row_counts, norm_gain, norm_shift, left_weight, left_bias,
    right_weight, right_bias, out_weight, out_bias, pair_cotangent,
):
    sems = lambda *shape: pltpu.SemaphoreType.DMA(shape)
    vmem = pltpu.VMEM
    scratch = [
        vmem((ROWS, N, C_Z), BF16), vmem((128 * ROWS, C_M), BF16), pltpu.SMEM((1, N), jnp.int32), pltpu.SMEM((1, CHAINS), jnp.int32), vmem((1, N), jnp.int32),
        vmem((128 * ROWS, C_M), BF16), vmem((1, C_M), F32), vmem((1, C_M), F32), vmem((1, C_H), F32),
        vmem((1, C_H), F32), vmem((C_H * C_H, C_Z), BF16), vmem((1, C_Z), F32), vmem((ROWS, N, C_Z), BF16),
        vmem((2 * C_H, C_M), BF16), vmem((C_H * C_H, C_Z), F32), vmem((C_H, C_H * C_Z), BF16),
        vmem((ENT, C_M), F32), vmem((ENT, C_M), BF16), vmem((ENT, 1), F32),
        vmem((ENT, C_H), BF16), vmem((C_H, ENT), BF16), vmem((256, 128), BF16),
        vmem((2048, 1024), BF16), vmem((512, 1024), BF16), vmem((N, 1024), BF16), vmem((N, 1024), BF16),
        vmem((NRES, 16, 1280), BF16), vmem((NRES, 16, 1280), BF16), vmem((N, 2048), BF16), vmem((N, 512), BF16),
        vmem((2, NZ, 16, HALF), BF16), vmem((2, NZ, 16, MAIN), BF16), vmem((NZ - 1, 16, MAIN), BF16), vmem((NZ - 1, 16, MAIN), BF16),
        vmem((NZ - 1, NY, 16, 256), BF16), vmem((NY, 16, 256), F32), vmem((NY, 16, 256), BF16), vmem((NY - 1, 16, 256), BF16),
        vmem((ENT, 4096), BF16),
        vmem((C_H, C_H, C_Z), F32), vmem((C_H, C_H, C_Z), BF16), vmem((C_H - 1, C_H, C_Z), BF16),
        vmem((NZ, C_H, C_Z), BF16), vmem((C_H, C_H, C_Z), BF16),
        vmem((NDP, 32, C_Z), BF16), vmem((NDP - 1, 32, C_Z), BF16), vmem((NY, 32, C_Z), BF16), vmem((NZ, 32, C_Z), BF16), vmem((NDP, 32, C_Z), BF16),
        vmem((ENT, C_M), BF16),
        sems(13), sems(4), sems(1), sems(1), sems(1), sems(1), sems(1), sems(1), sems(1), sems(1),
        sems(1), sems(NZ), sems(1), sems(2, NZ), sems(1), sems(1),
        sems(1), sems(2, NZ), sems(1), sems(2, NZ), sems(1), sems(1),
        sems(1), sems(1), sems(1), sems(1), sems(1), sems(1),
        sems(1), sems(1), sems(1), sems(1), sems(1), sems(1), sems(1), sems(1),
    ]
    hbm = pl.BlockSpec(memory_space=pltpu.HBM)
    upd, agrad, dw, small = pl.pallas_call(
        kernel,
        out_shape=(
            jax.ShapeDtypeStruct((ROWS, N, C_Z), BF16),
            jax.ShapeDtypeStruct((128 * ROWS, C_M), BF16),
            jax.ShapeDtypeStruct((C_H, C_H, C_Z), BF16),
            jax.ShapeDtypeStruct((NDP, 32, C_Z), BF16),
        ),
        in_specs=[hbm] * 12,
        out_specs=(hbm,) * 4,
        scratch_shapes=scratch,
        compiler_params=pltpu.CompilerParams(
            collective_id=0, has_side_effects=True, vmem_limit_bytes=56 * 1024 * 1024
        ),
    )(
        chain_ids, row_counts, alignment.reshape(128 * ROWS, C_M),
        norm_gain.reshape(1, C_M), norm_shift.reshape(1, C_M), left_weight.T, left_bias.reshape(1, C_H),
        right_weight.T, right_bias.reshape(1, C_H), out_weight, out_bias.reshape(1, C_Z), pair_cotangent[0],
    )
    outs = (
        ((ROWS, N, C_Z), BF16), ((128 * ROWS, C_M), BF16), ((C_H, C_M), F32), ((1, C_H), F32), ((C_H, C_M), F32),
        ((1, C_H), F32), ((C_H, C_H, C_Z), F32), ((1, C_Z), F32), ((1, C_M), F32), ((1, C_M), F32),
    )
    upd, agrad, lw, lb, rw, rb, dw, ob, gain, shift = pl.pallas_call(
        finish,
        out_shape=tuple(jax.ShapeDtypeStruct(*o) for o in outs),
        in_specs=[hbm] * 4,
        out_specs=(hbm,) * 10,
        scratch_shapes=[
            vmem((ROWS, N, C_Z), BF16), vmem((128 * ROWS, C_M), BF16),
            vmem((C_H, C_H, C_Z), BF16), vmem((NDP, 32, C_Z), BF16), vmem((C_H, C_H, C_Z), F32), vmem((C_H, C_M), F32), vmem((C_H, C_M), F32), vmem((1, C_H), F32), vmem((1, C_H), F32),
            vmem((1, C_Z), F32), vmem((1, C_M), F32), vmem((1, C_M), F32), sems(14),
        ],
        compiler_params=pltpu.CompilerParams(vmem_limit_bytes=56 * 1024 * 1024),
    )(upd, agrad, dw, small)
    return (
        upd[None],
        agrad.reshape(1, 128, ROWS, C_M),
        lw.T,
        lb.reshape(C_H),
        rw.T,
        rb.reshape(C_H),
        dw.reshape(C_H * C_H, C_Z),
        ob.reshape(C_Z),
        gain.reshape(C_M),
        shift.reshape(C_M),
    )


def solution(mesh):
    return jax.shard_map(
        body,
        mesh=mesh,
        in_specs=(
            P("dp", None, "res", None), P("dp", None), P("dp", None), P(), P(), P(), P(), P(), P(), P(), P(),
            P("dp", "res", None, None),
        ),
        out_specs=(
            P("dp", "res", None, None), P("dp", None, "res", None), P(), P(), P(), P(), P(), P(), P(), P(),
        ),
        check_vma=False,
    )
```

```python
import functools

import jax
import jax.numpy as jnp
from jax import lax
from jax.experimental import pallas as pl
from jax.experimental.pallas import tpu as pltpu
from jax.sharding import PartitionSpec as P

C_M = 256
C_H = 32
C_Z = 128
PAIRED = 64
UNP = 64
MOST = 16
CHAINS = 12
EPSILON = 1e-05
NORM_FLOOR = 0.001

ROWS = 8
SLOTS = PAIRED + MOST
NY, NZ, NDP = 4, 8, 8
NRES = NY * NZ
N = ROWS * NRES
ENT = ROWS * SLOTS
MAIN = 1024
HALF = MAIN // 2
F32, BF16 = jnp.float32, jnp.bfloat16
MESH = pl.DeviceIdType.MESH

NN = (((1,), (0,)), ((), ()))
NT = (((1,), (1,)), ((), ()))
TN = (((0,), (0,)), ((), ()))


def dot(a, b, dims=NN):
    return lax.dot_general(a, b, dims, preferred_element_type=F32)


def iota(shape, dim):
    return lax.broadcasted_iota(jnp.int32, shape, dim)


def onehot(cond):
    return jnp.where(cond, 1.0, 0.0).astype(BF16)


def kernel(
    chain_h, counts_h, x_h, gain_h, shift_h, lw_h, lb_h, rw_h, rb_h, w_h, ob_h, cot_h,
    upd_h, agrad_h, dw_h, small_h,
    upd_ref, agrad_ref, chain_s, counts_s, chain_v, x_ref, gain_ref, shift_ref, lb_ref, rb_ref, w_ref, obias_ref, cot_ref,
    wt_ref, wf, w2_ref,
    xc, normed, inv_ref, lrow, lt, q_ref, tp, tu, g_ref, gm_ref, v_ref, rx, rp, ru,
    ry1, ry2, vsum, rz, rbz, sbf, sb, rby, ucat, dwf, dws, a_rx, c_rx, d_rx,
    sm, t_rx, f_rx, so, ract,
    in_s, out_s, bgy_s, bgy_r, bgz_s, bgz_r, bsz_s, bsz_r, bsy_s, bsy_r, agz_s, agz_r, agy_s, agy_r, agf_s, agf_r, rs1_s, rs1_r, rs2_s, rs2_r, rsz_s, rsz_r,
    p_s, p_r, cz_s, cz_r, ed_s, ed_r,
    td_s, td_r, uz_s, uz_r, wd_s, wd_r,
):
    me = lax.axis_index("res")
    dp = lax.axis_index("dp")
    z, y = me // NY, me % NY

    def zpeer(k):
        return (z + k) % NZ

    def ypeer(k):
        return (y + k) % NY

    def dpeer(k):
        return (dp + k) % NDP

    def rc(src, dst, ss, rs, **where):
        return pltpu.make_async_remote_copy(
            src_ref=src, dst_ref=dst, send_sem=ss, recv_sem=rs,
            device_id=where, device_id_type=MESH,
        )

    fetches = [
        pltpu.make_async_copy(src, dst, in_s.at[n])
        for n, (src, dst) in enumerate((
            (x_h, x_ref), (chain_h, chain_s), (counts_h, counts_s), (chain_h, chain_v), (gain_h, gain_ref),
            (shift_h, shift_ref), (lw_h, wt_ref.at[0:C_H]), (lb_h, lb_ref), (rw_h, wt_ref.at[C_H:2 * C_H]), (rb_h, rb_ref),
            (w_h, w_ref), (ob_h, obias_ref), (cot_h, cot_ref),
        ))
    ]
    for f in fetches:
        f.start()

    barrier = pltpu.get_barrier_semaphore()

    @pl.loop(1, NRES)
    def _(k):
        pl.semaphore_signal(barrier, inc=1, device_id={"res": (me + k) % NRES}, device_id_type=MESH)

    owner = dp * NY + y

    def opeer(k):
        o = (owner + k) % C_H
        return {"dp": o // NY, "res": z * NY + o % NY}

    @pl.loop(1, NDP)
    def _(k):
        for j in range(NY):
            pl.semaphore_signal(
                barrier, inc=1, device_id={"dp": dpeer(k), "res": z * NY + ypeer(j)}, device_id_type=MESH
            )

    for f in fetches[:10]:
        f.wait()
    rb_col = jnp.transpose(jnp.broadcast_to(rb_ref[...], (8, C_H)))[:, 0:1]

    chain, start, count, base = [], [], [], []
    for r in range(ROWS):
        c = chain_s[0, me * ROWS + r]
        st = jnp.int32(0)
        ct = jnp.int32(0)
        for k in range(CHAINS):
            v = counts_s[0, k]
            st = st + jnp.where(c > k, v, 0)
            ct = ct + jnp.where(c == k, v, 0)
        chain.append(c)
        start.append(st)
        count.append(ct)
        base.append(jnp.minimum(st, UNP - MOST))

    def slot_mask(r, shape, dim):
        s = iota(shape, dim)
        row = s - PAIRED + base[r]
        live = (row >= start[r]) & (row < start[r] + count[r])
        return jnp.where((s < PAIRED) | live, 1.0, 0.0)

    ro, co = iota((128, 128), 0), iota((128, 128), 1)
    perm0 = onehot(co == (ro % 16) * ROWS + ro // 16)
    for b in range(PAIRED // 16):
        part = dot(perm0, x_ref[b * 128:(b + 1) * 128, :])
        for r in range(ROWS):
            xc[r * SLOTS + b * 16:r * SLOTS + b * 16 + 16, :] = part[r * 16:(r + 1) * 16]
    ru_i = iota((128, UNP * ROWS), 0)
    base_rows = jnp.zeros((128, UNP * ROWS), jnp.int32)
    for r in range(ROWS):
        base_rows = jnp.where(ru_i // 16 == r, base[r], base_rows)
    pick = onehot(iota((128, UNP * ROWS), 1) == (base_rows + ru_i % 16) * ROWS + ru_i // 16)
    part = dot(pick, x_ref[PAIRED * ROWS:, :])
    for r in range(ROWS):
        xc[r * SLOTS + PAIRED:(r + 1) * SLOTS, :] = part[r * 16:(r + 1) * 16]

    for r in range(ROWS):
        rows = slice(r * SLOTS, (r + 1) * SLOTS)
        floats = xc[rows, :]
        centred = floats - jnp.mean(floats, axis=-1, keepdims=True)
        inverse = lax.rsqrt(jnp.mean(centred * centred, axis=-1, keepdims=True) + EPSILON)
        scaled = centred * inverse
        nrm = (scaled * gain_ref[...] + shift_ref[...]).astype(BF16)
        xc[rows, :] = scaled
        inv_ref[rows, :] = inverse
        normed[rows, :] = nrm
        left = (dot(nrm, wt_ref[0:C_H, :], NT) + lb_ref[...]) * slot_mask(r, (SLOTS, C_H), 0)
        lrow[rows, :] = left.astype(BF16)
        right = (dot(wt_ref[C_H:, :], nrm, NT) + rb_col) * slot_mask(r, (C_H, SLOTS), 1)
        q_ref[r * C_H:(r + 1) * C_H, 0:SLOTS] = right.astype(BF16)
    re, ce = iota((256, 256), 0), iota((256, 256), 1)
    permq = onehot(ce == (re % 8) * 32 + ((re // 8) % 2) * 16 + re // 16)
    mixed = dot(permq, q_ref[:, 0:SLOTS])
    for p in range(8):
        rx[me, :, p * 128:(p + 1) * 128] = jnp.concatenate(
            [mixed[(2 * p + a) * 16:(2 * p + a + 1) * 16, 0:PAIRED] for a in range(2)], axis=1
        ).astype(BF16)
    for q in range(2):
        rx[me, :, 1024 + q * 128:1024 + (q + 1) * 128] = jnp.concatenate(
            [mixed[(8 * q + a) * 16:(8 * q + a + 1) * 16, PAIRED:SLOTS] for a in range(8)], axis=1
        ).astype(BF16)

    pl.semaphore_wait(barrier, NRES - 1 + NY * (NDP - 1))

    def agz(k):
        part = rx.at[me, :, 0:MAIN]
        return rc(part, part, agz_s.at[0], agz_r.at[k], res=zpeer(k) * NY + y)

    def agy(d, kz):
        slot = ((z - kz + NZ) % NZ) * NY + y
        part = rx.at[slot, :, 0:MAIN]
        return rc(part, part, agy_s.at[0], agy_r.at[d, kz], res=z * NY + ypeer(1 + 2 * d))

    def agf(d, kz):
        slot = ((z - kz + NZ) % NZ) * NY + ypeer(3 - 2 * d)
        part = rx.at[slot, :, d * HALF:(d + 1) * HALF]
        return rc(part, part, agf_s.at[0], agf_r.at[0], res=z * NY + ypeer(1 + 2 * d))

    def bgy(k):
        part = rx.at[me, :, MAIN:]
        return rc(part, part, bgy_s.at[0], bgy_r.at[0], res=z * NY + ypeer(k))

    def bgz(k):
        part = rx.at[pl.ds(z * NY, NY), :, MAIN:]
        return rc(part, part, bgz_s.at[0], bgz_r.at[0], res=zpeer(k) * NY + y)

    def drain(ref, send, recv, count):
        some = ref.at[0:count]
        rc(some, some, send.at[0], recv.at[0], dp=dpeer(1)).wait()

    def spread(*turns):
        for kz in turns:
            if kz:
                agz(kz).wait_recv()
            for d in range(2):
                agy(d, kz).start()

    def forward(*turns):
        for kz in turns:
            for d in range(2):
                agy(d, kz).wait_recv()
                agf(d, kz).start()

    for k in range(1, NY):
        bgy(k).start()
    for k in (1, 7, 2, 6, 3, 5, 4):
        agz(k).start()
    spread(0)

    for f in fetches[10:]:
        f.wait()
    wf[...] = w_ref[...].astype(F32)
    for e in range(C_H):
        w2_ref[:, e * 128:(e + 1) * 128] = wf[pl.ds(e, C_H, stride=C_H), :].astype(BF16)

    lt[...] = jnp.transpose(lrow[...].astype(F32)).astype(BF16)

    def t_step(g):
        h, p = g // 8, g % 8
        t = dot(lrow[...], w2_ref[:, pl.ds(pl.multiple_of(g * 256, 256), 256)]).astype(BF16)
        rowp = pl.multiple_of((p * 2 + h) * 128, 128)
        rowu = pl.multiple_of(((p // 4) * 2 + h) * 128 + (p % 4) * 32, 32)
        for i in range(ROWS):
            for a in range(2):
                tp[pl.ds(rowp + a * 64, 64), i * 128:(i + 1) * 128] = t[i * SLOTS:i * SLOTS + PAIRED, a * 128:(a + 1) * 128]
                tu[pl.ds(rowu + a * 16, 16), i * 128:(i + 1) * 128] = t[i * SLOTS + PAIRED:(i + 1) * SLOTS, a * 128:(a + 1) * 128]

    pl.loop(0, 12, unroll=2)(t_step)
    spread(1, 7)
    pl.loop(12, 16, unroll=2)(t_step)
    spread(2, 6)
    forward(0)
    chain_col = jnp.transpose(jnp.broadcast_to(chain_v[...].astype(F32), (128, N)))
    obg = jnp.zeros((8, C_Z), F32)
    inv_own = []
    for i in range(ROWS):
        same = chain_col == chain[i].astype(F32)
        cntf = jnp.full((8, C_Z), count[i].astype(F32))
        inv_own.append((1.0 / (PAIRED + cntf + NORM_FLOOR))[0:1, :])
        raw = cot_ref[i].astype(F32)
        obg = obg + jnp.sum(raw.reshape(N // 8, 8, C_Z), axis=0)
        g = (raw * jnp.where(same, inv_own[i], 1.0 / (PAIRED + NORM_FLOOR))).astype(BF16)
        g_ref[:, i * 128:(i + 1) * 128] = g
        gm_ref[:, i * 128:(i + 1) * 128] = jnp.where(same, g.astype(F32), 0.0).astype(BF16)

    spread(3, 5)
    drain(rx.at[:, :, MAIN:], bgy_s, bgy_r, NY - 1)
    for k in range(1, NZ):
        bgz(k).start()
    forward(1, 7)

    def put_v(v, lane):
        both = jnp.concatenate(
            [v[:, 0:128].reshape(NRES, ROWS, 128), v[:, 128:256].reshape(NRES, ROWS, 128)], axis=1
        )
        v_ref[:, :, pl.ds(lane, 128)] = both.astype(BF16)

    def v_step(p):
        put_v(dot(g_ref[...], tp[pl.ds(pl.multiple_of(p * 256, 256), 256), :], NT), pl.multiple_of(p * 128, 128))

    def rs1(d, kz):
        dst = zpeer(kz) * NY + ypeer(2)
        src = v_ref.at[dst, :, d * HALF:(d + 1) * HALF]
        return rc(src, ry1.at[d, kz], rs1_s.at[0], rs1_r.at[d, kz], res=z * NY + ypeer(3 - 2 * d))

    def rs2(d, kz):
        dst = zpeer(kz) * NY + ypeer(3 - 2 * d)
        return rc(v_ref.at[dst, :, 0:MAIN], ry2.at[d, kz], rs2_s.at[0], rs2_r.at[d, kz], res=z * NY + ypeer(3 - 2 * d))

    def rsz(k):
        return rc(vsum.at[k - 1], rz.at[k - 1], rsz_s.at[0], rsz_r.at[0], res=zpeer(k) * NY + y)

    def bsz(k):
        src = v_ref.at[pl.ds(zpeer(k) * NY, NY), :, MAIN:]
        return rc(src, rbz.at[k - 1], bsz_s.at[0], bsz_r.at[0], res=zpeer(k) * NY + y)

    def bsy(k):
        return rc(sb.at[ypeer(k)], rby.at[k - 1], bsy_s.at[0], bsy_r.at[0], res=z * NY + ypeer(k))

    def side_sums():
        drain(rbz, bsz_s, bsz_r, NZ - 1)
        sbf[...] = v_ref[pl.ds(z * NY, NY), :, MAIN:].astype(F32) + jnp.sum(rbz[...].astype(F32), axis=0)
        sb[...] = sbf[...].astype(BF16)
        for k in range(1, NY):
            bsy(k).start()

    def second(*turns):
        for kz in turns:
            for d in range(2):
                slab = zpeer(kz) * NY + ypeer(3 - 2 * d)
                lanes = slice(d * HALF, (d + 1) * HALF)
                rs1(d, kz).wait_recv()
                v_ref[slab, :, lanes] = (v_ref[slab, :, lanes].astype(F32) + ry1[d, kz].astype(F32)).astype(BF16)

    def pass_on(*turns):
        for kz in turns:
            for d in range(2):
                rs2(d, kz).start()

    def third(*turns):
        for kz in turns:
            total = v_ref[zpeer(kz) * NY + y, :, 0:MAIN].astype(F32)
            for d in range(2):
                rs2(d, kz).wait_recv()
                total = total + ry2[d, kz].astype(F32)
            if kz:
                vsum[kz - 1] = total.astype(BF16)
                rsz(kz).start()
        return total

    def first(*turns):
        for kz in turns:
            for d in range(2):
                rs1(d, kz).start()

    for q in range(2):
        put_v(dot(gm_ref[...], tu[q * 256:(q + 1) * 256, :], NT), MAIN + q * 128)
    pl.loop(0, 4, unroll=2)(v_step)
    spread(4)
    forward(2, 6)
    pl.loop(4, 8, unroll=2)(v_step)
    forward(3)
    forward(5)
    first(4, 3, 5, 2, 6)
    forward(4)
    first(1, 7, 0)
    for k in range(1, NZ):
        bsz(k).start()
    second(4, 3, 5, 2)
    pass_on(4, 3, 5, 2)
    second(6, 1, 7, 0)
    drain(rx.at[:, :, 0:HALF], agf_s, agf_r, 2 * NZ)
    pass_on(6, 1, 7, 0)
    drain(rx.at[:, :, MAIN:], bgz_s, bgz_r, NY * (NZ - 1))

    @pl.loop(0, NRES // 2)
    def _(d):
        a, b = rx[2 * d].astype(F32), rx[2 * d + 1].astype(F32)
        rows = pl.ds(pl.multiple_of(d * 16, 16), 16)
        for h in range(2):
            both = jnp.concatenate([a[h * 8:h * 8 + 8], b[h * 8:h * 8 + 8]], axis=0).astype(BF16)
            for p in range(8):
                rp[rows, p * 256 + h * 128:p * 256 + (h + 1) * 128] = both[:, p * 128:(p + 1) * 128]
            for q in range(2):
                ru[rows, q * 256 + h * 128:q * 256 + (h + 1) * 128] = both[:, 1024 + q * 128:1024 + (q + 1) * 128]

    def u_step(p):
        u = dot(rp[:, pl.ds(pl.multiple_of(p * 256, 256), 256)], g_ref[...], TN).astype(BF16)
        for h in range(2):
            for a in range(2):
                lane = pl.multiple_of((h * 16 + 2 * p + a) * 128, 128)
                for i in range(ROWS):
                    ucat[i * SLOTS:i * SLOTS + PAIRED, pl.ds(lane, 128)] = u[(h * 2 + a) * 64:(h * 2 + a + 1) * 64, i * 128:(i + 1) * 128]

    def u_side(q):
        u = dot(ru[:, q * 256:(q + 1) * 256], gm_ref[...], TN).astype(BF16)
        for h in range(2):
            for a in range(8):
                lane = (h * 16 + q * 8 + a) * 128
                for i in range(ROWS):
                    ucat[i * SLOTS + PAIRED:(i + 1) * SLOTS, lane:lane + 128] = u[(h * 8 + a) * 16:(h * 8 + a + 1) * 16, i * 128:(i + 1) * 128]

    def pd(e):
        k = (e - owner + C_H) % C_H
        return rc(dws.at[e], a_rx.at[k - 1], p_s.at[0], p_r.at[0], **opeer(k))

    def dw_step(g):
        dw = dot(lt[...], ucat[:, g * 256:(g + 1) * 256])
        for a in range(2):
            part = dw[:, a * 128:(a + 1) * 128]
            dwf[2 * g + a] = part
            dws[2 * g + a] = part.astype(BF16)

    def dw_send(first):
        @pl.loop(first, first + 8)
        def _(e):
            @pl.when(e != owner)
            def _():
                pd(e).start()

    pl.loop(0, 4, unroll=2)(u_step)
    u_side(0)
    for g in (0, 1, 2, 3, 8, 9, 10, 11):
        dw_step(g)
    dw_send(0)
    dw_send(16)
    pl.loop(4, 8, unroll=2)(u_step)
    u_side(1)
    third(4, 3, 5)
    side_sums()
    third(2)
    for g in (4, 5, 6, 7, 12, 13, 14, 15):
        dw_step(g)
    dw_send(8)
    dw_send(24)
    own = third(6, 1, 7, 0)

    def left_step(k, acc):
        cols = pl.ds(pl.multiple_of(k * 512, 512), 512)
        return acc + dot(ucat[:, cols], w2_ref[:, cols], NT)

    lgrad = lax.fori_loop(0, 8, left_step, jnp.zeros((ENT, C_H), F32), unroll=2)

    def td(k):
        slot = (owner + k) % C_H // NY
        return rc(sm.at[slot], t_rx.at[owner], td_s.at[0], td_r.at[0], **opeer(k))

    def uz(k):
        return rc(f_rx.at[z], f_rx.at[z], uz_s.at[0], uz_r.at[0], res=zpeer(k) * NY + y)

    def wd(k):
        return rc(so.at[dp], so.at[dp], wd_s.at[0], wd_r.at[0], dp=dpeer(k))

    rows8 = iota((8, C_Z), 0)

    def small_put(c, gw, tail_rows):
        tail = jnp.zeros((8, C_Z), F32)
        for k, row in enumerate(tail_rows):
            tail = jnp.where(rows8 == k, row, tail)
        main = jnp.concatenate([gw[:, 0:128], gw[:, 128:256]], axis=0).reshape(8, 8, C_Z)
        tails = jnp.broadcast_to(tail.reshape(8, 1, C_Z), (8, 8, C_Z))
        sm[:, c * 16:(c + 1) * 16, :] = jnp.concatenate([main, tails], axis=1).astype(BF16)

    def total(ref):
        return jnp.sum(ref[...].astype(F32), axis=0)

    gw_l = jnp.zeros((C_H, C_M), F32)
    gb_l = jnp.zeros((1, C_H), F32)
    for r in range(ROWS):
        rows = slice(r * SLOTS, (r + 1) * SLOTS)
        lact = (lgrad[rows] * slot_mask(r, (SLOTS, C_H), 0)).astype(BF16)
        gw_l = gw_l + dot(lact, normed[rows, :], TN)
        gb_l = gb_l + jnp.sum(lact.astype(F32), axis=0, keepdims=True)
        lrow[rows, :] = lact
    small_put(0, gw_l, (
        jnp.sum(obg, axis=0, keepdims=True),
        jnp.concatenate([gb_l, jnp.zeros((1, 96), F32)], axis=1),
    ))

    drain(rz, rsz_s, rsz_r, NZ - 1)
    drain(rby, bsy_s, bsy_r, NY - 1)
    own = jnp.concatenate(
        [own + jnp.sum(rz[...].astype(F32), axis=0), sbf[y] + jnp.sum(rby[...].astype(F32), axis=0)], axis=1
    )
    tiles = []
    for e in range(16):
        tiles.append(jnp.concatenate([own[:, e * 64:(e + 1) * 64], own[:, 1024 + e * 16:1024 + (e + 1) * 16]], axis=1))
    back = dot(permq, jnp.concatenate(tiles, axis=0).astype(BF16), TN)

    gw_r = jnp.zeros((C_H, C_M), F32)
    gb_r = jnp.zeros((C_H, 1), F32)
    gain_g = jnp.zeros((1, C_M), F32)
    shift_g = jnp.zeros((1, C_M), F32)
    for r in range(ROWS):
        rows = slice(r * SLOTS, (r + 1) * SLOTS)
        ract_t = (back[r * C_H:(r + 1) * C_H, :] * slot_mask(r, (C_H, SLOTS), 1)).astype(BF16)
        gw_r = gw_r + dot(ract_t, normed[rows, :])
        gb_r = gb_r + jnp.sum(ract_t.astype(F32), axis=1, keepdims=True)
        gn = dot(lrow[rows, :], wt_ref[0:C_H, :]) + dot(ract_t, wt_ref[C_H:, :], TN)
        scaled = xc[rows, :]
        gain_g = gain_g + jnp.sum(gn * scaled, axis=0, keepdims=True)
        shift_g = shift_g + jnp.sum(gn, axis=0, keepdims=True)
        gg = gn * gain_ref[...]
        mean_g = jnp.mean(gg, axis=-1, keepdims=True)
        mean_p = jnp.mean(gg * scaled, axis=-1, keepdims=True)
        ract[rows, :] = (inv_ref[rows, :] * (gg - mean_g - scaled * mean_p)).astype(BF16)
    gbr_row = jnp.transpose(jnp.broadcast_to(gb_r, (C_H, 128)))[0:1, :]
    small_put(1, gw_r, (
        gain_g[:, 0:128], gain_g[:, 128:256], shift_g[:, 0:128], shift_g[:, 128:256],
        jnp.concatenate([gbr_row, jnp.zeros((1, 96), F32)], axis=1),
    ))

    @pl.loop(1, C_H)
    def _(k):
        td(k).start()

    drain(a_rx, p_s, p_r, C_H - 1)

    def add(k, t):
        return t + a_rx[k].astype(F32)

    c_rx[z] = lax.fori_loop(0, C_H - 1, add, dwf[owner], unroll=True).astype(BF16)

    def cz(k):
        return rc(c_rx.at[z], c_rx.at[z], cz_s.at[0], cz_r.at[0], res=zpeer(k) * NY + y)

    for k in range(1, NZ):
        cz(k).start()

    t_rx[owner] = sm[dp]
    drain(t_rx, td_s, td_r, C_H - 1)
    f_rx[z] = total(t_rx).astype(BF16)
    for k in range(1, NZ):
        uz(k).start()

    drain(c_rx, cz_s, cz_r, NZ - 1)
    d_rx[owner] = (total(c_rx) * (1.0 / N)).astype(BF16)

    def ed(k):
        return rc(d_rx.at[owner], d_rx.at[owner], ed_s.at[0], ed_r.at[0], **opeer(k))

    @pl.loop(1, C_H)
    def _(k):
        ed(k).start()

    @pl.loop(0, 4)
    def _(g):
        cols = pl.ds(pl.multiple_of(g * 256, 256), 256)
        main = dot(rp[...], tp[:, cols])
        side = dot(ru[...], tu[:, cols])
        for a in range(2):
            i = 2 * g + a
            ch = jnp.int32(0)
            iv = jnp.zeros((1, C_Z), F32)
            for r in range(ROWS):
                ch = jnp.where(i == r, chain[r], ch)
                iv = jnp.where(i == r, inv_own[r], iv)
            same = chain_col == ch.astype(F32)
            m, s = main[:, a * 128:(a + 1) * 128], side[:, a * 128:(a + 1) * 128]
            out = jnp.where(same, (m + s) * iv, m * (1.0 / (PAIRED + NORM_FLOOR))) + obias_ref[...]
            upd_ref[i] = out.astype(BF16)

    for b in range(PAIRED // 16):
        src = jnp.concatenate([ract[r * SLOTS + b * 16:r * SLOTS + b * 16 + 16, :] for r in range(ROWS)], axis=0)
        agrad_ref[b * 128:(b + 1) * 128, :] = dot(perm0, src, TN).astype(BF16)
    src = jnp.concatenate([ract[r * SLOTS + PAIRED:(r + 1) * SLOTS, :] for r in range(ROWS)], axis=0)
    agrad_ref[PAIRED * ROWS:, :] = dot(pick, src, TN).astype(BF16)

    upd_out = pltpu.make_async_copy(upd_ref, upd_h, out_s.at[0])
    upd_out.start()

    agrad_out = pltpu.make_async_copy(agrad_ref, agrad_h, out_s.at[1])
    agrad_out.start()

    drain(f_rx, uz_s, uz_r, NZ - 1)
    so[dp] = (total(f_rx) * (1.0 / N)).astype(BF16)
    for k in range(1, NDP):
        wd(k).start()

    def sent(ref, sem):
        rc(ref, ref, sem.at[0], sem.at[0], dp=dpeer(1)).wait_send()

    sent(rx.at[0:NZ - 1, :, 0:MAIN], agz_s)
    sent(rx.at[0:2 * NZ, :, 0:MAIN], agy_s)
    sent(v_ref.at[0:2 * NZ, :, 0:HALF], rs1_s)
    sent(v_ref.at[0:2 * NZ, :, 0:MAIN], rs2_s)

    drain(d_rx, ed_s, ed_r, C_H - 1)
    dw_out = pltpu.make_async_copy(d_rx, dw_h, out_s.at[2])
    dw_out.start()
    drain(so, wd_s, wd_r, NDP - 1)
    small_out = pltpu.make_async_copy(so, small_h, out_s.at[3])
    small_out.start()
    for c in (upd_out, agrad_out, dw_out, small_out):
        c.wait()


def finish(
    upd_i, agrad_i, dw_i, small_i,
    upd_h, agrad_h, lw_h, lb_h, rw_h, rb_h, dw_h, ob_h, gain_h, shift_h,
    upd_v, agrad_v, dw_v, small_v, dw_f, lw_f, rw_f, lb_f, rb_f, ob_f, gain_f, shift_f, sem,
):
    copies = []

    def send(src, dst):
        copies.append(pltpu.make_async_copy(src, dst, sem.at[len(copies)]))
        copies[-1].start()

    fetches = [
        pltpu.make_async_copy(src, dst, sem.at[10 + n])
        for n, (src, dst) in enumerate(((dw_i, dw_v), (small_i, small_v), (upd_i, upd_v), (agrad_i, agrad_v)))
    ]
    for f in fetches:
        f.start()
    fetches[0].wait()
    for d in range(NDP):
        for a in range(4):
            dw_f[:, d * 4 + a, :] = dw_v[d * 4 + a].astype(F32)
    send(dw_f, dw_h)
    fetches[2].wait()
    send(upd_v, upd_h)
    fetches[3].wait()
    send(agrad_v, agrad_h)
    fetches[1].wait()

    def tail(c, k):
        return small_v[k].astype(F32)[c * 16 + 8:c * 16 + 9]

    for c, (buf, out) in enumerate(((lw_f, lw_h), (rw_f, rw_h))):
        for half in range(2):
            rows = [small_v[half * 4 + d].astype(F32)[c * 16:c * 16 + 8] for d in range(4)]
            buf[:, half * 128:(half + 1) * 128] = jnp.concatenate(rows, axis=0)
        send(buf, out)
    ob_f[...] = tail(0, 0)
    lb_f[...] = tail(0, 1)[:, 0:C_H]
    rb_f[...] = tail(1, 4)[:, 0:C_H]
    gain_f[...] = jnp.concatenate([tail(1, 0), tail(1, 1)], axis=1)
    shift_f[...] = jnp.concatenate([tail(1, 2), tail(1, 3)], axis=1)
    for buf, out in ((ob_f, ob_h), (lb_f, lb_h), (rb_f, rb_h), (gain_f, gain_h), (shift_f, shift_h)):
        send(buf, out)
    for c in copies:
        c.wait()


def body(
    alignment, chain_ids, row_counts, norm_gain, norm_shift, left_weight, left_bias,
    right_weight, right_bias, out_weight, out_bias, pair_cotangent,
):
    sems = lambda *shape: pltpu.SemaphoreType.DMA(shape)
    vmem = pltpu.VMEM
    scratch = [
        vmem((ROWS, N, C_Z), BF16), vmem((128 * ROWS, C_M), BF16), pltpu.SMEM((1, N), jnp.int32), pltpu.SMEM((1, CHAINS), jnp.int32), vmem((1, N), jnp.int32),
        vmem((128 * ROWS, C_M), BF16), vmem((1, C_M), F32), vmem((1, C_M), F32), vmem((1, C_H), F32),
        vmem((1, C_H), F32), vmem((C_H * C_H, C_Z), BF16), vmem((1, C_Z), F32), vmem((ROWS, N, C_Z), BF16),
        vmem((2 * C_H, C_M), BF16), vmem((C_H * C_H, C_Z), F32), vmem((C_H, C_H * C_Z), BF16),
        vmem((ENT, C_M), F32), vmem((ENT, C_M), BF16), vmem((ENT, 1), F32),
        vmem((ENT, C_H), BF16), vmem((C_H, ENT), BF16), vmem((256, 128), BF16),
        vmem((2048, 1024), BF16), vmem((512, 1024), BF16), vmem((N, 1024), BF16), vmem((N, 1024), BF16),
        vmem((NRES, 16, 1280), BF16), vmem((NRES, 16, 1280), BF16), vmem((N, 2048), BF16), vmem((N, 512), BF16),
        vmem((2, NZ, 16, HALF), BF16), vmem((2, NZ, 16, MAIN), BF16), vmem((NZ - 1, 16, MAIN), BF16), vmem((NZ - 1, 16, MAIN), BF16),
        vmem((NZ - 1, NY, 16, 256), BF16), vmem((NY, 16, 256), F32), vmem((NY, 16, 256), BF16), vmem((NY - 1, 16, 256), BF16),
        vmem((ENT, 4096), BF16),
        vmem((C_H, C_H, C_Z), F32), vmem((C_H, C_H, C_Z), BF16), vmem((C_H - 1, C_H, C_Z), BF16),
        vmem((NZ, C_H, C_Z), BF16), vmem((C_H, C_H, C_Z), BF16),
        vmem((NDP, 32, C_Z), BF16), vmem((C_H, 32, C_Z), BF16), vmem((NZ, 32, C_Z), BF16), vmem((NDP, 32, C_Z), BF16),
        vmem((ENT, C_M), BF16),
        sems(13), sems(4), sems(1), sems(1), sems(1), sems(1), sems(1), sems(1), sems(1), sems(1),
        sems(1), sems(NZ), sems(1), sems(2, NZ), sems(1), sems(1),
        sems(1), sems(2, NZ), sems(1), sems(2, NZ), sems(1), sems(1),
        sems(1), sems(1), sems(1), sems(1), sems(1), sems(1),
        sems(1), sems(1), sems(1), sems(1), sems(1), sems(1),
    ]
    hbm = pl.BlockSpec(memory_space=pltpu.HBM)
    upd, agrad, dw, small = pl.pallas_call(
        kernel,
        out_shape=(
            jax.ShapeDtypeStruct((ROWS, N, C_Z), BF16),
            jax.ShapeDtypeStruct((128 * ROWS, C_M), BF16),
            jax.ShapeDtypeStruct((C_H, C_H, C_Z), BF16),
            jax.ShapeDtypeStruct((NDP, 32, C_Z), BF16),
        ),
        in_specs=[hbm] * 12,
        out_specs=(hbm,) * 4,
        scratch_shapes=scratch,
        compiler_params=pltpu.CompilerParams(
            collective_id=0, has_side_effects=True, vmem_limit_bytes=56 * 1024 * 1024
        ),
    )(
        chain_ids, row_counts, alignment.reshape(128 * ROWS, C_M),
        norm_gain.reshape(1, C_M), norm_shift.reshape(1, C_M), left_weight.T, left_bias.reshape(1, C_H),
        right_weight.T, right_bias.reshape(1, C_H), out_weight, out_bias.reshape(1, C_Z), pair_cotangent[0],
    )
    outs = (
        ((ROWS, N, C_Z), BF16), ((128 * ROWS, C_M), BF16), ((C_H, C_M), F32), ((1, C_H), F32), ((C_H, C_M), F32),
        ((1, C_H), F32), ((C_H, C_H, C_Z), F32), ((1, C_Z), F32), ((1, C_M), F32), ((1, C_M), F32),
    )
    upd, agrad, lw, lb, rw, rb, dw, ob, gain, shift = pl.pallas_call(
        finish,
        out_shape=tuple(jax.ShapeDtypeStruct(*o) for o in outs),
        in_specs=[hbm] * 4,
        out_specs=(hbm,) * 10,
        scratch_shapes=[
            vmem((ROWS, N, C_Z), BF16), vmem((128 * ROWS, C_M), BF16),
            vmem((C_H, C_H, C_Z), BF16), vmem((NDP, 32, C_Z), BF16), vmem((C_H, C_H, C_Z), F32), vmem((C_H, C_M), F32), vmem((C_H, C_M), F32), vmem((1, C_H), F32), vmem((1, C_H), F32),
            vmem((1, C_Z), F32), vmem((1, C_M), F32), vmem((1, C_M), F32), sems(14),
        ],
        compiler_params=pltpu.CompilerParams(vmem_limit_bytes=56 * 1024 * 1024),
    )(upd, agrad, dw, small)
    return (
        upd[None],
        agrad.reshape(1, 128, ROWS, C_M),
        lw.T,
        lb.reshape(C_H),
        rw.T,
        rb.reshape(C_H),
        dw.reshape(C_H * C_H, C_Z),
        ob.reshape(C_Z),
        gain.reshape(C_M),
        shift.reshape(C_M),
    )


def solution(mesh):
    return jax.shard_map(
        body,
        mesh=mesh,
        in_specs=(
            P("dp", None, "res", None), P("dp", None), P("dp", None), P(), P(), P(), P(), P(), P(), P(), P(),
            P("dp", "res", None, None),
        ),
        out_specs=(
            P("dp", "res", None, None), P("dp", None, "res", None), P(), P(), P(), P(), P(), P(), P(), P(),
        ),
        check_vma=False,
    )
```

```python
import functools

import jax
import jax.numpy as jnp
from jax import lax
from jax.experimental import pallas as pl
from jax.experimental.pallas import tpu as pltpu
from jax.sharding import PartitionSpec as P

C_M = 256
C_H = 32
C_Z = 128
PAIRED = 64
UNP = 64
MOST = 16
CHAINS = 12
EPSILON = 1e-05
NORM_FLOOR = 0.001

ROWS = 8
SLOTS = PAIRED + MOST
NY, NZ, NDP = 4, 8, 8
NRES = NY * NZ
N = ROWS * NRES
ENT = ROWS * SLOTS
MAIN = 1024
HALF = MAIN // 2
F32, BF16 = jnp.float32, jnp.bfloat16
MESH = pl.DeviceIdType.MESH

NN = (((1,), (0,)), ((), ()))
NT = (((1,), (1,)), ((), ()))
TN = (((0,), (0,)), ((), ()))


def dot(a, b, dims=NN):
    return lax.dot_general(a, b, dims, preferred_element_type=F32)


def iota(shape, dim):
    return lax.broadcasted_iota(jnp.int32, shape, dim)


def onehot(cond):
    return jnp.where(cond, 1.0, 0.0).astype(BF16)


def kernel(
    chain_h, counts_h, x_h, gain_h, shift_h, lw_h, lb_h, rw_h, rb_h, w_h, ob_h, cot_h,
    upd_h, agrad_h, dw_h, small_h,
    upd_ref, agrad_ref, chain_s, counts_s, chain_v, x_ref, gain_ref, shift_ref, lb_ref, rb_ref, w_ref, obias_ref, cot_ref,
    wt_ref, wf, w2_ref,
    xc, normed, inv_ref, lrow, lt, q_ref, tp, tu, g_ref, gm_ref, v_ref, rx, rp, ru,
    ry1, ry2, vsum, rz, rbz, sbf, sb, rby, ucat, dwf, dws, a_rx, c_rx, d_rx,
    sm, t_rx, f_rx, so, ract, gn_ref,
    in_s, out_s, bgy_s, bgy_r, bgz_s, bgz_r, bsz_s, bsz_r, bsy_s, bsy_r, agz_s, agz_r, agy_s, agy_r, agf_s, agf_r, rs1_s, rs1_r, rs2_s, rs2_r, rsz_s, rsz_r,
    p_s, p_r, cz_s, cz_r, ed_s, ed_r,
    td_s, td_r, uz_s, uz_r, wd_s, wd_r,
):
    me = lax.axis_index("res")
    dp = lax.axis_index("dp")
    z, y = me // NY, me % NY

    def zpeer(k):
        return (z + k) % NZ

    def ypeer(k):
        return (y + k) % NY

    def dpeer(k):
        return (dp + k) % NDP

    def rc(src, dst, ss, rs, **where):
        return pltpu.make_async_remote_copy(
            src_ref=src, dst_ref=dst, send_sem=ss, recv_sem=rs,
            device_id=where, device_id_type=MESH,
        )

    fetches = [
        pltpu.make_async_copy(src, dst, in_s.at[n])
        for n, (src, dst) in enumerate((
            (x_h, x_ref), (chain_h, chain_s), (counts_h, counts_s), (chain_h, chain_v), (gain_h, gain_ref),
            (shift_h, shift_ref), (lw_h, wt_ref.at[0:C_H]), (lb_h, lb_ref), (rw_h, wt_ref.at[C_H:2 * C_H]), (rb_h, rb_ref),
            (w_h, w_ref), (ob_h, obias_ref), (cot_h, cot_ref),
        ))
    ]
    for f in fetches:
        f.start()

    barrier = pltpu.get_barrier_semaphore()

    @pl.loop(1, NRES)
    def _(k):
        pl.semaphore_signal(barrier, inc=1, device_id={"res": (me + k) % NRES}, device_id_type=MESH)

    owner = dp * NY + y

    def opeer(k):
        o = (owner + k) % C_H
        return {"dp": o // NY, "res": z * NY + o % NY}

    @pl.loop(1, NDP)
    def _(k):
        for j in range(NY):
            pl.semaphore_signal(
                barrier, inc=1, device_id={"dp": dpeer(k), "res": z * NY + ypeer(j)}, device_id_type=MESH
            )

    for f in fetches[:10]:
        f.wait()
    rb_col = jnp.transpose(jnp.broadcast_to(rb_ref[...], (8, C_H)))[:, 0:1]

    chain, start, count, base = [], [], [], []
    for r in range(ROWS):
        c = chain_s[0, me * ROWS + r]
        st = jnp.int32(0)
        ct = jnp.int32(0)
        for k in range(CHAINS):
            v = counts_s[0, k]
            st = st + jnp.where(c > k, v, 0)
            ct = ct + jnp.where(c == k, v, 0)
        chain.append(c)
        start.append(st)
        count.append(ct)
        base.append(jnp.minimum(st, UNP - MOST))

    def slot_mask(r, shape, dim):
        s = iota(shape, dim)
        row = s - PAIRED + base[r]
        live = (row >= start[r]) & (row < start[r] + count[r])
        return jnp.where((s < PAIRED) | live, 1.0, 0.0)

    ro, co = iota((128, 128), 0), iota((128, 128), 1)
    perm0 = onehot(co == (ro % 16) * ROWS + ro // 16)
    for b in range(PAIRED // 16):
        part = dot(perm0, x_ref[b * 128:(b + 1) * 128, :])
        for r in range(ROWS):
            xc[r * SLOTS + b * 16:r * SLOTS + b * 16 + 16, :] = part[r * 16:(r + 1) * 16]
    ru_i = iota((128, UNP * ROWS), 0)
    base_rows = jnp.zeros((128, UNP * ROWS), jnp.int32)
    for r in range(ROWS):
        base_rows = jnp.where(ru_i // 16 == r, base[r], base_rows)
    pick = onehot(iota((128, UNP * ROWS), 1) == (base_rows + ru_i % 16) * ROWS + ru_i // 16)
    part = dot(pick, x_ref[PAIRED * ROWS:, :])
    for r in range(ROWS):
        xc[r * SLOTS + PAIRED:(r + 1) * SLOTS, :] = part[r * 16:(r + 1) * 16]

    for r in range(ROWS):
        rows = slice(r * SLOTS, (r + 1) * SLOTS)
        floats = xc[rows, :]
        centred = floats - jnp.mean(floats, axis=-1, keepdims=True)
        inverse = lax.rsqrt(jnp.mean(centred * centred, axis=-1, keepdims=True) + EPSILON)
        scaled = centred * inverse
        nrm = (scaled * gain_ref[...] + shift_ref[...]).astype(BF16)
        xc[rows, :] = scaled
        inv_ref[rows, :] = inverse
        normed[rows, :] = nrm
        left = (dot(nrm, wt_ref[0:C_H, :], NT) + lb_ref[...]) * slot_mask(r, (SLOTS, C_H), 0)
        lrow[rows, :] = left.astype(BF16)
        right = (dot(wt_ref[C_H:, :], nrm, NT) + rb_col) * slot_mask(r, (C_H, SLOTS), 1)
        q_ref[r * C_H:(r + 1) * C_H, 0:SLOTS] = right.astype(BF16)
    re, ce = iota((256, 256), 0), iota((256, 256), 1)
    permq = onehot(ce == (re % 8) * 32 + ((re // 8) % 2) * 16 + re // 16)
    mixed = dot(permq, q_ref[:, 0:SLOTS])
    for p in range(8):
        rx[me, :, p * 128:(p + 1) * 128] = jnp.concatenate(
            [mixed[(2 * p + a) * 16:(2 * p + a + 1) * 16, 0:PAIRED] for a in range(2)], axis=1
        ).astype(BF16)
    for q in range(2):
        rx[me, :, 1024 + q * 128:1024 + (q + 1) * 128] = jnp.concatenate(
            [mixed[(8 * q + a) * 16:(8 * q + a + 1) * 16, PAIRED:SLOTS] for a in range(8)], axis=1
        ).astype(BF16)

    pl.semaphore_wait(barrier, NRES - 1 + NY * (NDP - 1))

    def agz(k):
        part = rx.at[me, :, 0:MAIN]
        return rc(part, part, agz_s.at[0], agz_r.at[k], res=zpeer(k) * NY + y)

    def agy(d, kz):
        slot = ((z - kz + NZ) % NZ) * NY + y
        part = rx.at[slot, :, 0:MAIN]
        return rc(part, part, agy_s.at[0], agy_r.at[d, kz], res=z * NY + ypeer(1 + 2 * d))

    def agf(d, kz):
        slot = ((z - kz + NZ) % NZ) * NY + ypeer(3 - 2 * d)
        part = rx.at[slot, :, d * HALF:(d + 1) * HALF]
        return rc(part, part, agf_s.at[0], agf_r.at[0], res=z * NY + ypeer(1 + 2 * d))

    def bgy(k):
        part = rx.at[me, :, MAIN:]
        return rc(part, part, bgy_s.at[0], bgy_r.at[0], res=z * NY + ypeer(k))

    def bgz(k):
        part = rx.at[pl.ds(z * NY, NY), :, MAIN:]
        return rc(part, part, bgz_s.at[0], bgz_r.at[0], res=zpeer(k) * NY + y)

    def drain(ref, send, recv, count):
        some = ref.at[0:count]
        rc(some, some, send.at[0], recv.at[0], dp=dpeer(1)).wait()

    def spread(*turns):
        for kz in turns:
            if kz:
                agz(kz).wait_recv()
            for d in range(2):
                agy(d, kz).start()

    def forward(*turns):
        for kz in turns:
            for d in range(2):
                agy(d, kz).wait_recv()
                agf(d, kz).start()

    for k in range(1, NY):
        bgy(k).start()
    for k in (1, 7, 2, 6, 3, 5, 4):
        agz(k).start()
    spread(0)

    for f in fetches[10:]:
        f.wait()
    wf[...] = w_ref[...].astype(F32)
    for e in range(C_H):
        w2_ref[:, e * 128:(e + 1) * 128] = wf[pl.ds(e, C_H, stride=C_H), :].astype(BF16)

    lt[...] = jnp.transpose(lrow[...].astype(F32)).astype(BF16)

    def t_step(g):
        h, p = g // 8, g % 8
        t = dot(lrow[...], w2_ref[:, pl.ds(pl.multiple_of(g * 256, 256), 256)]).astype(BF16)
        rowp = pl.multiple_of((p * 2 + h) * 128, 128)
        rowu = pl.multiple_of(((p // 4) * 2 + h) * 128 + (p % 4) * 32, 32)
        for i in range(ROWS):
            for a in range(2):
                tp[pl.ds(rowp + a * 64, 64), i * 128:(i + 1) * 128] = t[i * SLOTS:i * SLOTS + PAIRED, a * 128:(a + 1) * 128]
                tu[pl.ds(rowu + a * 16, 16), i * 128:(i + 1) * 128] = t[i * SLOTS + PAIRED:(i + 1) * SLOTS, a * 128:(a + 1) * 128]

    pl.loop(0, 12, unroll=2)(t_step)
    spread(1, 7)
    pl.loop(12, 16, unroll=2)(t_step)
    spread(2, 6)
    forward(0)
    chain_col = jnp.transpose(jnp.broadcast_to(chain_v[...].astype(F32), (128, N)))
    obg = jnp.zeros((8, C_Z), F32)
    inv_own = []
    for i in range(ROWS):
        same = chain_col == chain[i].astype(F32)
        cntf = jnp.full((8, C_Z), count[i].astype(F32))
        inv_own.append((1.0 / (PAIRED + cntf + NORM_FLOOR))[0:1, :])
        raw = cot_ref[i].astype(F32)
        obg = obg + jnp.sum(raw.reshape(N // 8, 8, C_Z), axis=0)
        g = (raw * jnp.where(same, inv_own[i], 1.0 / (PAIRED + NORM_FLOOR))).astype(BF16)
        g_ref[:, i * 128:(i + 1) * 128] = g
        gm_ref[:, i * 128:(i + 1) * 128] = jnp.where(same, g.astype(F32), 0.0).astype(BF16)

    spread(3, 5)
    drain(rx.at[:, :, MAIN:], bgy_s, bgy_r, NY - 1)
    for k in range(1, NZ):
        bgz(k).start()
    forward(1, 7)

    def put_v(v, lane):
        both = jnp.concatenate(
            [v[:, 0:128].reshape(NRES, ROWS, 128), v[:, 128:256].reshape(NRES, ROWS, 128)], axis=1
        )
        v_ref[:, :, pl.ds(lane, 128)] = both.astype(BF16)

    def v_step(p):
        put_v(dot(g_ref[...], tp[pl.ds(pl.multiple_of(p * 256, 256), 256), :], NT), pl.multiple_of(p * 128, 128))

    def rs1(d, kz):
        dst = zpeer(kz) * NY + ypeer(2)
        src = v_ref.at[dst, :, d * HALF:(d + 1) * HALF]
        return rc(src, ry1.at[d, kz], rs1_s.at[0], rs1_r.at[d, kz], res=z * NY + ypeer(3 - 2 * d))

    def rs2(d, kz):
        dst = zpeer(kz) * NY + ypeer(3 - 2 * d)
        return rc(v_ref.at[dst, :, 0:MAIN], ry2.at[d, kz], rs2_s.at[0], rs2_r.at[d, kz], res=z * NY + ypeer(3 - 2 * d))

    def rsz(k):
        return rc(vsum.at[k - 1], rz.at[k - 1], rsz_s.at[0], rsz_r.at[0], res=zpeer(k) * NY + y)

    def bsz(k):
        src = v_ref.at[pl.ds(zpeer(k) * NY, NY), :, MAIN:]
        return rc(src, rbz.at[k - 1], bsz_s.at[0], bsz_r.at[0], res=zpeer(k) * NY + y)

    def bsy(k):
        return rc(sb.at[ypeer(k)], rby.at[k - 1], bsy_s.at[0], bsy_r.at[0], res=z * NY + ypeer(k))

    def side_sums():
        drain(rbz, bsz_s, bsz_r, NZ - 1)
        sbf[...] = v_ref[pl.ds(z * NY, NY), :, MAIN:].astype(F32) + jnp.sum(rbz[...].astype(F32), axis=0)
        sb[...] = sbf[...].astype(BF16)
        for k in range(1, NY):
            bsy(k).start()

    def second(*turns):
        for kz in turns:
            for d in range(2):
                slab = zpeer(kz) * NY + ypeer(3 - 2 * d)
                lanes = slice(d * HALF, (d + 1) * HALF)
                rs1(d, kz).wait_recv()
                v_ref[slab, :, lanes] = (v_ref[slab, :, lanes].astype(F32) + ry1[d, kz].astype(F32)).astype(BF16)

    def pass_on(*turns):
        for kz in turns:
            for d in range(2):
                rs2(d, kz).start()

    def third(*turns):
        for kz in turns:
            total = v_ref[zpeer(kz) * NY + y, :, 0:MAIN].astype(F32)
            for d in range(2):
                rs2(d, kz).wait_recv()
                total = total + ry2[d, kz].astype(F32)
            if kz:
                vsum[kz - 1] = total.astype(BF16)
                rsz(kz).start()
        return total

    def first(*turns):
        for kz in turns:
            for d in range(2):
                rs1(d, kz).start()

    for q in range(2):
        put_v(dot(gm_ref[...], tu[q * 256:(q + 1) * 256, :], NT), MAIN + q * 128)
    pl.loop(0, 4, unroll=2)(v_step)
    spread(4)
    forward(2, 6)
    pl.loop(4, 8, unroll=2)(v_step)
    forward(3)
    forward(5)
    first(4, 3, 5, 2, 6)
    forward(4)
    first(1, 7, 0)
    for k in range(1, NZ):
        bsz(k).start()
    second(4, 3, 5, 2)
    pass_on(4, 3, 5, 2)
    second(6)
    pass_on(6)
    second(1, 7, 0)
    drain(rx.at[:, :, 0:HALF], agf_s, agf_r, 2 * NZ)
    pass_on(1, 7, 0)
    drain(rx.at[:, :, MAIN:], bgz_s, bgz_r, NY * (NZ - 1))

    @pl.loop(0, NRES // 2)
    def _(d):
        a, b = rx[2 * d].astype(F32), rx[2 * d + 1].astype(F32)
        rows = pl.ds(pl.multiple_of(d * 16, 16), 16)
        for h in range(2):
            both = jnp.concatenate([a[h * 8:h * 8 + 8], b[h * 8:h * 8 + 8]], axis=0).astype(BF16)
            for p in range(8):
                rp[rows, p * 256 + h * 128:p * 256 + (h + 1) * 128] = both[:, p * 128:(p + 1) * 128]
            for q in range(2):
                ru[rows, q * 256 + h * 128:q * 256 + (h + 1) * 128] = both[:, 1024 + q * 128:1024 + (q + 1) * 128]

    def u_step(p):
        u = dot(rp[:, pl.ds(pl.multiple_of(p * 256, 256), 256)], g_ref[...], TN).astype(BF16)
        for h in range(2):
            for a in range(2):
                lane = pl.multiple_of((h * 16 + 2 * p + a) * 128, 128)
                for i in range(ROWS):
                    ucat[i * SLOTS:i * SLOTS + PAIRED, pl.ds(lane, 128)] = u[(h * 2 + a) * 64:(h * 2 + a + 1) * 64, i * 128:(i + 1) * 128]

    def u_side(q):
        u = dot(ru[:, q * 256:(q + 1) * 256], gm_ref[...], TN).astype(BF16)
        for h in range(2):
            for a in range(8):
                lane = (h * 16 + q * 8 + a) * 128
                for i in range(ROWS):
                    ucat[i * SLOTS + PAIRED:(i + 1) * SLOTS, lane:lane + 128] = u[(h * 8 + a) * 16:(h * 8 + a + 1) * 16, i * 128:(i + 1) * 128]

    def pd(e):
        k = (e - owner + C_H) % C_H
        return rc(dws.at[e], a_rx.at[k - 1], p_s.at[0], p_r.at[0], **opeer(k))

    def dw_step(g):
        dw = dot(lt[...], ucat[:, g * 256:(g + 1) * 256])
        for a in range(2):
            part = dw[:, a * 128:(a + 1) * 128]
            dwf[2 * g + a] = part
            dws[2 * g + a] = part.astype(BF16)

    def dw_send(first):
        @pl.loop(first, first + 8)
        def _(e):
            @pl.when(e != owner)
            def _():
                pd(e).start()

    pl.loop(0, 4, unroll=2)(u_step)
    u_side(0)
    for g in (0, 1, 2, 3, 8, 9, 10, 11):
        dw_step(g)
    dw_send(0)
    dw_send(16)
    third(4, 3)
    pl.loop(4, 8, unroll=2)(u_step)
    u_side(1)
    third(5, 2)
    side_sums()
    for g in (4, 5, 6, 7, 12, 13, 14, 15):
        dw_step(g)
    dw_send(8)
    dw_send(24)
    own = third(6, 1, 7, 0)

    def left_step(k, acc):
        cols = pl.ds(pl.multiple_of(k * 512, 512), 512)
        return acc + dot(ucat[:, cols], w2_ref[:, cols], NT)

    lgrad = lax.fori_loop(0, 8, left_step, jnp.zeros((ENT, C_H), F32), unroll=2)

    def td(k):
        slot = (owner + k) % C_H // NY
        return rc(sm.at[slot], t_rx.at[owner], td_s.at[0], td_r.at[0], **opeer(k))

    def uz(k):
        return rc(f_rx.at[z], f_rx.at[z], uz_s.at[0], uz_r.at[0], res=zpeer(k) * NY + y)

    def wd(k):
        return rc(so.at[dp], so.at[dp], wd_s.at[0], wd_r.at[0], dp=dpeer(k))

    rows8 = iota((8, C_Z), 0)

    def small_put(c, gw, tail_rows):
        tail = jnp.zeros((8, C_Z), F32)
        for k, row in enumerate(tail_rows):
            tail = jnp.where(rows8 == k, row, tail)
        main = jnp.concatenate([gw[:, 0:128], gw[:, 128:256]], axis=0).reshape(8, 8, C_Z)
        tails = jnp.broadcast_to(tail.reshape(8, 1, C_Z), (8, 8, C_Z))
        sm[:, c * 16:(c + 1) * 16, :] = jnp.concatenate([main, tails], axis=1).astype(BF16)

    def total(ref):
        return jnp.sum(ref[...].astype(F32), axis=0)

    gw_l = jnp.zeros((C_H, C_M), F32)
    gb_l = jnp.zeros((1, C_H), F32)
    for r in range(ROWS):
        rows = slice(r * SLOTS, (r + 1) * SLOTS)
        lact = (lgrad[rows] * slot_mask(r, (SLOTS, C_H), 0)).astype(BF16)
        gw_l = gw_l + dot(lact, normed[rows, :], TN)
        gb_l = gb_l + jnp.sum(lact.astype(F32), axis=0, keepdims=True)
        gn_ref[rows, :] = dot(lact, wt_ref[0:C_H, :])
    small_put(0, gw_l, (
        jnp.sum(obg, axis=0, keepdims=True),
        jnp.concatenate([gb_l, jnp.zeros((1, 96), F32)], axis=1),
    ))

    drain(rz, rsz_s, rsz_r, NZ - 1)
    drain(rby, bsy_s, bsy_r, NY - 1)
    own = jnp.concatenate(
        [own + jnp.sum(rz[...].astype(F32), axis=0), sbf[y] + jnp.sum(rby[...].astype(F32), axis=0)], axis=1
    )
    tiles = []
    for e in range(16):
        tiles.append(jnp.concatenate([own[:, e * 64:(e + 1) * 64], own[:, 1024 + e * 16:1024 + (e + 1) * 16]], axis=1))
    back = dot(permq, jnp.concatenate(tiles, axis=0).astype(BF16), TN)

    gw_r = jnp.zeros((C_H, C_M), F32)
    gb_r = jnp.zeros((C_H, 1), F32)
    gain_g = jnp.zeros((1, C_M), F32)
    shift_g = jnp.zeros((1, C_M), F32)
    for r in range(ROWS):
        rows = slice(r * SLOTS, (r + 1) * SLOTS)
        ract_t = (back[r * C_H:(r + 1) * C_H, :] * slot_mask(r, (C_H, SLOTS), 1)).astype(BF16)
        gw_r = gw_r + dot(ract_t, normed[rows, :])
        gb_r = gb_r + jnp.sum(ract_t.astype(F32), axis=1, keepdims=True)
        gn = gn_ref[rows, :] + dot(ract_t, wt_ref[C_H:, :], TN)
        gn_ref[rows, :] = gn
        gain_g = gain_g + jnp.sum(gn * xc[rows, :], axis=0, keepdims=True)
        shift_g = shift_g + jnp.sum(gn, axis=0, keepdims=True)
    gbr_row = jnp.transpose(jnp.broadcast_to(gb_r, (C_H, 128)))[0:1, :]
    small_put(1, gw_r, (
        gain_g[:, 0:128], gain_g[:, 128:256], shift_g[:, 0:128], shift_g[:, 128:256],
        jnp.concatenate([gbr_row, jnp.zeros((1, 96), F32)], axis=1),
    ))

    @pl.loop(1, C_H)
    def _(k):
        td(k).start()

    drain(a_rx, p_s, p_r, C_H - 1)

    def add(k, t):
        return t + a_rx[k].astype(F32)

    c_rx[z] = lax.fori_loop(0, C_H - 1, add, dwf[owner], unroll=True).astype(BF16)

    def cz(k):
        return rc(c_rx.at[z], c_rx.at[z], cz_s.at[0], cz_r.at[0], res=zpeer(k) * NY + y)

    for k in range(1, NZ):
        cz(k).start()

    t_rx[owner] = sm[dp]
    drain(t_rx, td_s, td_r, C_H - 1)
    f_rx[z] = total(t_rx).astype(BF16)
    for k in range(1, NZ):
        uz(k).start()

    drain(c_rx, cz_s, cz_r, NZ - 1)
    d_rx[owner] = (total(c_rx) * (1.0 / N)).astype(BF16)

    def ed(k):
        return rc(d_rx.at[owner], d_rx.at[owner], ed_s.at[0], ed_r.at[0], **opeer(k))

    @pl.loop(1, C_H)
    def _(k):
        ed(k).start()

    @pl.loop(0, 4)
    def _(g):
        cols = pl.ds(pl.multiple_of(g * 256, 256), 256)
        main = dot(rp[...], tp[:, cols])
        side = dot(ru[...], tu[:, cols])
        for a in range(2):
            i = 2 * g + a
            ch = jnp.int32(0)
            iv = jnp.zeros((1, C_Z), F32)
            for r in range(ROWS):
                ch = jnp.where(i == r, chain[r], ch)
                iv = jnp.where(i == r, inv_own[r], iv)
            same = chain_col == ch.astype(F32)
            m, s = main[:, a * 128:(a + 1) * 128], side[:, a * 128:(a + 1) * 128]
            out = jnp.where(same, (m + s) * iv, m * (1.0 / (PAIRED + NORM_FLOOR))) + obias_ref[...]
            upd_ref[i] = out.astype(BF16)

    for r in range(ROWS):
        rows = slice(r * SLOTS, (r + 1) * SLOTS)
        scaled = xc[rows, :]
        gg = gn_ref[rows, :] * gain_ref[...]
        mean_g = jnp.mean(gg, axis=-1, keepdims=True)
        mean_p = jnp.mean(gg * scaled, axis=-1, keepdims=True)
        ract[rows, :] = (inv_ref[rows, :] * (gg - mean_g - scaled * mean_p)).astype(BF16)
    for b in range(PAIRED // 16):
        src = jnp.concatenate([ract[r * SLOTS + b * 16:r * SLOTS + b * 16 + 16, :] for r in range(ROWS)], axis=0)
        agrad_ref[b * 128:(b + 1) * 128, :] = dot(perm0, src, TN).astype(BF16)
    src = jnp.concatenate([ract[r * SLOTS + PAIRED:(r + 1) * SLOTS, :] for r in range(ROWS)], axis=0)
    agrad_ref[PAIRED * ROWS:, :] = dot(pick, src, TN).astype(BF16)

    upd_out = pltpu.make_async_copy(upd_ref, upd_h, out_s.at[0])
    upd_out.start()

    agrad_out = pltpu.make_async_copy(agrad_ref, agrad_h, out_s.at[1])
    agrad_out.start()

    drain(f_rx, uz_s, uz_r, NZ - 1)
    so[dp] = (total(f_rx) * (1.0 / N)).astype(BF16)
    for k in range(1, NDP):
        wd(k).start()

    def sent(ref, sem):
        rc(ref, ref, sem.at[0], sem.at[0], dp=dpeer(1)).wait_send()

    sent(rx.at[0:NZ - 1, :, 0:MAIN], agz_s)
    sent(rx.at[0:2 * NZ, :, 0:MAIN], agy_s)
    sent(v_ref.at[0:2 * NZ, :, 0:HALF], rs1_s)
    sent(v_ref.at[0:2 * NZ, :, 0:MAIN], rs2_s)

    drain(d_rx, ed_s, ed_r, C_H - 1)
    dw_out = pltpu.make_async_copy(d_rx, dw_h, out_s.at[2])
    dw_out.start()
    drain(so, wd_s, wd_r, NDP - 1)
    small_out = pltpu.make_async_copy(so, small_h, out_s.at[3])
    small_out.start()
    for c in (upd_out, agrad_out, dw_out, small_out):
        c.wait()


def finish(
    upd_i, agrad_i, dw_i, small_i,
    upd_h, agrad_h, lw_h, lb_h, rw_h, rb_h, dw_h, ob_h, gain_h, shift_h,
    upd_v, agrad_v, dw_v, small_v, dw_f, lw_f, rw_f, lb_f, rb_f, ob_f, gain_f, shift_f, sem,
):
    copies = []

    def send(src, dst):
        copies.append(pltpu.make_async_copy(src, dst, sem.at[len(copies)]))
        copies[-1].start()

    fetches = [
        pltpu.make_async_copy(src, dst, sem.at[10 + n])
        for n, (src, dst) in enumerate(((dw_i, dw_v), (small_i, small_v), (upd_i, upd_v), (agrad_i, agrad_v)))
    ]
    for f in fetches:
        f.start()
    fetches[0].wait()
    for d in range(NDP):
        for a in range(4):
            dw_f[:, d * 4 + a, :] = dw_v[d * 4 + a].astype(F32)
    send(dw_f, dw_h)
    fetches[2].wait()
    send(upd_v, upd_h)
    fetches[3].wait()
    send(agrad_v, agrad_h)
    fetches[1].wait()

    def tail(c, k):
        return small_v[k].astype(F32)[c * 16 + 8:c * 16 + 9]

    for c, (buf, out) in enumerate(((lw_f, lw_h), (rw_f, rw_h))):
        for half in range(2):
            rows = [small_v[half * 4 + d].astype(F32)[c * 16:c * 16 + 8] for d in range(4)]
            buf[:, half * 128:(half + 1) * 128] = jnp.concatenate(rows, axis=0)
        send(buf, out)
    ob_f[...] = tail(0, 0)
    lb_f[...] = tail(0, 1)[:, 0:C_H]
    rb_f[...] = tail(1, 4)[:, 0:C_H]
    gain_f[...] = jnp.concatenate([tail(1, 0), tail(1, 1)], axis=1)
    shift_f[...] = jnp.concatenate([tail(1, 2), tail(1, 3)], axis=1)
    for buf, out in ((ob_f, ob_h), (lb_f, lb_h), (rb_f, rb_h), (gain_f, gain_h), (shift_f, shift_h)):
        send(buf, out)
    for c in copies:
        c.wait()


def body(
    alignment, chain_ids, row_counts, norm_gain, norm_shift, left_weight, left_bias,
    right_weight, right_bias, out_weight, out_bias, pair_cotangent,
):
    sems = lambda *shape: pltpu.SemaphoreType.DMA(shape)
    vmem = pltpu.VMEM
    scratch = [
        vmem((ROWS, N, C_Z), BF16), vmem((128 * ROWS, C_M), BF16), pltpu.SMEM((1, N), jnp.int32), pltpu.SMEM((1, CHAINS), jnp.int32), vmem((1, N), jnp.int32),
        vmem((128 * ROWS, C_M), BF16), vmem((1, C_M), F32), vmem((1, C_M), F32), vmem((1, C_H), F32),
        vmem((1, C_H), F32), vmem((C_H * C_H, C_Z), BF16), vmem((1, C_Z), F32), vmem((ROWS, N, C_Z), BF16),
        vmem((2 * C_H, C_M), BF16), vmem((C_H * C_H, C_Z), F32), vmem((C_H, C_H * C_Z), BF16),
        vmem((ENT, C_M), F32), vmem((ENT, C_M), BF16), vmem((ENT, 1), F32),
        vmem((ENT, C_H), BF16), vmem((C_H, ENT), BF16), vmem((256, 128), BF16),
        vmem((2048, 1024), BF16), vmem((512, 1024), BF16), vmem((N, 1024), BF16), vmem((N, 1024), BF16),
        vmem((NRES, 16, 1280), BF16), vmem((NRES, 16, 1280), BF16), vmem((N, 2048), BF16), vmem((N, 512), BF16),
        vmem((2, NZ, 16, HALF), BF16), vmem((2, NZ, 16, MAIN), BF16), vmem((NZ - 1, 16, MAIN), BF16), vmem((NZ - 1, 16, MAIN), BF16),
        vmem((NZ - 1, NY, 16, 256), BF16), vmem((NY, 16, 256), F32), vmem((NY, 16, 256), BF16), vmem((NY - 1, 16, 256), BF16),
        vmem((ENT, 4096), BF16),
        vmem((C_H, C_H, C_Z), F32), vmem((C_H, C_H, C_Z), BF16), vmem((C_H - 1, C_H, C_Z), BF16),
        vmem((NZ, C_H, C_Z), BF16), vmem((C_H, C_H, C_Z), BF16),
        vmem((NDP, 32, C_Z), BF16), vmem((C_H, 32, C_Z), BF16), vmem((NZ, 32, C_Z), BF16), vmem((NDP, 32, C_Z), BF16),
        vmem((ENT, C_M), BF16), vmem((ENT, C_M), F32),
        sems(13), sems(4), sems(1), sems(1), sems(1), sems(1), sems(1), sems(1), sems(1), sems(1),
        sems(1), sems(NZ), sems(1), sems(2, NZ), sems(1), sems(1),
        sems(1), sems(2, NZ), sems(1), sems(2, NZ), sems(1), sems(1),
        sems(1), sems(1), sems(1), sems(1), sems(1), sems(1),
        sems(1), sems(1), sems(1), sems(1), sems(1), sems(1),
    ]
    hbm = pl.BlockSpec(memory_space=pltpu.HBM)
    upd, agrad, dw, small = pl.pallas_call(
        kernel,
        out_shape=(
            jax.ShapeDtypeStruct((ROWS, N, C_Z), BF16),
            jax.ShapeDtypeStruct((128 * ROWS, C_M), BF16),
            jax.ShapeDtypeStruct((C_H, C_H, C_Z), BF16),
            jax.ShapeDtypeStruct((NDP, 32, C_Z), BF16),
        ),
        in_specs=[hbm] * 12,
        out_specs=(hbm,) * 4,
        scratch_shapes=scratch,
        compiler_params=pltpu.CompilerParams(
            collective_id=0, has_side_effects=True, vmem_limit_bytes=56 * 1024 * 1024
        ),
    )(
        chain_ids, row_counts, alignment.reshape(128 * ROWS, C_M),
        norm_gain.reshape(1, C_M), norm_shift.reshape(1, C_M), left_weight.T, left_bias.reshape(1, C_H),
        right_weight.T, right_bias.reshape(1, C_H), out_weight, out_bias.reshape(1, C_Z), pair_cotangent[0],
    )
    outs = (
        ((ROWS, N, C_Z), BF16), ((128 * ROWS, C_M), BF16), ((C_H, C_M), F32), ((1, C_H), F32), ((C_H, C_M), F32),
        ((1, C_H), F32), ((C_H, C_H, C_Z), F32), ((1, C_Z), F32), ((1, C_M), F32), ((1, C_M), F32),
    )
    upd, agrad, lw, lb, rw, rb, dw, ob, gain, shift = pl.pallas_call(
        finish,
        out_shape=tuple(jax.ShapeDtypeStruct(*o) for o in outs),
        in_specs=[hbm] * 4,
        out_specs=(hbm,) * 10,
        scratch_shapes=[
            vmem((ROWS, N, C_Z), BF16), vmem((128 * ROWS, C_M), BF16),
            vmem((C_H, C_H, C_Z), BF16), vmem((NDP, 32, C_Z), BF16), vmem((C_H, C_H, C_Z), F32), vmem((C_H, C_M), F32), vmem((C_H, C_M), F32), vmem((1, C_H), F32), vmem((1, C_H), F32),
            vmem((1, C_Z), F32), vmem((1, C_M), F32), vmem((1, C_M), F32), sems(14),
        ],
        compiler_params=pltpu.CompilerParams(vmem_limit_bytes=56 * 1024 * 1024),
    )(upd, agrad, dw, small)
    return (
        upd[None],
        agrad.reshape(1, 128, ROWS, C_M),
        lw.T,
        lb.reshape(C_H),
        rw.T,
        rb.reshape(C_H),
        dw.reshape(C_H * C_H, C_Z),
        ob.reshape(C_Z),
        gain.reshape(C_M),
        shift.reshape(C_M),
    )


def solution(mesh):
    return jax.shard_map(
        body,
        mesh=mesh,
        in_specs=(
            P("dp", None, "res", None), P("dp", None), P("dp", None), P(), P(), P(), P(), P(), P(), P(), P(),
            P("dp", "res", None, None),
        ),
        out_specs=(
            P("dp", "res", None, None), P("dp", None, "res", None), P(), P(), P(), P(), P(), P(), P(), P(),
        ),
        check_vma=False,
    )
```

```python
import functools

import jax
import jax.numpy as jnp
from jax import lax
from jax.experimental import pallas as pl
from jax.experimental.pallas import tpu as pltpu
from jax.sharding import PartitionSpec as P

C_M = 256
C_H = 32
C_Z = 128
PAIRED = 64
UNP = 64
MOST = 16
CHAINS = 12
EPSILON = 1e-05
NORM_FLOOR = 0.001

ROWS = 8
SLOTS = PAIRED + MOST
NY, NZ, NDP = 4, 8, 8
NRES = NY * NZ
N = ROWS * NRES
ENT = ROWS * SLOTS
MAIN = 1024
HALF = MAIN // 2
F32, BF16 = jnp.float32, jnp.bfloat16
MESH = pl.DeviceIdType.MESH

NN = (((1,), (0,)), ((), ()))
NT = (((1,), (1,)), ((), ()))
TN = (((0,), (0,)), ((), ()))


def dot(a, b, dims=NN):
    return lax.dot_general(a, b, dims, preferred_element_type=F32)


def iota(shape, dim):
    return lax.broadcasted_iota(jnp.int32, shape, dim)


def onehot(cond):
    return jnp.where(cond, 1.0, 0.0).astype(BF16)


def kernel(
    chain_h, counts_h, x_h, gain_h, shift_h, lw_h, lb_h, rw_h, rb_h, w_h, ob_h, cot_h,
    upd_h, agrad_h, dw_h, small_h,
    upd_ref, agrad_ref, chain_s, counts_s, chain_v, x_ref, gain_ref, shift_ref, lb_ref, rb_ref, w_ref, obias_ref, cot_ref,
    wt_ref, wf, w2_ref,
    xc, normed, inv_ref, lrow, lt, q_ref, tp, tu, g_ref, gm_ref, v_ref, rx, rp, ru,
    ry1, ry2, vsum, rz, rbz, sbf, sb, rby, ucat, dwf, dws, a_rx, c_rx, d_rx,
    sm, t_rx, f_rx, so, ract, gn_ref,
    in_s, out_s, bgy_s, bgy_r, bgz_s, bgz_r, bsz_s, bsz_r, bsy_s, bsy_r, agz_s, agz_r, agy_s, agy_r, agf_s, agf_r, rs1_s, rs1_r, rs2_s, rs2_r, rsz_s, rsz_r,
    p_s, p_r, cz_s, cz_r, ed_s, ed_r,
    td_s, td_r, uz_s, uz_r, wd_s, wd_r,
):
    me = lax.axis_index("res")
    dp = lax.axis_index("dp")
    z, y = me // NY, me % NY

    def zpeer(k):
        return (z + k) % NZ

    def ypeer(k):
        return (y + k) % NY

    def dpeer(k):
        return (dp + k) % NDP

    def rc(src, dst, ss, rs, **where):
        return pltpu.make_async_remote_copy(
            src_ref=src, dst_ref=dst, send_sem=ss, recv_sem=rs,
            device_id=where, device_id_type=MESH,
        )

    fetches = [
        pltpu.make_async_copy(src, dst, in_s.at[n])
        for n, (src, dst) in enumerate((
            (x_h, x_ref), (chain_h, chain_s), (counts_h, counts_s), (chain_h, chain_v), (gain_h, gain_ref),
            (shift_h, shift_ref), (lw_h, wt_ref.at[0:C_H]), (lb_h, lb_ref), (rw_h, wt_ref.at[C_H:2 * C_H]), (rb_h, rb_ref),
            (w_h, w_ref), (ob_h, obias_ref), (cot_h, cot_ref),
        ))
    ]
    for f in fetches:
        f.start()

    barrier = pltpu.get_barrier_semaphore()

    @pl.loop(1, NRES)
    def _(k):
        pl.semaphore_signal(barrier, inc=1, device_id={"res": (me + k) % NRES}, device_id_type=MESH)

    owner = dp * NY + y

    def opeer(k):
        o = (owner + k) % C_H
        return {"dp": o // NY, "res": z * NY + o % NY}

    @pl.loop(1, NDP)
    def _(k):
        for j in range(NY):
            pl.semaphore_signal(
                barrier, inc=1, device_id={"dp": dpeer(k), "res": z * NY + ypeer(j)}, device_id_type=MESH
            )

    for f in fetches[:10]:
        f.wait()
    rb_col = jnp.transpose(jnp.broadcast_to(rb_ref[...], (8, C_H)))[:, 0:1]

    chain, start, count, base = [], [], [], []
    for r in range(ROWS):
        c = chain_s[0, me * ROWS + r]
        st = jnp.int32(0)
        ct = jnp.int32(0)
        for k in range(CHAINS):
            v = counts_s[0, k]
            st = st + jnp.where(c > k, v, 0)
            ct = ct + jnp.where(c == k, v, 0)
        chain.append(c)
        start.append(st)
        count.append(ct)
        base.append(jnp.minimum(st, UNP - MOST))

    def slot_mask(r, shape, dim):
        s = iota(shape, dim)
        row = s - PAIRED + base[r]
        live = (row >= start[r]) & (row < start[r] + count[r])
        return jnp.where((s < PAIRED) | live, 1.0, 0.0)

    ro, co = iota((128, 128), 0), iota((128, 128), 1)
    perm0 = onehot(co == (ro % 16) * ROWS + ro // 16)
    for b in range(PAIRED // 16):
        part = dot(perm0, x_ref[b * 128:(b + 1) * 128, :])
        for r in range(ROWS):
            xc[r * SLOTS + b * 16:r * SLOTS + b * 16 + 16, :] = part[r * 16:(r + 1) * 16]
    ru_i = iota((128, UNP * ROWS), 0)
    base_rows = jnp.zeros((128, UNP * ROWS), jnp.int32)
    for r in range(ROWS):
        base_rows = jnp.where(ru_i // 16 == r, base[r], base_rows)
    pick = onehot(iota((128, UNP * ROWS), 1) == (base_rows + ru_i % 16) * ROWS + ru_i // 16)
    part = dot(pick, x_ref[PAIRED * ROWS:, :])
    for r in range(ROWS):
        xc[r * SLOTS + PAIRED:(r + 1) * SLOTS, :] = part[r * 16:(r + 1) * 16]

    for r in range(ROWS):
        rows = slice(r * SLOTS, (r + 1) * SLOTS)
        floats = xc[rows, :]
        centred = floats - jnp.mean(floats, axis=-1, keepdims=True)
        inverse = lax.rsqrt(jnp.mean(centred * centred, axis=-1, keepdims=True) + EPSILON)
        scaled = centred * inverse
        nrm = (scaled * gain_ref[...] + shift_ref[...]).astype(BF16)
        xc[rows, :] = scaled
        inv_ref[rows, :] = inverse
        normed[rows, :] = nrm
        left = (dot(nrm, wt_ref[0:C_H, :], NT) + lb_ref[...]) * slot_mask(r, (SLOTS, C_H), 0)
        lrow[rows, :] = left.astype(BF16)
        right = (dot(wt_ref[C_H:, :], nrm, NT) + rb_col) * slot_mask(r, (C_H, SLOTS), 1)
        q_ref[r * C_H:(r + 1) * C_H, 0:SLOTS] = right.astype(BF16)
    re, ce = iota((256, 256), 0), iota((256, 256), 1)
    permq = onehot(ce == (re % 8) * 32 + ((re // 8) % 2) * 16 + re // 16)
    mixed = dot(permq, q_ref[:, 0:SLOTS])
    for p in range(8):
        rx[me, :, p * 128:(p + 1) * 128] = jnp.concatenate(
            [mixed[(2 * p + a) * 16:(2 * p + a + 1) * 16, 0:PAIRED] for a in range(2)], axis=1
        ).astype(BF16)
    for q in range(2):
        rx[me, :, 1024 + q * 128:1024 + (q + 1) * 128] = jnp.concatenate(
            [mixed[(8 * q + a) * 16:(8 * q + a + 1) * 16, PAIRED:SLOTS] for a in range(8)], axis=1
        ).astype(BF16)

    pl.semaphore_wait(barrier, NRES - 1 + NY * (NDP - 1))

    def agz(k):
        part = rx.at[me, :, 0:MAIN]
        return rc(part, part, agz_s.at[0], agz_r.at[k], res=zpeer(k) * NY + y)

    def agy(d, kz):
        slot = ((z - kz + NZ) % NZ) * NY + y
        part = rx.at[slot, :, 0:MAIN]
        return rc(part, part, agy_s.at[0], agy_r.at[d, kz], res=z * NY + ypeer(1 + 2 * d))

    def agf(d, kz):
        slot = ((z - kz + NZ) % NZ) * NY + ypeer(3 - 2 * d)
        part = rx.at[slot, :, d * HALF:(d + 1) * HALF]
        return rc(part, part, agf_s.at[0], agf_r.at[0], res=z * NY + ypeer(1 + 2 * d))

    def bgy(k):
        part = rx.at[me, :, MAIN:]
        return rc(part, part, bgy_s.at[0], bgy_r.at[0], res=z * NY + ypeer(k))

    def bgz(k):
        part = rx.at[pl.ds(z * NY, NY), :, MAIN:]
        return rc(part, part, bgz_s.at[0], bgz_r.at[0], res=zpeer(k) * NY + y)

    def drain(ref, send, recv, count):
        some = ref.at[0:count]
        rc(some, some, send.at[0], recv.at[0], dp=dpeer(1)).wait()

    def spread(*turns):
        for kz in turns:
            if kz:
                agz(kz).wait_recv()
            for d in range(2):
                agy(d, kz).start()

    def forward(*turns):
        for kz in turns:
            for d in range(2):
                agy(d, kz).wait_recv()
                agf(d, kz).start()

    for k in range(1, NY):
        bgy(k).start()
    for k in (1, 7, 2, 6, 3, 5, 4):
        agz(k).start()
    spread(0)

    for f in fetches[10:]:
        f.wait()
    wf[...] = w_ref[...].astype(F32)
    for e in range(C_H):
        w2_ref[:, e * 128:(e + 1) * 128] = wf[pl.ds(e, C_H, stride=C_H), :].astype(BF16)

    lt[...] = jnp.transpose(lrow[...].astype(F32)).astype(BF16)

    def t_step(g):
        h, p = g // 8, g % 8
        t = dot(lrow[...], w2_ref[:, pl.ds(pl.multiple_of(g * 256, 256), 256)]).astype(BF16)
        rowp = pl.multiple_of((p * 2 + h) * 128, 128)
        rowu = pl.multiple_of(((p // 4) * 2 + h) * 128 + (p % 4) * 32, 32)
        for i in range(ROWS):
            for a in range(2):
                tp[pl.ds(rowp + a * 64, 64), i * 128:(i + 1) * 128] = t[i * SLOTS:i * SLOTS + PAIRED, a * 128:(a + 1) * 128]
                tu[pl.ds(rowu + a * 16, 16), i * 128:(i + 1) * 128] = t[i * SLOTS + PAIRED:(i + 1) * SLOTS, a * 128:(a + 1) * 128]

    pl.loop(0, 12, unroll=2)(t_step)
    spread(1, 7)
    pl.loop(12, 16, unroll=2)(t_step)
    spread(2, 6)
    forward(0)
    chain_col = jnp.transpose(jnp.broadcast_to(chain_v[...].astype(F32), (128, N)))
    obg = jnp.zeros((8, C_Z), F32)
    inv_own = []
    for i in range(ROWS):
        same = chain_col == chain[i].astype(F32)
        cntf = jnp.full((8, C_Z), count[i].astype(F32))
        inv_own.append((1.0 / (PAIRED + cntf + NORM_FLOOR))[0:1, :])
        raw = cot_ref[i].astype(F32)
        obg = obg + jnp.sum(raw.reshape(N // 8, 8, C_Z), axis=0)
        g = (raw * jnp.where(same, inv_own[i], 1.0 / (PAIRED + NORM_FLOOR))).astype(BF16)
        g_ref[:, i * 128:(i + 1) * 128] = g
        gm_ref[:, i * 128:(i + 1) * 128] = jnp.where(same, g.astype(F32), 0.0).astype(BF16)

    spread(3, 5)
    drain(rx.at[:, :, MAIN:], bgy_s, bgy_r, NY - 1)
    for k in range(1, NZ):
        bgz(k).start()
    forward(1, 7)

    def put_v(v, lane):
        both = jnp.concatenate(
            [v[:, 0:128].reshape(NRES, ROWS, 128), v[:, 128:256].reshape(NRES, ROWS, 128)], axis=1
        )
        v_ref[:, :, pl.ds(lane, 128)] = both.astype(BF16)

    def v_step(p):
        put_v(dot(g_ref[...], tp[pl.ds(pl.multiple_of(p * 256, 256), 256), :], NT), pl.multiple_of(p * 128, 128))

    def rs1(d, kz):
        dst = zpeer(kz) * NY + ypeer(2)
        src = v_ref.at[dst, :, d * HALF:(d + 1) * HALF]
        return rc(src, ry1.at[d, kz], rs1_s.at[0], rs1_r.at[d, kz], res=z * NY + ypeer(3 - 2 * d))

    def rs2(d, kz):
        dst = zpeer(kz) * NY + ypeer(3 - 2 * d)
        return rc(v_ref.at[dst, :, 0:MAIN], ry2.at[d, kz], rs2_s.at[0], rs2_r.at[d, kz], res=z * NY + ypeer(3 - 2 * d))

    def rsz(k):
        return rc(vsum.at[k - 1], rz.at[k - 1], rsz_s.at[0], rsz_r.at[0], res=zpeer(k) * NY + y)

    def bsz(k):
        src = v_ref.at[pl.ds(zpeer(k) * NY, NY), :, MAIN:]
        return rc(src, rbz.at[k - 1], bsz_s.at[0], bsz_r.at[0], res=zpeer(k) * NY + y)

    def bsy(k):
        return rc(sb.at[ypeer(k)], rby.at[k - 1], bsy_s.at[0], bsy_r.at[0], res=z * NY + ypeer(k))

    def side_sums():
        drain(rbz, bsz_s, bsz_r, NZ - 1)
        sbf[...] = v_ref[pl.ds(z * NY, NY), :, MAIN:].astype(F32) + jnp.sum(rbz[...].astype(F32), axis=0)
        sb[...] = sbf[...].astype(BF16)
        for k in range(1, NY):
            bsy(k).start()

    def second(*turns):
        for kz in turns:
            for d in range(2):
                slab = zpeer(kz) * NY + ypeer(3 - 2 * d)
                lanes = slice(d * HALF, (d + 1) * HALF)
                rs1(d, kz).wait_recv()
                v_ref[slab, :, lanes] = (v_ref[slab, :, lanes].astype(F32) + ry1[d, kz].astype(F32)).astype(BF16)

    def pass_on(*turns):
        for kz in turns:
            for d in range(2):
                rs2(d, kz).start()

    def third(*turns):
        for kz in turns:
            total = v_ref[zpeer(kz) * NY + y, :, 0:MAIN].astype(F32)
            for d in range(2):
                rs2(d, kz).wait_recv()
                total = total + ry2[d, kz].astype(F32)
            if kz:
                vsum[kz - 1] = total.astype(BF16)
                rsz(kz).start()
        return total

    def first(*turns):
        for kz in turns:
            for d in range(2):
                rs1(d, kz).start()

    for q in range(2):
        put_v(dot(gm_ref[...], tu[q * 256:(q + 1) * 256, :], NT), MAIN + q * 128)
    pl.loop(0, 4, unroll=2)(v_step)
    spread(4)
    forward(2, 6)
    pl.loop(4, 8, unroll=2)(v_step)
    forward(3)
    forward(5)
    first(4, 3, 5, 2, 6)
    forward(4)
    first(1, 7, 0)
    for k in range(1, NZ):
        bsz(k).start()
    second(4, 3, 5, 2)
    pass_on(4, 3, 5, 2)
    second(6)
    pass_on(6)
    second(1, 7, 0)
    drain(rx.at[:, :, 0:HALF], agf_s, agf_r, 2 * NZ)
    pass_on(1, 7, 0)
    drain(rx.at[:, :, MAIN:], bgz_s, bgz_r, NY * (NZ - 1))

    @pl.loop(0, NRES // 2)
    def _(d):
        a, b = rx[2 * d].astype(F32), rx[2 * d + 1].astype(F32)
        rows = pl.ds(pl.multiple_of(d * 16, 16), 16)
        for h in range(2):
            both = jnp.concatenate([a[h * 8:h * 8 + 8], b[h * 8:h * 8 + 8]], axis=0).astype(BF16)
            for p in range(8):
                rp[rows, p * 256 + h * 128:p * 256 + (h + 1) * 128] = both[:, p * 128:(p + 1) * 128]
            for q in range(2):
                ru[rows, q * 256 + h * 128:q * 256 + (h + 1) * 128] = both[:, 1024 + q * 128:1024 + (q + 1) * 128]

    def u_step(p):
        u = dot(rp[:, pl.ds(pl.multiple_of(p * 256, 256), 256)], g_ref[...], TN).astype(BF16)
        for h in range(2):
            for a in range(2):
                lane = pl.multiple_of((h * 16 + 2 * p + a) * 128, 128)
                for i in range(ROWS):
                    ucat[i * SLOTS:i * SLOTS + PAIRED, pl.ds(lane, 128)] = u[(h * 2 + a) * 64:(h * 2 + a + 1) * 64, i * 128:(i + 1) * 128]

    def u_side(q):
        u = dot(ru[:, q * 256:(q + 1) * 256], gm_ref[...], TN).astype(BF16)
        for h in range(2):
            for a in range(8):
                lane = (h * 16 + q * 8 + a) * 128
                for i in range(ROWS):
                    ucat[i * SLOTS + PAIRED:(i + 1) * SLOTS, lane:lane + 128] = u[(h * 8 + a) * 16:(h * 8 + a + 1) * 16, i * 128:(i + 1) * 128]

    def pd(e):
        k = (e - owner + C_H) % C_H
        return rc(dws.at[e], a_rx.at[k - 1], p_s.at[0], p_r.at[0], **opeer(k))

    def dw_step(g):
        dw = dot(lt[...], ucat[:, g * 256:(g + 1) * 256])
        for a in range(2):
            part = dw[:, a * 128:(a + 1) * 128]
            dwf[2 * g + a] = part
            dws[2 * g + a] = part.astype(BF16)

    def dw_send(first):
        @pl.loop(first, first + 8)
        def _(e):
            @pl.when(e != owner)
            def _():
                pd(e).start()

    pl.loop(0, 4, unroll=2)(u_step)
    u_side(0)
    for g in (0, 1, 2, 3, 8, 9, 10, 11):
        dw_step(g)
    third(4, 3)
    dw_send(0)
    dw_send(16)
    pl.loop(4, 8, unroll=2)(u_step)
    u_side(1)
    third(5, 2)
    side_sums()
    for g in (4, 5, 6, 7, 12, 13, 14, 15):
        dw_step(g)
    own = third(6, 1, 7, 0)
    dw_send(8)
    dw_send(24)

    def left_step(k, acc):
        cols = pl.ds(pl.multiple_of(k * 512, 512), 512)
        return acc + dot(ucat[:, cols], w2_ref[:, cols], NT)

    lgrad = lax.fori_loop(0, 8, left_step, jnp.zeros((ENT, C_H), F32), unroll=2)

    def td(k):
        slot = (owner + k) % C_H // NY
        return rc(sm.at[slot], t_rx.at[owner], td_s.at[0], td_r.at[0], **opeer(k))

    def uz(k):
        return rc(f_rx.at[z], f_rx.at[z], uz_s.at[0], uz_r.at[0], res=zpeer(k) * NY + y)

    def wd(k):
        return rc(so.at[dp], so.at[dp], wd_s.at[0], wd_r.at[0], dp=dpeer(k))

    rows8 = iota((8, C_Z), 0)

    def small_put(c, gw, tail_rows):
        tail = jnp.zeros((8, C_Z), F32)
        for k, row in enumerate(tail_rows):
            tail = jnp.where(rows8 == k, row, tail)
        main = jnp.concatenate([gw[:, 0:128], gw[:, 128:256]], axis=0).reshape(8, 8, C_Z)
        tails = jnp.broadcast_to(tail.reshape(8, 1, C_Z), (8, 8, C_Z))
        sm[:, c * 16:(c + 1) * 16, :] = jnp.concatenate([main, tails], axis=1).astype(BF16)

    def total(ref):
        return jnp.sum(ref[...].astype(F32), axis=0)

    gw_l = jnp.zeros((C_H, C_M), F32)
    gb_l = jnp.zeros((1, C_H), F32)
    for r in range(ROWS):
        rows = slice(r * SLOTS, (r + 1) * SLOTS)
        lact = (lgrad[rows] * slot_mask(r, (SLOTS, C_H), 0)).astype(BF16)
        gw_l = gw_l + dot(lact, normed[rows, :], TN)
        gb_l = gb_l + jnp.sum(lact.astype(F32), axis=0, keepdims=True)
        gn_ref[rows, :] = dot(lact, wt_ref[0:C_H, :])
    small_put(0, gw_l, (
        jnp.sum(obg, axis=0, keepdims=True),
        jnp.concatenate([gb_l, jnp.zeros((1, 96), F32)], axis=1),
    ))

    drain(rz, rsz_s, rsz_r, NZ - 1)
    drain(rby, bsy_s, bsy_r, NY - 1)
    own = jnp.concatenate(
        [own + jnp.sum(rz[...].astype(F32), axis=0), sbf[y] + jnp.sum(rby[...].astype(F32), axis=0)], axis=1
    )
    tiles = []
    for e in range(16):
        tiles.append(jnp.concatenate([own[:, e * 64:(e + 1) * 64], own[:, 1024 + e * 16:1024 + (e + 1) * 16]], axis=1))
    back = dot(permq, jnp.concatenate(tiles, axis=0).astype(BF16), TN)

    gw_r = jnp.zeros((C_H, C_M), F32)
    gb_r = jnp.zeros((C_H, 1), F32)
    gain_g = jnp.zeros((1, C_M), F32)
    shift_g = jnp.zeros((1, C_M), F32)
    for r in range(ROWS):
        rows = slice(r * SLOTS, (r + 1) * SLOTS)
        ract_t = (back[r * C_H:(r + 1) * C_H, :] * slot_mask(r, (C_H, SLOTS), 1)).astype(BF16)
        gw_r = gw_r + dot(ract_t, normed[rows, :])
        gb_r = gb_r + jnp.sum(ract_t.astype(F32), axis=1, keepdims=True)
        gn = gn_ref[rows, :] + dot(ract_t, wt_ref[C_H:, :], TN)
        gn_ref[rows, :] = gn
        gain_g = gain_g + jnp.sum(gn * xc[rows, :], axis=0, keepdims=True)
        shift_g = shift_g + jnp.sum(gn, axis=0, keepdims=True)
    gbr_row = jnp.transpose(jnp.broadcast_to(gb_r, (C_H, 128)))[0:1, :]
    small_put(1, gw_r, (
        gain_g[:, 0:128], gain_g[:, 128:256], shift_g[:, 0:128], shift_g[:, 128:256],
        jnp.concatenate([gbr_row, jnp.zeros((1, 96), F32)], axis=1),
    ))

    @pl.loop(1, C_H)
    def _(k):
        td(k).start()

    drain(a_rx, p_s, p_r, C_H - 1)

    def add(k, t):
        return t + a_rx[k].astype(F32)

    c_rx[z] = lax.fori_loop(0, C_H - 1, add, dwf[owner], unroll=True).astype(BF16)

    def cz(k):
        return rc(c_rx.at[z], c_rx.at[z], cz_s.at[0], cz_r.at[0], res=zpeer(k) * NY + y)

    for k in range(1, NZ):
        cz(k).start()

    t_rx[owner] = sm[dp]
    drain(t_rx, td_s, td_r, C_H - 1)
    f_rx[z] = total(t_rx).astype(BF16)
    for k in range(1, NZ):
        uz(k).start()

    drain(c_rx, cz_s, cz_r, NZ - 1)
    d_rx[owner] = (total(c_rx) * (1.0 / N)).astype(BF16)

    def ed(k):
        return rc(d_rx.at[owner], d_rx.at[owner], ed_s.at[0], ed_r.at[0], **opeer(k))

    @pl.loop(1, C_H)
    def _(k):
        ed(k).start()

    @pl.loop(0, 4)
    def _(g):
        cols = pl.ds(pl.multiple_of(g * 256, 256), 256)
        main = dot(rp[...], tp[:, cols])
        side = dot(ru[...], tu[:, cols])
        for a in range(2):
            i = 2 * g + a
            ch = jnp.int32(0)
            iv = jnp.zeros((1, C_Z), F32)
            for r in range(ROWS):
                ch = jnp.where(i == r, chain[r], ch)
                iv = jnp.where(i == r, inv_own[r], iv)
            same = chain_col == ch.astype(F32)
            m, s = main[:, a * 128:(a + 1) * 128], side[:, a * 128:(a + 1) * 128]
            out = jnp.where(same, (m + s) * iv, m * (1.0 / (PAIRED + NORM_FLOOR))) + obias_ref[...]
            upd_ref[i] = out.astype(BF16)

    upd_out = pltpu.make_async_copy(upd_ref, upd_h, out_s.at[0])
    upd_out.start()

    drain(f_rx, uz_s, uz_r, NZ - 1)
    so[dp] = (total(f_rx) * (1.0 / N)).astype(BF16)
    for k in range(1, NDP):
        wd(k).start()

    for r in range(ROWS):
        rows = slice(r * SLOTS, (r + 1) * SLOTS)
        scaled = xc[rows, :]
        gg = gn_ref[rows, :] * gain_ref[...]
        mean_g = jnp.mean(gg, axis=-1, keepdims=True)
        mean_p = jnp.mean(gg * scaled, axis=-1, keepdims=True)
        ract[rows, :] = (inv_ref[rows, :] * (gg - mean_g - scaled * mean_p)).astype(BF16)
    for b in range(PAIRED // 16):
        src = jnp.concatenate([ract[r * SLOTS + b * 16:r * SLOTS + b * 16 + 16, :] for r in range(ROWS)], axis=0)
        agrad_ref[b * 128:(b + 1) * 128, :] = dot(perm0, src, TN).astype(BF16)
    src = jnp.concatenate([ract[r * SLOTS + PAIRED:(r + 1) * SLOTS, :] for r in range(ROWS)], axis=0)
    agrad_ref[PAIRED * ROWS:, :] = dot(pick, src, TN).astype(BF16)

    agrad_out = pltpu.make_async_copy(agrad_ref, agrad_h, out_s.at[1])
    agrad_out.start()

    def sent(ref, sem):
        rc(ref, ref, sem.at[0], sem.at[0], dp=dpeer(1)).wait_send()

    sent(rx.at[0:NZ - 1, :, 0:MAIN], agz_s)
    sent(rx.at[0:2 * NZ, :, 0:MAIN], agy_s)
    sent(v_ref.at[0:2 * NZ, :, 0:HALF], rs1_s)
    sent(v_ref.at[0:2 * NZ, :, 0:MAIN], rs2_s)

    drain(d_rx, ed_s, ed_r, C_H - 1)
    dw_out = pltpu.make_async_copy(d_rx, dw_h, out_s.at[2])
    dw_out.start()
    drain(so, wd_s, wd_r, NDP - 1)
    small_out = pltpu.make_async_copy(so, small_h, out_s.at[3])
    small_out.start()
    for c in (upd_out, agrad_out, dw_out, small_out):
        c.wait()


def finish(
    upd_i, agrad_i, dw_i, small_i,
    upd_h, agrad_h, lw_h, lb_h, rw_h, rb_h, dw_h, ob_h, gain_h, shift_h,
    upd_v, agrad_v, dw_v, small_v, dw_f, lw_f, rw_f, lb_f, rb_f, ob_f, gain_f, shift_f, sem,
):
    copies = []

    def send(src, dst):
        copies.append(pltpu.make_async_copy(src, dst, sem.at[len(copies)]))
        copies[-1].start()

    fetches = [
        pltpu.make_async_copy(src, dst, sem.at[11 + n])
        for n, (src, dst) in enumerate(((dw_i, dw_v), (small_i, small_v), (upd_i, upd_v), (agrad_i, agrad_v)))
    ]
    for f in fetches:
        f.start()
    fetches[2].wait()
    send(upd_v, upd_h)
    fetches[3].wait()
    send(agrad_v, agrad_h)
    fetches[0].wait()
    for half in range(2):
        rows = slice(half * 16, (half + 1) * 16)
        for e in range(C_H):
            dw_f[rows, e, :] = dw_v[e, rows, :].astype(F32)
        send(dw_f.at[rows], dw_h.at[rows])
    fetches[1].wait()

    def tail(c, k):
        return small_v[k].astype(F32)[c * 16 + 8:c * 16 + 9]

    for c, (buf, out) in enumerate(((lw_f, lw_h), (rw_f, rw_h))):
        for half in range(2):
            rows = [small_v[half * 4 + d].astype(F32)[c * 16:c * 16 + 8] for d in range(4)]
            buf[:, half * 128:(half + 1) * 128] = jnp.concatenate(rows, axis=0)
        send(buf, out)
    ob_f[...] = tail(0, 0)
    lb_f[...] = tail(0, 1)[:, 0:C_H]
    rb_f[...] = tail(1, 4)[:, 0:C_H]
    gain_f[...] = jnp.concatenate([tail(1, 0), tail(1, 1)], axis=1)
    shift_f[...] = jnp.concatenate([tail(1, 2), tail(1, 3)], axis=1)
    for buf, out in ((ob_f, ob_h), (lb_f, lb_h), (rb_f, rb_h), (gain_f, gain_h), (shift_f, shift_h)):
        send(buf, out)
    for c in copies:
        c.wait()


def body(
    alignment, chain_ids, row_counts, norm_gain, norm_shift, left_weight, left_bias,
    right_weight, right_bias, out_weight, out_bias, pair_cotangent,
):
    sems = lambda *shape: pltpu.SemaphoreType.DMA(shape)
    vmem = pltpu.VMEM
    scratch = [
        vmem((ROWS, N, C_Z), BF16), vmem((128 * ROWS, C_M), BF16), pltpu.SMEM((1, N), jnp.int32), pltpu.SMEM((1, CHAINS), jnp.int32), vmem((1, N), jnp.int32),
        vmem((128 * ROWS, C_M), BF16), vmem((1, C_M), F32), vmem((1, C_M), F32), vmem((1, C_H), F32),
        vmem((1, C_H), F32), vmem((C_H * C_H, C_Z), BF16), vmem((1, C_Z), F32), vmem((ROWS, N, C_Z), BF16),
        vmem((2 * C_H, C_M), BF16), vmem((C_H * C_H, C_Z), F32), vmem((C_H, C_H * C_Z), BF16),
        vmem((ENT, C_M), F32), vmem((ENT, C_M), BF16), vmem((ENT, 1), F32),
        vmem((ENT, C_H), BF16), vmem((C_H, ENT), BF16), vmem((256, 128), BF16),
        vmem((2048, 1024), BF16), vmem((512, 1024), BF16), vmem((N, 1024), BF16), vmem((N, 1024), BF16),
        vmem((NRES, 16, 1280), BF16), vmem((NRES, 16, 1280), BF16), vmem((N, 2048), BF16), vmem((N, 512), BF16),
        vmem((2, NZ, 16, HALF), BF16), vmem((2, NZ, 16, MAIN), BF16), vmem((NZ - 1, 16, MAIN), BF16), vmem((NZ - 1, 16, MAIN), BF16),
        vmem((NZ - 1, NY, 16, 256), BF16), vmem((NY, 16, 256), F32), vmem((NY, 16, 256), BF16), vmem((NY - 1, 16, 256), BF16),
        vmem((ENT, 4096), BF16),
        vmem((C_H, C_H, C_Z), F32), vmem((C_H, C_H, C_Z), BF16), vmem((C_H - 1, C_H, C_Z), BF16),
        vmem((NZ, C_H, C_Z), BF16), vmem((C_H, C_H, C_Z), BF16),
        vmem((NDP, 32, C_Z), BF16), vmem((C_H, 32, C_Z), BF16), vmem((NZ, 32, C_Z), BF16), vmem((NDP, 32, C_Z), BF16),
        vmem((ENT, C_M), BF16), vmem((ENT, C_M), F32),
        sems(13), sems(4), sems(1), sems(1), sems(1), sems(1), sems(1), sems(1), sems(1), sems(1),
        sems(1), sems(NZ), sems(1), sems(2, NZ), sems(1), sems(1),
        sems(1), sems(2, NZ), sems(1), sems(2, NZ), sems(1), sems(1),
        sems(1), sems(1), sems(1), sems(1), sems(1), sems(1),
        sems(1), sems(1), sems(1), sems(1), sems(1), sems(1),
    ]
    hbm = pl.BlockSpec(memory_space=pltpu.HBM)
    upd, agrad, dw, small = pl.pallas_call(
        kernel,
        out_shape=(
            jax.ShapeDtypeStruct((ROWS, N, C_Z), BF16),
            jax.ShapeDtypeStruct((128 * ROWS, C_M), BF16),
            jax.ShapeDtypeStruct((C_H, C_H, C_Z), BF16),
            jax.ShapeDtypeStruct((NDP, 32, C_Z), BF16),
        ),
        in_specs=[hbm] * 12,
        out_specs=(hbm,) * 4,
        scratch_shapes=scratch,
        compiler_params=pltpu.CompilerParams(
            collective_id=0, has_side_effects=True, vmem_limit_bytes=56 * 1024 * 1024
        ),
    )(
        chain_ids, row_counts, alignment.reshape(128 * ROWS, C_M),
        norm_gain.reshape(1, C_M), norm_shift.reshape(1, C_M), left_weight.T, left_bias.reshape(1, C_H),
        right_weight.T, right_bias.reshape(1, C_H), out_weight, out_bias.reshape(1, C_Z), pair_cotangent[0],
    )
    outs = (
        ((ROWS, N, C_Z), BF16), ((128 * ROWS, C_M), BF16), ((C_H, C_M), F32), ((1, C_H), F32), ((C_H, C_M), F32),
        ((1, C_H), F32), ((C_H, C_H, C_Z), F32), ((1, C_Z), F32), ((1, C_M), F32), ((1, C_M), F32),
    )
    upd, agrad, lw, lb, rw, rb, dw, ob, gain, shift = pl.pallas_call(
        finish,
        out_shape=tuple(jax.ShapeDtypeStruct(*o) for o in outs),
        in_specs=[hbm] * 4,
        out_specs=(hbm,) * 10,
        scratch_shapes=[
            vmem((ROWS, N, C_Z), BF16), vmem((128 * ROWS, C_M), BF16),
            vmem((C_H, C_H, C_Z), BF16), vmem((NDP, 32, C_Z), BF16), vmem((C_H, C_H, C_Z), F32), vmem((C_H, C_M), F32), vmem((C_H, C_M), F32), vmem((1, C_H), F32), vmem((1, C_H), F32),
            vmem((1, C_Z), F32), vmem((1, C_M), F32), vmem((1, C_M), F32), sems(15),
        ],
        compiler_params=pltpu.CompilerParams(vmem_limit_bytes=56 * 1024 * 1024),
    )(upd, agrad, dw, small)
    return (
        upd[None],
        agrad.reshape(1, 128, ROWS, C_M),
        lw.T,
        lb.reshape(C_H),
        rw.T,
        rb.reshape(C_H),
        dw.reshape(C_H * C_H, C_Z),
        ob.reshape(C_Z),
        gain.reshape(C_M),
        shift.reshape(C_M),
    )


def solution(mesh):
    return jax.shard_map(
        body,
        mesh=mesh,
        in_specs=(
            P("dp", None, "res", None), P("dp", None), P("dp", None), P(), P(), P(), P(), P(), P(), P(), P(),
            P("dp", "res", None, None),
        ),
        out_specs=(
            P("dp", "res", None, None), P("dp", None, "res", None), P(), P(), P(), P(), P(), P(), P(), P(),
        ),
        check_vma=False,
    )
```

```python
import functools

import jax
import jax.numpy as jnp
from jax import lax
from jax.experimental import pallas as pl
from jax.experimental.pallas import tpu as pltpu
from jax.sharding import PartitionSpec as P

C_M = 256
C_H = 32
C_Z = 128
PAIRED = 64
UNP = 64
MOST = 16
CHAINS = 12
EPSILON = 1e-05
NORM_FLOOR = 0.001

ROWS = 8
SLOTS = PAIRED + MOST
NY, NZ, NDP = 4, 8, 8
NRES = NY * NZ
N = ROWS * NRES
ENT = ROWS * SLOTS
MAIN = 1024
HALF = MAIN // 2
F32, BF16 = jnp.float32, jnp.bfloat16
MESH = pl.DeviceIdType.MESH

NN = (((1,), (0,)), ((), ()))
NT = (((1,), (1,)), ((), ()))
TN = (((0,), (0,)), ((), ()))


def dot(a, b, dims=NN):
    return lax.dot_general(a, b, dims, preferred_element_type=F32)


def iota(shape, dim):
    return lax.broadcasted_iota(jnp.int32, shape, dim)


def onehot(cond):
    return jnp.where(cond, 1.0, 0.0).astype(BF16)


def kernel(
    chain_h, counts_h, x_h, gain_h, shift_h, lw_h, lb_h, rw_h, rb_h, w_h, ob_h, cot_h,
    upd_h, agrad_h, dw_h, small_h,
    upd_ref, agrad_ref, chain_s, counts_s, chain_v, x_ref, gain_ref, shift_ref, lb_ref, rb_ref, w_ref, obias_ref, cot_ref,
    wt_ref, wf, w2_ref,
    xc, normed, inv_ref, lrow, lt, q_ref, tp, tu, g_ref, gm_ref, v_ref, rx, rp, ru,
    ry1, ry2, vsum, rz, rbz, sbf, sb, rby, ucat, dwf, dws, a_rx, c_rx, d_rx,
    sm, t_rx, f_rx, so, ract, gn_ref,
    in_s, out_s, bgy_s, bgy_r, bgz_s, bgz_r, bsz_s, bsz_r, bsy_s, bsy_r, agz_s, agz_r, agy_s, agy_r, agf_s, agf_r, rs1_s, rs1_r, rs2_s, rs2_r, rsz_s, rsz_r,
    p_s, p_r, cz_s, cz_r, ed_s, ed_r,
    td_s, td_r, uz_s, uz_r, wd_s, wd_r,
):
    me = lax.axis_index("res")
    dp = lax.axis_index("dp")
    z, y = me // NY, me % NY

    def zpeer(k):
        return (z + k) % NZ

    def ypeer(k):
        return (y + k) % NY

    def dpeer(k):
        return (dp + k) % NDP

    def rc(src, dst, ss, rs, **where):
        return pltpu.make_async_remote_copy(
            src_ref=src, dst_ref=dst, send_sem=ss, recv_sem=rs,
            device_id=where, device_id_type=MESH,
        )

    fetches = [
        pltpu.make_async_copy(src, dst, in_s.at[n])
        for n, (src, dst) in enumerate((
            (x_h, x_ref), (chain_h, chain_s), (counts_h, counts_s), (chain_h, chain_v), (gain_h, gain_ref),
            (shift_h, shift_ref), (lw_h, wt_ref.at[0:C_H]), (lb_h, lb_ref), (rw_h, wt_ref.at[C_H:2 * C_H]), (rb_h, rb_ref),
            (w_h, w_ref), (ob_h, obias_ref), (cot_h, cot_ref),
        ))
    ]
    for f in fetches:
        f.start()

    barrier = pltpu.get_barrier_semaphore()

    for k in range(1, NZ):
        pl.semaphore_signal(barrier, inc=1, device_id={"res": zpeer(k) * NY + y}, device_id_type=MESH)
    for k in range(1, NY):
        pl.semaphore_signal(barrier, inc=1, device_id={"res": z * NY + ypeer(k)}, device_id_type=MESH)

    owner = dp * NY + y

    def opeer(k):
        o = (owner + k) % C_H
        return {"dp": o // NY, "res": z * NY + o % NY}

    @pl.loop(1, NDP)
    def _(k):
        for j in range(NY):
            pl.semaphore_signal(
                barrier, inc=1, device_id={"dp": dpeer(k), "res": z * NY + ypeer(j)}, device_id_type=MESH
            )

    for f in fetches[:10]:
        f.wait()
    rb_col = jnp.transpose(jnp.broadcast_to(rb_ref[...], (8, C_H)))[:, 0:1]

    chain, start, count, base = [], [], [], []
    for r in range(ROWS):
        c = chain_s[0, me * ROWS + r]
        st = jnp.int32(0)
        ct = jnp.int32(0)
        for k in range(CHAINS):
            v = counts_s[0, k]
            st = st + jnp.where(c > k, v, 0)
            ct = ct + jnp.where(c == k, v, 0)
        chain.append(c)
        start.append(st)
        count.append(ct)
        base.append(jnp.minimum(st, UNP - MOST))

    def slot_mask(r, shape, dim):
        s = iota(shape, dim)
        row = s - PAIRED + base[r]
        live = (row >= start[r]) & (row < start[r] + count[r])
        return jnp.where((s < PAIRED) | live, 1.0, 0.0)

    ro, co = iota((128, 128), 0), iota((128, 128), 1)
    perm0 = onehot(co == (ro % 16) * ROWS + ro // 16)
    for b in range(PAIRED // 16):
        part = dot(perm0, x_ref[b * 128:(b + 1) * 128, :])
        for r in range(ROWS):
            xc[r * SLOTS + b * 16:r * SLOTS + b * 16 + 16, :] = part[r * 16:(r + 1) * 16]
    ru_i = iota((128, UNP * ROWS), 0)
    base_rows = jnp.zeros((128, UNP * ROWS), jnp.int32)
    for r in range(ROWS):
        base_rows = jnp.where(ru_i // 16 == r, base[r], base_rows)
    pick = onehot(iota((128, UNP * ROWS), 1) == (base_rows + ru_i % 16) * ROWS + ru_i // 16)
    part = dot(pick, x_ref[PAIRED * ROWS:, :])
    for r in range(ROWS):
        xc[r * SLOTS + PAIRED:(r + 1) * SLOTS, :] = part[r * 16:(r + 1) * 16]

    for r in range(ROWS):
        rows = slice(r * SLOTS, (r + 1) * SLOTS)
        floats = xc[rows, :]
        centred = floats - jnp.mean(floats, axis=-1, keepdims=True)
        inverse = lax.rsqrt(jnp.mean(centred * centred, axis=-1, keepdims=True) + EPSILON)
        scaled = centred * inverse
        nrm = (scaled * gain_ref[...] + shift_ref[...]).astype(BF16)
        xc[rows, :] = scaled
        inv_ref[rows, :] = inverse
        normed[rows, :] = nrm
        left = (dot(nrm, wt_ref[0:C_H, :], NT) + lb_ref[...]) * slot_mask(r, (SLOTS, C_H), 0)
        lrow[rows, :] = left.astype(BF16)
        right = (dot(wt_ref[C_H:, :], nrm, NT) + rb_col) * slot_mask(r, (C_H, SLOTS), 1)
        q_ref[r * C_H:(r + 1) * C_H, 0:SLOTS] = right.astype(BF16)
    re, ce = iota((256, 256), 0), iota((256, 256), 1)
    permq = onehot(ce == (re % 8) * 32 + ((re // 8) % 2) * 16 + re // 16)
    mixed = dot(permq, q_ref[:, 0:SLOTS])
    for p in range(8):
        rx[me, :, p * 128:(p + 1) * 128] = jnp.concatenate(
            [mixed[(2 * p + a) * 16:(2 * p + a + 1) * 16, 0:PAIRED] for a in range(2)], axis=1
        ).astype(BF16)
    for q in range(2):
        rx[me, :, 1024 + q * 128:1024 + (q + 1) * 128] = jnp.concatenate(
            [mixed[(8 * q + a) * 16:(8 * q + a + 1) * 16, PAIRED:SLOTS] for a in range(8)], axis=1
        ).astype(BF16)

    pl.semaphore_wait(barrier, NZ + NY - 2 + NY * (NDP - 1))

    def agz(k):
        part = rx.at[me, :, 0:MAIN]
        return rc(part, part, agz_s.at[0], agz_r.at[k], res=zpeer(k) * NY + y)

    def agy(d, kz):
        slot = ((z - kz + NZ) % NZ) * NY + y
        part = rx.at[slot, :, 0:MAIN]
        return rc(part, part, agy_s.at[0], agy_r.at[d, kz], res=z * NY + ypeer(1 + 2 * d))

    def agf(d, kz):
        slot = ((z - kz + NZ) % NZ) * NY + ypeer(3 - 2 * d)
        part = rx.at[slot, :, d * HALF:(d + 1) * HALF]
        return rc(part, part, agf_s.at[0], agf_r.at[0], res=z * NY + ypeer(1 + 2 * d))

    def bgy(k):
        part = rx.at[me, :, MAIN:]
        return rc(part, part, bgy_s.at[0], bgy_r.at[0], res=z * NY + ypeer(k))

    def bgz(k):
        part = rx.at[pl.ds(z * NY, NY), :, MAIN:]
        return rc(part, part, bgz_s.at[0], bgz_r.at[0], res=zpeer(k) * NY + y)

    def drain(ref, send, recv, count):
        some = ref.at[0:count]
        rc(some, some, send.at[0], recv.at[0], dp=dpeer(1)).wait()

    def spread(*turns):
        for kz in turns:
            if kz:
                agz(kz).wait_recv()
            for d in range(2):
                agy(d, kz).start()

    def forward(*turns):
        for kz in turns:
            for d in range(2):
                agy(d, kz).wait_recv()
                agf(d, kz).start()

    for k in range(1, NY):
        bgy(k).start()
    for k in (1, 7, 2, 6, 3, 5, 4):
        agz(k).start()
    spread(0)

    for f in fetches[10:]:
        f.wait()
    wf[...] = w_ref[...].astype(F32)
    for e in range(C_H):
        w2_ref[:, e * 128:(e + 1) * 128] = wf[pl.ds(e, C_H, stride=C_H), :].astype(BF16)

    lt[...] = jnp.transpose(lrow[...].astype(F32)).astype(BF16)

    def t_step(g):
        h, p = g // 8, g % 8
        t = dot(lrow[...], w2_ref[:, pl.ds(pl.multiple_of(g * 256, 256), 256)]).astype(BF16)
        rowp = pl.multiple_of((p * 2 + h) * 128, 128)
        rowu = pl.multiple_of(((p // 4) * 2 + h) * 128 + (p % 4) * 32, 32)
        for i in range(ROWS):
            for a in range(2):
                tp[pl.ds(rowp + a * 64, 64), i * 128:(i + 1) * 128] = t[i * SLOTS:i * SLOTS + PAIRED, a * 128:(a + 1) * 128]
                tu[pl.ds(rowu + a * 16, 16), i * 128:(i + 1) * 128] = t[i * SLOTS + PAIRED:(i + 1) * SLOTS, a * 128:(a + 1) * 128]

    pl.loop(0, 12, unroll=2)(t_step)
    spread(1, 7)
    pl.loop(12, 16, unroll=2)(t_step)
    spread(2, 6)
    forward(0)
    chain_col = jnp.transpose(jnp.broadcast_to(chain_v[...].astype(F32), (128, N)))
    obg = jnp.zeros((8, C_Z), F32)
    inv_own = []
    for i in range(ROWS):
        same = chain_col == chain[i].astype(F32)
        cntf = jnp.full((8, C_Z), count[i].astype(F32))
        inv_own.append((1.0 / (PAIRED + cntf + NORM_FLOOR))[0:1, :])
        raw = cot_ref[i].astype(F32)
        obg = obg + jnp.sum(raw.reshape(N // 8, 8, C_Z), axis=0)
        g = (raw * jnp.where(same, inv_own[i], 1.0 / (PAIRED + NORM_FLOOR))).astype(BF16)
        g_ref[:, i * 128:(i + 1) * 128] = g
        gm_ref[:, i * 128:(i + 1) * 128] = jnp.where(same, g.astype(F32), 0.0).astype(BF16)

    spread(3, 5)
    drain(rx.at[:, :, MAIN:], bgy_s, bgy_r, NY - 1)
    for k in range(1, NZ):
        bgz(k).start()
    forward(1, 7)

    def put_v(v, lane):
        both = jnp.concatenate(
            [v[:, 0:128].reshape(NRES, ROWS, 128), v[:, 128:256].reshape(NRES, ROWS, 128)], axis=1
        )
        v_ref[:, :, pl.ds(lane, 128)] = both.astype(BF16)

    def v_step(p):
        put_v(dot(g_ref[...], tp[pl.ds(pl.multiple_of(p * 256, 256), 256), :], NT), pl.multiple_of(p * 128, 128))

    def rs1(d, kz):
        dst = zpeer(kz) * NY + ypeer(2)
        src = v_ref.at[dst, :, d * HALF:(d + 1) * HALF]
        return rc(src, ry1.at[d, kz], rs1_s.at[0], rs1_r.at[d, kz], res=z * NY + ypeer(3 - 2 * d))

    def rs2(d, kz):
        dst = zpeer(kz) * NY + ypeer(3 - 2 * d)
        return rc(v_ref.at[dst, :, 0:MAIN], ry2.at[d, kz], rs2_s.at[0], rs2_r.at[d, kz], res=z * NY + ypeer(3 - 2 * d))

    def rsz(k):
        return rc(vsum.at[k - 1], rz.at[k - 1], rsz_s.at[0], rsz_r.at[0], res=zpeer(k) * NY + y)

    def bsz(k):
        src = v_ref.at[pl.ds(zpeer(k) * NY, NY), :, MAIN:]
        return rc(src, rbz.at[k - 1], bsz_s.at[0], bsz_r.at[0], res=zpeer(k) * NY + y)

    def bsy(k):
        return rc(sb.at[ypeer(k)], rby.at[k - 1], bsy_s.at[0], bsy_r.at[0], res=z * NY + ypeer(k))

    def side_sums():
        drain(rbz, bsz_s, bsz_r, NZ - 1)
        sbf[...] = v_ref[pl.ds(z * NY, NY), :, MAIN:].astype(F32) + jnp.sum(rbz[...].astype(F32), axis=0)
        sb[...] = sbf[...].astype(BF16)
        for k in range(1, NY):
            bsy(k).start()

    def second(*turns):
        for kz in turns:
            for d in range(2):
                slab = zpeer(kz) * NY + ypeer(3 - 2 * d)
                lanes = slice(d * HALF, (d + 1) * HALF)
                rs1(d, kz).wait_recv()
                v_ref[slab, :, lanes] = (v_ref[slab, :, lanes].astype(F32) + ry1[d, kz].astype(F32)).astype(BF16)

    def pass_on(*turns):
        for kz in turns:
            for d in range(2):
                rs2(d, kz).start()

    def third(*turns):
        for kz in turns:
            total = v_ref[zpeer(kz) * NY + y, :, 0:MAIN].astype(F32)
            for d in range(2):
                rs2(d, kz).wait_recv()
                total = total + ry2[d, kz].astype(F32)
            if kz:
                vsum[kz - 1] = total.astype(BF16)
                rsz(kz).start()
        return total

    def first(*turns):
        for kz in turns:
            for d in range(2):
                rs1(d, kz).start()

    for q in range(2):
        put_v(dot(gm_ref[...], tu[q * 256:(q + 1) * 256, :], NT), MAIN + q * 128)
    pl.loop(0, 4, unroll=2)(v_step)
    spread(4)
    forward(2, 6)
    pl.loop(4, 8, unroll=2)(v_step)
    forward(3)
    forward(5)
    first(4, 3, 5, 2, 6)
    forward(4)
    first(1, 7, 0)
    for k in range(1, NZ):
        bsz(k).start()
    second(4, 3, 5, 2)
    pass_on(4, 3, 5, 2)
    second(6)
    pass_on(6)
    second(1, 7, 0)
    drain(rx.at[:, :, 0:HALF], agf_s, agf_r, 2 * NZ)
    pass_on(1, 7, 0)
    drain(rx.at[:, :, MAIN:], bgz_s, bgz_r, NY * (NZ - 1))

    @pl.loop(0, NRES // 2)
    def _(d):
        a, b = rx[2 * d].astype(F32), rx[2 * d + 1].astype(F32)
        rows = pl.ds(pl.multiple_of(d * 16, 16), 16)
        for h in range(2):
            both = jnp.concatenate([a[h * 8:h * 8 + 8], b[h * 8:h * 8 + 8]], axis=0).astype(BF16)
            for p in range(8):
                rp[rows, p * 256 + h * 128:p * 256 + (h + 1) * 128] = both[:, p * 128:(p + 1) * 128]
            for q in range(2):
                ru[rows, q * 256 + h * 128:q * 256 + (h + 1) * 128] = both[:, 1024 + q * 128:1024 + (q + 1) * 128]

    def u_step(p):
        u = dot(rp[:, pl.ds(pl.multiple_of(p * 256, 256), 256)], g_ref[...], TN).astype(BF16)
        for h in range(2):
            for a in range(2):
                lane = pl.multiple_of((h * 16 + 2 * p + a) * 128, 128)
                for i in range(ROWS):
                    ucat[i * SLOTS:i * SLOTS + PAIRED, pl.ds(lane, 128)] = u[(h * 2 + a) * 64:(h * 2 + a + 1) * 64, i * 128:(i + 1) * 128]

    def u_side(q):
        u = dot(ru[:, q * 256:(q + 1) * 256], gm_ref[...], TN).astype(BF16)
        for h in range(2):
            for a in range(8):
                lane = (h * 16 + q * 8 + a) * 128
                for i in range(ROWS):
                    ucat[i * SLOTS + PAIRED:(i + 1) * SLOTS, lane:lane + 128] = u[(h * 8 + a) * 16:(h * 8 + a + 1) * 16, i * 128:(i + 1) * 128]

    def pd(e):
        k = (e - owner + C_H) % C_H
        return rc(dws.at[e], a_rx.at[k - 1], p_s.at[0], p_r.at[0], **opeer(k))

    def dw_step(g):
        dw = dot(lt[...], ucat[:, g * 256:(g + 1) * 256])
        for a in range(2):
            part = dw[:, a * 128:(a + 1) * 128]
            dwf[2 * g + a] = part
            dws[2 * g + a] = part.astype(BF16)

    def dw_send(first):
        @pl.loop(first, first + 8)
        def _(e):
            @pl.when(e != owner)
            def _():
                pd(e).start()

    pl.loop(0, 4, unroll=2)(u_step)
    u_side(0)
    for g in (0, 1, 2, 3, 8, 9, 10, 11):
        dw_step(g)
    dw_send(0)
    dw_send(16)
    third(4, 3)
    pl.loop(4, 8, unroll=2)(u_step)
    u_side(1)
    third(5, 2)
    side_sums()
    for g in (4, 5, 6, 7, 12, 13, 14, 15):
        dw_step(g)
    dw_send(8)
    dw_send(24)
    own = third(6, 1, 7, 0)

    def left_step(k, acc):
        cols = pl.ds(pl.multiple_of(k * 512, 512), 512)
        return acc + dot(ucat[:, cols], w2_ref[:, cols], NT)

    lgrad = lax.fori_loop(0, 8, left_step, jnp.zeros((ENT, C_H), F32), unroll=2)

    def td(k):
        slot = (owner + k) % C_H // NY
        return rc(sm.at[slot], t_rx.at[owner], td_s.at[0], td_r.at[0], **opeer(k))

    def uz(k):
        return rc(f_rx.at[z], f_rx.at[z], uz_s.at[0], uz_r.at[0], res=zpeer(k) * NY + y)

    def wd(k):
        return rc(so.at[dp], so.at[dp], wd_s.at[0], wd_r.at[0], dp=dpeer(k))

    rows8 = iota((8, C_Z), 0)

    def small_put(c, gw, tail_rows):
        tail = jnp.zeros((8, C_Z), F32)
        for k, row in enumerate(tail_rows):
            tail = jnp.where(rows8 == k, row, tail)
        main = jnp.concatenate([gw[:, 0:128], gw[:, 128:256]], axis=0).reshape(8, 8, C_Z)
        tails = jnp.broadcast_to(tail.reshape(8, 1, C_Z), (8, 8, C_Z))
        sm[:, c * 16:(c + 1) * 16, :] = jnp.concatenate([main, tails], axis=1).astype(BF16)

    def total(ref):
        return jnp.sum(ref[...].astype(F32), axis=0)

    gw_l = jnp.zeros((C_H, C_M), F32)
    gb_l = jnp.zeros((1, C_H), F32)
    for r in range(ROWS):
        rows = slice(r * SLOTS, (r + 1) * SLOTS)
        lact = (lgrad[rows] * slot_mask(r, (SLOTS, C_H), 0)).astype(BF16)
        gw_l = gw_l + dot(lact, normed[rows, :], TN)
        gb_l = gb_l + jnp.sum(lact.astype(F32), axis=0, keepdims=True)
        gn_ref[rows, :] = dot(lact, wt_ref[0:C_H, :])
    small_put(0, gw_l, (
        jnp.sum(obg, axis=0, keepdims=True),
        jnp.concatenate([gb_l, jnp.zeros((1, 96), F32)], axis=1),
    ))

    drain(rz, rsz_s, rsz_r, NZ - 1)
    drain(rby, bsy_s, bsy_r, NY - 1)
    own = jnp.concatenate(
        [own + jnp.sum(rz[...].astype(F32), axis=0), sbf[y] + jnp.sum(rby[...].astype(F32), axis=0)], axis=1
    )
    tiles = []
    for e in range(16):
        tiles.append(jnp.concatenate([own[:, e * 64:(e + 1) * 64], own[:, 1024 + e * 16:1024 + (e + 1) * 16]], axis=1))
    back = dot(permq, jnp.concatenate(tiles, axis=0).astype(BF16), TN)

    gw_r = jnp.zeros((C_H, C_M), F32)
    gb_r = jnp.zeros((C_H, 1), F32)
    gain_g = jnp.zeros((1, C_M), F32)
    shift_g = jnp.zeros((1, C_M), F32)
    for r in range(ROWS):
        rows = slice(r * SLOTS, (r + 1) * SLOTS)
        ract_t = (back[r * C_H:(r + 1) * C_H, :] * slot_mask(r, (C_H, SLOTS), 1)).astype(BF16)
        gw_r = gw_r + dot(ract_t, normed[rows, :])
        gb_r = gb_r + jnp.sum(ract_t.astype(F32), axis=1, keepdims=True)
        gn = gn_ref[rows, :] + dot(ract_t, wt_ref[C_H:, :], TN)
        gn_ref[rows, :] = gn
        gain_g = gain_g + jnp.sum(gn * xc[rows, :], axis=0, keepdims=True)
        shift_g = shift_g + jnp.sum(gn, axis=0, keepdims=True)
    gbr_row = jnp.transpose(jnp.broadcast_to(gb_r, (C_H, 128)))[0:1, :]
    small_put(1, gw_r, (
        gain_g[:, 0:128], gain_g[:, 128:256], shift_g[:, 0:128], shift_g[:, 128:256],
        jnp.concatenate([gbr_row, jnp.zeros((1, 96), F32)], axis=1),
    ))

    @pl.loop(1, C_H)
    def _(k):
        td(k).start()

    drain(a_rx, p_s, p_r, C_H - 1)

    def add(k, t):
        return t + a_rx[k].astype(F32)

    c_rx[z] = lax.fori_loop(0, C_H - 1, add, dwf[owner], unroll=True).astype(BF16)

    def cz(k):
        return rc(c_rx.at[z], c_rx.at[z], cz_s.at[0], cz_r.at[0], res=zpeer(k) * NY + y)

    for k in range(1, NZ):
        cz(k).start()

    t_rx[owner] = sm[dp]
    drain(t_rx, td_s, td_r, C_H - 1)
    f_rx[z] = total(t_rx).astype(BF16)
    for k in range(1, NZ):
        uz(k).start()

    drain(c_rx, cz_s, cz_r, NZ - 1)
    d_rx[owner] = (total(c_rx) * (1.0 / N)).astype(BF16)

    def ed(k):
        return rc(d_rx.at[owner], d_rx.at[owner], ed_s.at[0], ed_r.at[0], **opeer(k))

    @pl.loop(1, C_H)
    def _(k):
        ed(k).start()

    @pl.loop(0, 4)
    def _(g):
        cols = pl.ds(pl.multiple_of(g * 256, 256), 256)
        main = dot(rp[...], tp[:, cols])
        side = dot(ru[...], tu[:, cols])
        for a in range(2):
            i = 2 * g + a
            ch = jnp.int32(0)
            iv = jnp.zeros((1, C_Z), F32)
            for r in range(ROWS):
                ch = jnp.where(i == r, chain[r], ch)
                iv = jnp.where(i == r, inv_own[r], iv)
            same = chain_col == ch.astype(F32)
            m, s = main[:, a * 128:(a + 1) * 128], side[:, a * 128:(a + 1) * 128]
            out = jnp.where(same, (m + s) * iv, m * (1.0 / (PAIRED + NORM_FLOOR))) + obias_ref[...]
            upd_ref[i] = out.astype(BF16)

    for r in range(ROWS):
        rows = slice(r * SLOTS, (r + 1) * SLOTS)
        scaled = xc[rows, :]
        gg = gn_ref[rows, :] * gain_ref[...]
        mean_g = jnp.mean(gg, axis=-1, keepdims=True)
        mean_p = jnp.mean(gg * scaled, axis=-1, keepdims=True)
        ract[rows, :] = (inv_ref[rows, :] * (gg - mean_g - scaled * mean_p)).astype(BF16)
    for b in range(PAIRED // 16):
        src = jnp.concatenate([ract[r * SLOTS + b * 16:r * SLOTS + b * 16 + 16, :] for r in range(ROWS)], axis=0)
        agrad_ref[b * 128:(b + 1) * 128, :] = dot(perm0, src, TN).astype(BF16)
    src = jnp.concatenate([ract[r * SLOTS + PAIRED:(r + 1) * SLOTS, :] for r in range(ROWS)], axis=0)
    agrad_ref[PAIRED * ROWS:, :] = dot(pick, src, TN).astype(BF16)

    upd_out = pltpu.make_async_copy(upd_ref, upd_h, out_s.at[0])
    upd_out.start()

    agrad_out = pltpu.make_async_copy(agrad_ref, agrad_h, out_s.at[1])
    agrad_out.start()

    drain(f_rx, uz_s, uz_r, NZ - 1)
    so[dp] = (total(f_rx) * (1.0 / N)).astype(BF16)
    for k in range(1, NDP):
        wd(k).start()

    def sent(ref, sem):
        rc(ref, ref, sem.at[0], sem.at[0], dp=dpeer(1)).wait_send()

    sent(rx.at[0:NZ - 1, :, 0:MAIN], agz_s)
    sent(rx.at[0:2 * NZ, :, 0:MAIN], agy_s)
    sent(v_ref.at[0:2 * NZ, :, 0:HALF], rs1_s)
    sent(v_ref.at[0:2 * NZ, :, 0:MAIN], rs2_s)

    drain(d_rx, ed_s, ed_r, C_H - 1)
    dw_out = pltpu.make_async_copy(d_rx, dw_h, out_s.at[2])
    dw_out.start()
    drain(so, wd_s, wd_r, NDP - 1)
    small_out = pltpu.make_async_copy(so, small_h, out_s.at[3])
    small_out.start()
    for c in (upd_out, agrad_out, dw_out, small_out):
        c.wait()


def finish(
    upd_i, agrad_i, dw_i, small_i,
    upd_h, agrad_h, lw_h, lb_h, rw_h, rb_h, dw_h, ob_h, gain_h, shift_h,
    upd_v, agrad_v, dw_v, small_v, dw_f, lw_f, rw_f, lb_f, rb_f, ob_f, gain_f, shift_f, sem,
):
    copies = []

    def send(src, dst):
        copies.append(pltpu.make_async_copy(src, dst, sem.at[len(copies)]))
        copies[-1].start()

    fetches = [
        pltpu.make_async_copy(src, dst, sem.at[10 + n])
        for n, (src, dst) in enumerate(((dw_i, dw_v), (small_i, small_v), (upd_i, upd_v), (agrad_i, agrad_v)))
    ]
    for f in fetches:
        f.start()
    fetches[0].wait()
    for d in range(NDP):
        for a in range(4):
            dw_f[:, d * 4 + a, :] = dw_v[d * 4 + a].astype(F32)
    send(dw_f, dw_h)
    fetches[2].wait()
    send(upd_v, upd_h)
    fetches[3].wait()
    send(agrad_v, agrad_h)
    fetches[1].wait()

    def tail(c, k):
        return small_v[k].astype(F32)[c * 16 + 8:c * 16 + 9]

    for c, (buf, out) in enumerate(((lw_f, lw_h), (rw_f, rw_h))):
        for half in range(2):
            rows = [small_v[half * 4 + d].astype(F32)[c * 16:c * 16 + 8] for d in range(4)]
            buf[:, half * 128:(half + 1) * 128] = jnp.concatenate(rows, axis=0)
        send(buf, out)
    ob_f[...] = tail(0, 0)
    lb_f[...] = tail(0, 1)[:, 0:C_H]
    rb_f[...] = tail(1, 4)[:, 0:C_H]
    gain_f[...] = jnp.concatenate([tail(1, 0), tail(1, 1)], axis=1)
    shift_f[...] = jnp.concatenate([tail(1, 2), tail(1, 3)], axis=1)
    for buf, out in ((ob_f, ob_h), (lb_f, lb_h), (rb_f, rb_h), (gain_f, gain_h), (shift_f, shift_h)):
        send(buf, out)
    for c in copies:
        c.wait()


def body(
    alignment, chain_ids, row_counts, norm_gain, norm_shift, left_weight, left_bias,
    right_weight, right_bias, out_weight, out_bias, pair_cotangent,
):
    sems = lambda *shape: pltpu.SemaphoreType.DMA(shape)
    vmem = pltpu.VMEM
    scratch = [
        vmem((ROWS, N, C_Z), BF16), vmem((128 * ROWS, C_M), BF16), pltpu.SMEM((1, N), jnp.int32), pltpu.SMEM((1, CHAINS), jnp.int32), vmem((1, N), jnp.int32),
        vmem((128 * ROWS, C_M), BF16), vmem((1, C_M), F32), vmem((1, C_M), F32), vmem((1, C_H), F32),
        vmem((1, C_H), F32), vmem((C_H * C_H, C_Z), BF16), vmem((1, C_Z), F32), vmem((ROWS, N, C_Z), BF16),
        vmem((2 * C_H, C_M), BF16), vmem((C_H * C_H, C_Z), F32), vmem((C_H, C_H * C_Z), BF16),
        vmem((ENT, C_M), F32), vmem((ENT, C_M), BF16), vmem((ENT, 1), F32),
        vmem((ENT, C_H), BF16), vmem((C_H, ENT), BF16), vmem((256, 128), BF16),
        vmem((2048, 1024), BF16), vmem((512, 1024), BF16), vmem((N, 1024), BF16), vmem((N, 1024), BF16),
        vmem((NRES, 16, 1280), BF16), vmem((NRES, 16, 1280), BF16), vmem((N, 2048), BF16), vmem((N, 512), BF16),
        vmem((2, NZ, 16, HALF), BF16), vmem((2, NZ, 16, MAIN), BF16), vmem((NZ - 1, 16, MAIN), BF16), vmem((NZ - 1, 16, MAIN), BF16),
        vmem((NZ - 1, NY, 16, 256), BF16), vmem((NY, 16, 256), F32), vmem((NY, 16, 256), BF16), vmem((NY - 1, 16, 256), BF16),
        vmem((ENT, 4096), BF16),
        vmem((C_H, C_H, C_Z), F32), vmem((C_H, C_H, C_Z), BF16), vmem((C_H - 1, C_H, C_Z), BF16),
        vmem((NZ, C_H, C_Z), BF16), vmem((C_H, C_H, C_Z), BF16),
        vmem((NDP, 32, C_Z), BF16), vmem((C_H, 32, C_Z), BF16), vmem((NZ, 32, C_Z), BF16), vmem((NDP, 32, C_Z), BF16),
        vmem((ENT, C_M), BF16), vmem((ENT, C_M), F32),
        sems(13), sems(4), sems(1), sems(1), sems(1), sems(1), sems(1), sems(1), sems(1), sems(1),
        sems(1), sems(NZ), sems(1), sems(2, NZ), sems(1), sems(1),
        sems(1), sems(2, NZ), sems(1), sems(2, NZ), sems(1), sems(1),
        sems(1), sems(1), sems(1), sems(1), sems(1), sems(1),
        sems(1), sems(1), sems(1), sems(1), sems(1), sems(1),
    ]
    hbm = pl.BlockSpec(memory_space=pltpu.HBM)
    upd, agrad, dw, small = pl.pallas_call(
        kernel,
        out_shape=(
            jax.ShapeDtypeStruct((ROWS, N, C_Z), BF16),
            jax.ShapeDtypeStruct((128 * ROWS, C_M), BF16),
            jax.ShapeDtypeStruct((C_H, C_H, C_Z), BF16),
            jax.ShapeDtypeStruct((NDP, 32, C_Z), BF16),
        ),
        in_specs=[hbm] * 12,
        out_specs=(hbm,) * 4,
        scratch_shapes=scratch,
        compiler_params=pltpu.CompilerParams(
            collective_id=0, has_side_effects=True, vmem_limit_bytes=56 * 1024 * 1024
        ),
    )(
        chain_ids, row_counts, alignment.reshape(128 * ROWS, C_M),
        norm_gain.reshape(1, C_M), norm_shift.reshape(1, C_M), left_weight.T, left_bias.reshape(1, C_H),
        right_weight.T, right_bias.reshape(1, C_H), out_weight, out_bias.reshape(1, C_Z), pair_cotangent[0],
    )
    outs = (
        ((ROWS, N, C_Z), BF16), ((128 * ROWS, C_M), BF16), ((C_H, C_M), F32), ((1, C_H), F32), ((C_H, C_M), F32),
        ((1, C_H), F32), ((C_H, C_H, C_Z), F32), ((1, C_Z), F32), ((1, C_M), F32), ((1, C_M), F32),
    )
    upd, agrad, lw, lb, rw, rb, dw, ob, gain, shift = pl.pallas_call(
        finish,
        out_shape=tuple(jax.ShapeDtypeStruct(*o) for o in outs),
        in_specs=[hbm] * 4,
        out_specs=(hbm,) * 10,
        scratch_shapes=[
            vmem((ROWS, N, C_Z), BF16), vmem((128 * ROWS, C_M), BF16),
            vmem((C_H, C_H, C_Z), BF16), vmem((NDP, 32, C_Z), BF16), vmem((C_H, C_H, C_Z), F32), vmem((C_H, C_M), F32), vmem((C_H, C_M), F32), vmem((1, C_H), F32), vmem((1, C_H), F32),
            vmem((1, C_Z), F32), vmem((1, C_M), F32), vmem((1, C_M), F32), sems(14),
        ],
        compiler_params=pltpu.CompilerParams(vmem_limit_bytes=56 * 1024 * 1024),
    )(upd, agrad, dw, small)
    return (
        upd[None],
        agrad.reshape(1, 128, ROWS, C_M),
        lw.T,
        lb.reshape(C_H),
        rw.T,
        rb.reshape(C_H),
        dw.reshape(C_H * C_H, C_Z),
        ob.reshape(C_Z),
        gain.reshape(C_M),
        shift.reshape(C_M),
    )


def solution(mesh):
    return jax.shard_map(
        body,
        mesh=mesh,
        in_specs=(
            P("dp", None, "res", None), P("dp", None), P("dp", None), P(), P(), P(), P(), P(), P(), P(), P(),
            P("dp", "res", None, None),
        ),
        out_specs=(
            P("dp", "res", None, None), P("dp", None, "res", None), P(), P(), P(), P(), P(), P(), P(), P(),
        ),
        check_vma=False,
    )
```
